32 devices in a mesh: depth: 8 (over y, x, core), light: 4 (over z).
Axes of the slice: x: 2, y: 2, z: 4, core: 2. Of those that a mesh axis runs over, the one named last changes fastest.
Arguments:
- density: bfloat16 [512, 32, 1024], P('depth', 'light'), may hold values from 0.049804688 to 1
- light_rate: float32 [1024], replicated, may hold values from 0.001 to 0.3
- view_rate: float32 [2, 1024], replicated, may hold values from 5e-05 to 0.005
- centers: float32 [3], replicated, may hold values from 0.1 to 0.9
- rank: int32 [2, 8], replicated, may hold values from 0 to 7, each once within a row
Outputs:
- image: float32 [2, 4, 32, 1024], P(None, None, 'light', 'depth')
The draws below stay inside these ranges and needn't reach their ends.
Inputs may be any that keep to these rules, and one draw needn't show every extreme that they name: Each row of rank is a permutation of 0 to 7.
All inputs are finite; a program needn't handle non-finite values.
Results may differ from the reference program's by a relative error of at most 0.0003.
Values sent between devices are 32-bit elements; how exact they have to be, the bound alone decides.
No kernel may reach another device: no remote copies, remote signals or barrier semaphores. Data moves between devices by JAX's collectives and lax.ppermute only.
A program may use at most 64 MiB of HBM per device.

```python
import math
import jax
import jax.numpy as jnp
from jax import lax

SAMPLES = 64
COLUMNS = 1024
VIEWPOINTS = 2
DEPTH_CELLS = 512
IMAGE_ROWS = 32
N_DEPTH = 8


def levels(stream_key, extent, pieces, smallest, high):
    factor_of, own = 1.0, jax.random.fold_in(stream_key, 6)
    for position, parts in pieces:
        steps = jnp.exp(jax.random.uniform(jax.random.fold_in(own, position), (parts,), jnp.float32, smallest / len(pieces), high / len(pieces)))
        factor_of = factor_of * jnp.repeat(steps, extent[position] // parts).reshape([-1 if axis == position else 1 for axis in range(len(extent))])
    return factor_of


def setup_inputs(seed: int = 0) -> dict:
    keys = jax.random.split(jax.random.key(seed), 6)
    density = jnp.clip(0.049804688 + 0.9501953 * jax.random.uniform(keys[0], (DEPTH_CELLS, IMAGE_ROWS, COLUMNS), jnp.float32) ** levels(keys[0], (DEPTH_CELLS, IMAGE_ROWS, COLUMNS), ((0, 8), (1, 4)), -0.2, 0.2), 0.049804688, 1.0).astype(jnp.bfloat16)
    light_rate = jnp.clip(jnp.exp(jax.random.uniform(keys[1], (COLUMNS,), jnp.float32, math.log(0.001), math.log(0.3))), 0.001, 0.3)
    view_rate = jnp.clip(jnp.exp(jax.random.uniform(keys[2], (VIEWPOINTS, COLUMNS), jnp.float32, math.log(4.999999873689376e-05), math.log(0.005))), 4.999999873689376e-05, 0.005)
    centers = jnp.clip(jax.random.uniform(keys[3], (3,), jnp.float32, 0.1, 0.9), 0.1, 0.9)
    rank = jax.vmap(lambda own: jax.random.permutation(own, N_DEPTH))(jax.random.split(keys[4], VIEWPOINTS)).reshape((VIEWPOINTS, N_DEPTH)).astype(jnp.int32)
    return {"density": density, "light_rate": light_rate, "view_rate": view_rate, "centers": centers, "rank": rank}


def brick_image(block, light_rate, view_rate, centers, before):
    rho = block.astype(jnp.float32)
    extinct = rho * light_rate
    lit_field = jnp.exp(-(jnp.cumsum(extinct, axis=1) - extinct))
    shape = rho.shape
    layers = []
    for view in range(VIEWPOINTS):
        depth_rate = rho * view_rate[view]
        order_mat = before if view == 0 else before.T
        ahead = jnp.dot(order_mat, depth_rate.reshape(shape[0], -1), precision=lax.Precision.HIGHEST).reshape(shape)
        weight = -jnp.expm1(-depth_rate) * jnp.exp(-ahead) * lit_field * 4.0
        channels = [jnp.sum(weight * jnp.exp(-8.0 * (rho - centers[k]) ** 2), axis=0) for k in range(3)]
        channels.append(jnp.sum(depth_rate, axis=0))
        layers.append(jnp.stack(channels))
    return jnp.stack(layers)


def reference(density, light_rate, view_rate, centers, rank):
    steps = jnp.arange(SAMPLES, dtype=jnp.int32)
    before = (steps[:, None] > steps[None, :]).astype(jnp.float32)

    def one_brick(index):
        block = lax.dynamic_slice_in_dim(density, index.astype(jnp.int32) * SAMPLES, SAMPLES, 0)
        return brick_image(block, light_rate, view_rate, centers, before)

    images = lax.map(one_brick, jnp.arange(N_DEPTH, dtype=jnp.int32))
    order_mat = (rank[:, None, :] < rank[:, :, None]).astype(jnp.float32)
    optical = images[:, :, 3]
    front = jnp.einsum("vij,jvrc->ivrc", order_mat, optical, precision=lax.Precision.HIGHEST)
    colors = jnp.sum(images[:, :, :3] * jnp.exp(-front)[:, :, None], axis=0)
    opacity = -jnp.expm1(-jnp.sum(optical, axis=0))
    return jnp.concatenate([colors, opacity[:, None]], axis=1)
```

```python
import functools
import math

import jax
import jax.numpy as jnp
from jax import lax
from jax.experimental import pallas as pl
from jax.experimental.pallas import tpu as pltpu
from jax.sharding import PartitionSpec as P

F32 = jnp.float32
LOG2E = math.log2(math.e)
LANES = 128


def row_sums_kernel(samples, rows, rho_ref, keep_ref, send_ref, total_ref):
    half = samples // 2
    odd = lax.axis_index("light") % 2
    wide = (samples, samples * rows)
    target = (lax.broadcasted_iota(jnp.int32, wide, 0) + half * odd) % samples
    source = lax.broadcasted_iota(jnp.int32, wide, 1)
    of_sample = (source // rows == target).astype(jnp.bfloat16)
    narrow = (rows, samples * rows)
    of_row = (
        lax.broadcasted_iota(jnp.int32, narrow, 1) % rows
        == lax.broadcasted_iota(jnp.int32, narrow, 0)
    ).astype(jnp.bfloat16)
    rho = rho_ref[...]
    sums = jnp.dot(of_sample, rho, preferred_element_type=F32)
    keep_ref[...] = sums[:half]
    send_ref[...] = sums[half:]
    total_ref[...] = jnp.dot(of_row, rho, preferred_element_type=F32)


def row_sums(rho, samples, rows):
    columns = rho.shape[1]
    half = jax.ShapeDtypeStruct((samples // 2, columns), F32)
    return pl.pallas_call(
        functools.partial(row_sums_kernel, samples, rows),
        out_shape=(half, half, jax.ShapeDtypeStruct((rows, columns), F32)),
    )(rho)


def main_kernel(
    samples, rows, width, rho_ref, mine_ref, other_ref, total_ref, light_ref, view_ref,
    center_ref, out_ref, above_ref, light_sum,
):
    half = samples // 2
    odd = lax.axis_index("light") % 2
    light_sum[pl.ds(pl.multiple_of(half * odd, half), half), :] = mine_ref[...]
    light_sum[pl.ds(pl.multiple_of(half * (1 - odd), half), half), :] = other_ref[...]
    columns = rho_ref.shape[1]

    block = 256
    square = (block, block)
    i = lax.broadcasted_iota(jnp.int32, square, 0)
    j = lax.broadcasted_iota(jnp.int32, square, 1)
    above = ((i // rows == j // rows) & (j < i)).astype(jnp.bfloat16)
    for start in range(0, samples * rows, block):
        above_ref[start : start + block, :] = jnp.dot(
            above, rho_ref[start : start + block, :], preferred_element_type=F32
        )

    shape = (rows, width)
    tone = [center_ref[k] * (16.0 * LOG2E) for k in range(3)]
    for first in range(0, columns, width):
        at = pl.ds(first, width)
        light = jnp.broadcast_to(light_ref[:, at] * LOG2E, shape)
        r0, r1 = view_ref[0:1, at], view_ref[1:2, at]
        fade = [jnp.broadcast_to(c, shape) for c in (r0, r0 * r0 * 0.5, r0 * r0 * r0 * (1 / 6))]
        grow = [jnp.broadcast_to(c, shape) for c in (r1, r1 * r1 * 0.5, r1 * r1 * r1 * (1 / 6))]

        def pair(step, carry):
            clear, behind, *sums = carry
            two = rho_ref[pl.ds(pl.multiple_of(step * 2 * rows, 2 * rows), 2 * rows), at].astype(F32)
            for part in range(2):
                rho = two[part * rows : (part + 1) * rows]
                s = step * 2 + part
                inner = above_ref[pl.ds(pl.multiple_of(s * rows, rows), rows), at]
                outer = light_sum[pl.ds(s, 1), at]
                tint = jnp.exp2(rho * rho * (-8.0 * LOG2E) - light * (inner + outer))
                w0 = clear * (rho * (fade[0] - rho * (fade[1] - rho * fade[2])))
                clear = clear - w0
                w1 = behind * (rho * (grow[0] + rho * (grow[1] + rho * grow[2])))
                behind = behind + w1
                w0, w1 = w0 * tint, w1 * tint
                for k in range(3):
                    e = jnp.exp2(rho * tone[k])
                    sums[k] = sums[k] + w0 * e
                    sums[3 + k] = sums[3 + k] + w1 * e
            return (clear, behind, *sums)

        zero = jnp.zeros(shape, F32)
        total = total_ref[:, at]
        start = (jnp.ones(shape, F32), jnp.exp2(total * view_ref[1:2, at] * -LOG2E)) + (zero,) * 6
        done = lax.fori_loop(0, samples // 2, pair, start, unroll=4)
        for k in range(3):
            c = jnp.full(shape, center_ref[k], F32)
            scale = 4.0 * jnp.exp2(c * c * (-8.0 * LOG2E))
            for view in range(2):
                value = done[2 + 3 * view + k] * scale
                for tile in range(width // LANES):
                    out_ref[first // LANES + tile, 3 * view + k] = value[:, tile * LANES : (tile + 1) * LANES]
        for tile in range(width // LANES):
            out_ref[first // LANES + tile, 6] = total[:, tile * LANES : (tile + 1) * LANES]


def brick_colors(rho, mine, other, total, light_rate, view_rate, centers, samples, rows):
    columns = rho.shape[1]
    vmem, smem = pl.BlockSpec(memory_space=pltpu.VMEM), pl.BlockSpec(memory_space=pltpu.SMEM)
    return pl.pallas_call(
        functools.partial(main_kernel, samples, rows, 256),
        out_shape=jax.ShapeDtypeStruct((columns // LANES, 7, rows, LANES), F32),
        in_specs=[vmem] * 6 + [smem],
        out_specs=vmem,
        scratch_shapes=[
            pltpu.VMEM((samples * rows, columns), F32),
            pltpu.VMEM((samples, columns), F32),
        ],
    )(rho, mine, other, total, light_rate.reshape(1, -1), view_rate, centers)


def composite_kernel(bricks, got_ref, rate_ref, rank_ref, out_ref, order_ref):
    shape = out_ref.shape[2:]
    for view in range(2):
        def place(d, carry, view=view):
            order_ref[view, rank_ref[view, d]] = d
            return carry

        lax.fori_loop(0, bricks, place, 0, unroll=bricks <= 8)
        rate = jnp.broadcast_to(rate_ref[view : view + 1, :], shape)

        def nearer(p, carry, view=view, rate=rate):
            front, red, green, blue = carry
            d = order_ref[view, p]
            seen = jnp.exp2(front * rate * -LOG2E)
            red = red + got_ref[d, 3 * view] * seen
            green = green + got_ref[d, 3 * view + 1] * seen
            blue = blue + got_ref[d, 3 * view + 2] * seen
            return front + got_ref[d, 6], red, green, blue

        zero = jnp.zeros(shape, F32)
        depth, *colors = lax.fori_loop(0, bricks, nearer, (zero,) * 4, unroll=bricks <= 8)
        for k in range(3):
            out_ref[view, k] = colors[k]
        depth = depth * rate
        small = jnp.full(shape, 1.0, F32)
        for n in range(8, 1, -1):
            small = 1.0 - depth * (1.0 / n) * small
        out_ref[view, 3] = jnp.where(depth < 0.35, depth * small, 1.0 - jnp.exp2(depth * -LOG2E))


def composite(got, rate, rank):
    bricks, _, rows, columns = got.shape
    vmem, smem = pl.BlockSpec(memory_space=pltpu.VMEM), pl.BlockSpec(memory_space=pltpu.SMEM)
    return pl.pallas_call(
        functools.partial(composite_kernel, bricks),
        out_shape=jax.ShapeDtypeStruct((2, 4, rows, columns), F32),
        in_specs=[vmem, vmem, smem],
        out_specs=vmem,
        scratch_shapes=[pltpu.SMEM((2, bricks), jnp.int32)],
    )(got, rate, rank)


def swap(x, stride, n):
    return lax.ppermute(x, "light", [(i, i ^ stride) for i in range(n)])


def lower_halves(keep, send, stride, n):
    odd = (lax.axis_index("light") // stride) % 2 == 1
    sibling = swap(send, stride, n)
    below = lower(keep + sibling, 2 * stride, n)
    other = swap(below + jnp.where(odd, 0.0, keep), stride, n)
    return below + jnp.where(odd, sibling, 0.0), other


def lower(x, stride, n):
    if stride == n:
        return jnp.zeros_like(x)
    odd = (lax.axis_index("light") // stride) % 2 == 1
    if 2 * stride == n:
        return jnp.where(odd, swap(x, stride, n), 0.0)
    half = x.shape[0] // 2
    first, last = x[:half], x[half:]
    mine, other = lower_halves(jnp.where(odd, last, first), jnp.where(odd, first, last), stride, n)
    return jnp.where(odd, jnp.concatenate([other, mine]), jnp.concatenate([mine, other]))


def shards(depth_n, light_n, density, light_rate, view_rate, centers, rank):
    samples, rows, columns = density.shape
    rho = density.reshape(samples * rows, columns)
    keep, send, total = row_sums(rho, samples, rows)
    mine, other = lower_halves(keep, send, 1, light_n)
    packed = brick_colors(rho, mine, other, total, light_rate, view_rate, centers, samples, rows)
    own = columns // depth_n
    if own % LANES == 0:
        parts = packed.reshape(depth_n, own // LANES, 7, rows, LANES)
        parts = parts[:, 0] if own == LANES else parts.transpose(0, 2, 3, 1, 4).reshape(depth_n, 7, rows, own)
    else:
        parts = packed.reshape(columns // LANES, 7, rows, LANES // own, own)
        parts = parts.transpose(0, 3, 1, 2, 4).reshape(depth_n, 7, rows, own)
    got = lax.all_to_all(parts, "depth", split_axis=0, concat_axis=0, tiled=True)
    rate = lax.dynamic_slice_in_dim(view_rate, lax.axis_index("depth") * own, own, axis=1)
    return composite(got, rate, rank)


def solution(mesh):
    return jax.shard_map(
        functools.partial(shards, mesh.shape["depth"], mesh.shape["light"]),
        mesh=mesh,
        in_specs=(P("depth", "light", None), P(), P(), P(), P()),
        out_specs=P(None, None, "light", "depth"),
        check_vma=False,
    )
```

```python
import functools
import math

import jax
import jax.numpy as jnp
from jax import lax
from jax.experimental import pallas as pl
from jax.experimental.pallas import tpu as pltpu
from jax.sharding import PartitionSpec as P

F32 = jnp.float32
LOG2E = math.log2(math.e)
LANES = 128


def sample_sums(rho, samples, rows):
    wide = (samples, samples * rows)
    target = lax.broadcasted_iota(jnp.int32, wide, 0)
    source = lax.broadcasted_iota(jnp.int32, wide, 1)
    return jnp.dot((source // rows == target).astype(jnp.bfloat16), rho, preferred_element_type=F32)


def send_kernel(half, rows, rho_hbm, send_ref, rho_ref, sem):
    odd = lax.axis_index("light") % 2
    first = pl.multiple_of((1 - odd) * half * rows, half * rows)
    copy = pltpu.make_async_copy(rho_hbm.at[pl.ds(first, half * rows)], rho_ref, sem)
    copy.start()
    copy.wait()
    send_ref[...] = sample_sums(rho_ref[...], half, rows)


def keep_kernel(half, rows, rho_hbm, keep_ref, total_ref, rho_ref, sem):
    odd = lax.axis_index("light") % 2
    copy = pltpu.make_async_copy(rho_hbm, rho_ref, sem)
    copy.start()
    copy.wait()
    first = pl.multiple_of(odd * half * rows, half * rows)
    keep_ref[...] = sample_sums(rho_ref[pl.ds(first, half * rows), :], half, rows)
    narrow = (rows, 2 * half * rows)
    of_row = (
        lax.broadcasted_iota(jnp.int32, narrow, 1) % rows
        == lax.broadcasted_iota(jnp.int32, narrow, 0)
    ).astype(jnp.bfloat16)
    total_ref[...] = jnp.dot(of_row, rho_ref[...], preferred_element_type=F32)


def pre_kernel(
    samples, rows, width, rho_ref, total_ref, light_ref, view_ref, center_ref,
    near_ref, far_ref, red_ref, green_ref, blue_ref, above_ref,
):
    columns = rho_ref.shape[1]
    block = 256
    square = (block, block)
    i = lax.broadcasted_iota(jnp.int32, square, 0)
    j = lax.broadcasted_iota(jnp.int32, square, 1)
    above = ((i // rows == j // rows) & (j < i)).astype(jnp.bfloat16)
    for start in range(0, samples * rows, block):
        above_ref[start : start + block, :] = jnp.dot(
            above, rho_ref[start : start + block, :], preferred_element_type=F32
        )

    shape = (rows, width)
    tone = [center_ref[k] * (16.0 * LOG2E) for k in range(3)]
    for first in range(0, columns, width):
        at = pl.ds(first, width)
        light = jnp.broadcast_to(light_ref[:, at] * LOG2E, shape)
        r0, r1 = view_ref[0:1, at], view_ref[1:2, at]
        fade = [jnp.broadcast_to(c, shape) for c in (r0, r0 * r0 * 0.5, r0 * r0 * r0 * (1 / 6))]
        grow = [jnp.broadcast_to(c, shape) for c in (r1, r1 * r1 * 0.5, r1 * r1 * r1 * (1 / 6))]

        def pair(step, carry):
            clear, behind = carry
            two = rho_ref[pl.ds(pl.multiple_of(step * 2 * rows, 2 * rows), 2 * rows), at].astype(F32)
            for part in range(2):
                rho = two[part * rows : (part + 1) * rows]
                here = pl.ds(pl.multiple_of((step * 2 + part) * rows, rows), rows)
                tint = jnp.exp2(rho * rho * (-8.0 * LOG2E) - light * above_ref[here, at])
                w0 = clear * (rho * (fade[0] - rho * (fade[1] - rho * fade[2])))
                clear = clear - w0
                w1 = behind * (rho * (grow[0] + rho * (grow[1] + rho * grow[2])))
                behind = behind + w1
                near_ref[here, at] = w0 * tint
                far_ref[here, at] = w1 * tint
                for k, color_ref in enumerate((red_ref, green_ref, blue_ref)):
                    color_ref[here, at] = jnp.exp2(rho * tone[k])
            return clear, behind

        start = (jnp.ones(shape, F32), jnp.exp2(total_ref[:, at] * view_ref[1:2, at] * -LOG2E))
        lax.fori_loop(0, samples // 2, pair, start, unroll=4)


def post_kernel(
    samples, rows, width, mine_ref, other_ref, total_ref, light_ref, center_ref,
    near_ref, far_ref, red_ref, green_ref, blue_ref, out_ref, lit_ref,
):
    half = samples // 2
    odd = lax.axis_index("light") % 2
    columns = total_ref.shape[1]
    light = light_ref[...] * -LOG2E
    lit_ref[pl.ds(pl.multiple_of(half * odd, half), half), :] = jnp.exp2(mine_ref[...] * light)
    lit_ref[pl.ds(pl.multiple_of(half * (1 - odd), half), half), :] = jnp.exp2(other_ref[...] * light)
    shape = (rows, width)
    for first in range(0, columns, width):
        at = pl.ds(first, width)

        def step(s, sums):
            here = pl.ds(pl.multiple_of(s * rows, rows), rows)
            lit = jnp.broadcast_to(lit_ref[pl.ds(s, 1), at], shape)
            weights = near_ref[here, at] * lit, far_ref[here, at] * lit
            colors = [ref[here, at] for ref in (red_ref, green_ref, blue_ref)]
            return tuple(sums[3 * v + k] + weights[v] * colors[k] for v in range(2) for k in range(3))

        done = lax.fori_loop(0, samples, step, (jnp.zeros(shape, F32),) * 6, unroll=8)
        for k in range(3):
            c = jnp.full(shape, center_ref[k], F32)
            scale = 4.0 * jnp.exp2(c * c * (-8.0 * LOG2E))
            for view in range(2):
                value = done[3 * view + k] * scale
                for tile in range(width // LANES):
                    out_ref[first // LANES + tile, 3 * view + k] = value[:, tile * LANES : (tile + 1) * LANES]
        for tile in range(width // LANES):
            out_ref[first // LANES + tile, 6] = total_ref[:, first + tile * LANES : first + (tile + 1) * LANES]


def call(kernel, outs, spaces, scratch, flops, moved, *args, limit=8):
    specs = {"v": pl.BlockSpec(memory_space=pltpu.VMEM), "s": pl.BlockSpec(memory_space=pltpu.SMEM), "a": pl.BlockSpec(memory_space=pl.ANY)}
    args = [pltpu.with_memory_space_constraint(a, pltpu.VMEM) if k == "V" else a for a, k in zip(args, spaces, strict=True)]
    return pl.pallas_call(
        kernel,
        out_shape=tuple(pltpu.VMEM(o, t) for o, t in outs) if outs else None,
        in_specs=[specs[k.lower()] for k in spaces],
        out_specs=tuple([specs["v"]] * len(outs)),
        scratch_shapes=scratch,
        cost_estimate=pl.CostEstimate(flops=flops, bytes_accessed=moved, transcendentals=0),
        compiler_params=pltpu.CompilerParams(vmem_limit_bytes=limit << 20),
    )(*args)


def composite_kernel(bricks, got_ref, rate_ref, rank_ref, out_ref, order_ref):
    shape = out_ref.shape[2:]
    for view in range(2):
        def place(d, carry, view=view):
            order_ref[view, rank_ref[view, d]] = d
            return carry

        lax.fori_loop(0, bricks, place, 0, unroll=bricks <= 8)
        rate = jnp.broadcast_to(rate_ref[view : view + 1, :], shape)

        def nearer(p, carry, view=view, rate=rate):
            front, red, green, blue = carry
            d = order_ref[view, p]
            seen = jnp.exp2(front * rate * -LOG2E)
            red = red + got_ref[d, 3 * view] * seen
            green = green + got_ref[d, 3 * view + 1] * seen
            blue = blue + got_ref[d, 3 * view + 2] * seen
            return front + got_ref[d, 6], red, green, blue

        zero = jnp.zeros(shape, F32)
        depth, *colors = lax.fori_loop(0, bricks, nearer, (zero,) * 4, unroll=bricks <= 8)
        for k in range(3):
            out_ref[view, k] = colors[k]
        depth = depth * rate
        small = jnp.full(shape, 1.0, F32)
        for n in range(8, 1, -1):
            small = 1.0 - depth * (1.0 / n) * small
        out_ref[view, 3] = jnp.where(depth < 0.35, depth * small, 1.0 - jnp.exp2(depth * -LOG2E))


def composite(got, rate, rank):
    bricks, _, rows, columns = got.shape
    vmem, smem = pl.BlockSpec(memory_space=pltpu.VMEM), pl.BlockSpec(memory_space=pltpu.SMEM)
    return pl.pallas_call(
        functools.partial(composite_kernel, bricks),
        out_shape=jax.ShapeDtypeStruct((2, 4, rows, columns), F32),
        in_specs=[vmem, vmem, smem],
        out_specs=vmem,
        scratch_shapes=[pltpu.SMEM((2, bricks), jnp.int32)],
        compiler_params=pltpu.CompilerParams(vmem_limit_bytes=8 << 20),
    )(pltpu.with_memory_space_constraint(got, pltpu.VMEM), rate, rank)


def swap(x, stride, n):
    return lax.ppermute(x, "light", [(i, i ^ stride) for i in range(n)])


def lower_halves(keep, send, stride, n):
    odd = (lax.axis_index("light") // stride) % 2 == 1
    sibling = swap(send, stride, n)
    below = lower(keep + sibling, 2 * stride, n)
    other = swap(below + jnp.where(odd, 0.0, keep), stride, n)
    return below + jnp.where(odd, sibling, 0.0), other


def lower(x, stride, n):
    if stride == n:
        return jnp.zeros_like(x)
    odd = (lax.axis_index("light") // stride) % 2 == 1
    if 2 * stride == n:
        return jnp.where(odd, swap(x, stride, n), 0.0)
    half = x.shape[0] // 2
    first, last = x[:half], x[half:]
    mine, other = lower_halves(jnp.where(odd, last, first), jnp.where(odd, first, last), stride, n)
    return jnp.where(odd, jnp.concatenate([other, mine]), jnp.concatenate([mine, other]))


def shards(depth_n, light_n, density, light_rate, view_rate, centers, rank):
    samples, rows, columns = density.shape
    rho = density.reshape(samples * rows, columns)
    half = samples // 2
    light = light_rate.reshape(1, -1)
    whole, part = (samples * rows, columns), (half, columns)
    sem = pltpu.SemaphoreType.DMA
    (send,) = call(
        functools.partial(send_kernel, half, rows), [(part, F32)], "a",
        [pltpu.VMEM((half * rows, columns), jnp.bfloat16), sem], 1 << 20, 1 << 19, rho,
    )
    keep, total, rho = call(
        functools.partial(keep_kernel, half, rows), [(part, F32), ((rows, columns), F32), (whole, jnp.bfloat16)], "a",
        [sem], 1 << 20, 1 << 20, rho,
    )
    odd = lax.axis_index("light") % 2 == 1
    sibling = swap(send, 1, light_n)
    sums = keep + sibling
    sums, total = lax.optimization_barrier((sums, total))
    near, far, red, green, blue = call(
        functools.partial(pre_kernel, samples, rows, 256), [(whole, F32)] * 5, "VVvvs",
        [pltpu.VMEM(whole, F32)], 1 << 20, 12 << 20, rho, total, light, view_rate, centers,
    )
    below = lower(sums, 2, light_n)
    other = swap(below + jnp.where(odd, 0.0, keep), 1, light_n)
    mine = below + jnp.where(odd, sibling, 0.0)
    (packed,) = call(
        functools.partial(post_kernel, samples, rows, 256), [((columns // LANES, 7, rows, LANES), F32)], "VVVvsVVVVV",
        [pltpu.VMEM((samples, columns), F32)], 1 << 20, 10 << 20,
        mine, other, total, light, centers, near, far, red, green, blue,
    )
    own = columns // depth_n
    if own % LANES == 0:
        parts = packed.reshape(depth_n, own // LANES, 7, rows, LANES)
        parts = parts[:, 0] if own == LANES else parts.transpose(0, 2, 3, 1, 4).reshape(depth_n, 7, rows, own)
    else:
        parts = packed.reshape(columns // LANES, 7, rows, LANES // own, own)
        parts = parts.transpose(0, 3, 1, 2, 4).reshape(depth_n, 7, rows, own)
    got = lax.all_to_all(parts, "depth", split_axis=0, concat_axis=0, tiled=True)
    rate = lax.dynamic_slice_in_dim(view_rate, lax.axis_index("depth") * own, own, axis=1)
    return composite(got, rate, rank)


def solution(mesh):
    return jax.shard_map(
        functools.partial(shards, mesh.shape["depth"], mesh.shape["light"]),
        mesh=mesh,
        in_specs=(P("depth", "light", None), P(), P(), P(), P()),
        out_specs=P(None, None, "light", "depth"),
        check_vma=False,
    )
```

```python
import functools
import math

import jax
import jax.numpy as jnp
from jax import lax
from jax.experimental import pallas as pl
from jax.experimental.pallas import tpu as pltpu
from jax.sharding import PartitionSpec as P

F32 = jnp.float32
LOG2E = math.log2(math.e)
LANES = 128


def sample_sums(rho, samples, rows):
    wide = (samples, samples * rows)
    target = lax.broadcasted_iota(jnp.int32, wide, 0)
    source = lax.broadcasted_iota(jnp.int32, wide, 1)
    return jnp.dot((source // rows == target).astype(jnp.bfloat16), rho, preferred_element_type=F32)


def send_kernel(half, rows, rho_hbm, send_ref, rho_ref, sem):
    odd = lax.axis_index("light") % 2
    first = pl.multiple_of((1 - odd) * half * rows, half * rows)
    copy = pltpu.make_async_copy(rho_hbm.at[pl.ds(first, half * rows)], rho_ref, sem)
    copy.start()
    copy.wait()
    send_ref[...] = sample_sums(rho_ref[...], half, rows)


def keep_kernel(half, rows, rho_hbm, keep_ref, total_ref, rho_ref, sem):
    odd = lax.axis_index("light") % 2
    copy = pltpu.make_async_copy(rho_hbm, rho_ref, sem)
    copy.start()
    copy.wait()
    first = pl.multiple_of(odd * half * rows, half * rows)
    keep_ref[...] = sample_sums(rho_ref[pl.ds(first, half * rows), :], half, rows)
    narrow = (rows, 2 * half * rows)
    of_row = (
        lax.broadcasted_iota(jnp.int32, narrow, 1) % rows
        == lax.broadcasted_iota(jnp.int32, narrow, 0)
    ).astype(jnp.bfloat16)
    total_ref[...] = jnp.dot(of_row, rho_ref[...], preferred_element_type=F32)


def pre_kernel(
    samples, rows, width, rho_ref, total_ref, light_ref, view_ref, center_ref,
    near_ref, far_ref, red_ref, green_ref, blue_ref, above_ref,
):
    columns = rho_ref.shape[1]
    block = 256
    square = (block, block)
    i = lax.broadcasted_iota(jnp.int32, square, 0)
    j = lax.broadcasted_iota(jnp.int32, square, 1)
    above = ((i // rows == j // rows) & (j < i)).astype(jnp.bfloat16)
    for start in range(0, samples * rows, block):
        above_ref[start : start + block, :] = jnp.dot(
            above, rho_ref[start : start + block, :], preferred_element_type=F32
        )

    shape = (rows, width)
    tone = [center_ref[k] * (16.0 * LOG2E) for k in range(3)]
    for first in range(0, columns, width):
        at = pl.ds(first, width)
        light = jnp.broadcast_to(light_ref[:, at] * LOG2E, shape)
        r0, r1 = view_ref[0:1, at], view_ref[1:2, at]
        fade = [jnp.broadcast_to(c, shape) for c in (r0, r0 * r0 * 0.5, r0 * r0 * r0 * (1 / 6))]
        grow = [jnp.broadcast_to(c, shape) for c in (r1, r1 * r1 * 0.5, r1 * r1 * r1 * (1 / 6))]

        def pair(step, carry):
            clear, behind = carry
            two = rho_ref[pl.ds(pl.multiple_of(step * 2 * rows, 2 * rows), 2 * rows), at].astype(F32)
            for part in range(2):
                rho = two[part * rows : (part + 1) * rows]
                here = pl.ds(pl.multiple_of((step * 2 + part) * rows, rows), rows)
                tint = jnp.exp2(rho * rho * (-8.0 * LOG2E) - light * above_ref[here, at])
                w0 = clear * (rho * (fade[0] - rho * (fade[1] - rho * fade[2])))
                clear = clear - w0
                w1 = behind * (rho * (grow[0] + rho * (grow[1] + rho * grow[2])))
                behind = behind + w1
                near_ref[here, at] = w0 * tint
                far_ref[here, at] = w1 * tint
                for k, color_ref in enumerate((red_ref, green_ref, blue_ref)):
                    color_ref[here, at] = jnp.exp2(rho * tone[k])
            return clear, behind

        start = (jnp.ones(shape, F32), jnp.exp2(total_ref[:, at] * view_ref[1:2, at] * -LOG2E))
        lax.fori_loop(0, samples // 2, pair, start, unroll=True)


def post_kernel(
    rows, second, sliced, place_ref, below_ref, *refs
):
    early_ref = refs[0] if second else None
    light_ref, center_ref, near_ref, far_ref, red_ref, green_ref, blue_ref, rest_ref, out_ref, lit_ref = refs[second:]
    half, columns = below_ref.shape
    odd = lax.axis_index("light") % 2
    base = (1 - odd if second else odd) * half
    chip, core = (place_ref[0] // 2, place_ref[0] % 2) if sliced else (0, 0)
    below = below_ref[...]
    if second:
        below = below + jnp.where(odd == 1, early_ref[...], 0.0)
    lit_ref[...] = jnp.exp2(below * (light_ref[...] * -LOG2E))
    width = 2 * LANES
    shape = (rows, width)
    scales = [4.0 * jnp.exp2(jnp.full((rows, LANES), center_ref[k], F32) ** 2 * (-8.0 * LOG2E)) for k in range(3)]
    for slot in range(columns // width):
        at = pl.ds(pl.multiple_of((slot ^ chip) * width, width), width)
        sums = [jnp.zeros(shape, F32)] * 6
        for group in range(half // 8):
            lit = lit_ref[group * 8 : group * 8 + 8, at]
            for part in range(8):
                here = pl.ds(pl.multiple_of((base + group * 8 + part) * rows, rows), rows)
                shade = jnp.broadcast_to(lit[part : part + 1], shape)
                weights = near_ref[here, at] * shade, far_ref[here, at] * shade
                colors = [ref[here, at] for ref in (red_ref, green_ref, blue_ref)]
                sums = [sums[3 * v + k] + weights[v] * colors[k] for v in range(2) for k in range(3)]
        for tile in range(2):
            lanes = slice(tile * LANES, (tile + 1) * LANES)
            for n in range(6):
                value = sums[n][:, lanes] * scales[n % 3]
                if second:
                    value = value + rest_ref[tile ^ core, slot, n]
                out_ref[tile ^ core, slot, n] = value
            out_ref[tile ^ core, slot, 6] = rest_ref[tile ^ core, slot, 6] if second else rest_ref[:, at][:, lanes]


def call(kernel, outs, spaces, scratch, flops, moved, *args, limit=8):
    specs = {"v": pl.BlockSpec(memory_space=pltpu.VMEM), "s": pl.BlockSpec(memory_space=pltpu.SMEM), "a": pl.BlockSpec(memory_space=pl.ANY)}
    forced = {"V": pltpu.VMEM, "A": pltpu.HBM, "S": pltpu.SMEM}
    args = [pltpu.with_memory_space_constraint(a, forced[k]) if k in forced else a for a, k in zip(args, spaces, strict=True)]
    return pl.pallas_call(
        kernel,
        out_shape=tuple(pltpu.VMEM(o, t) for o, t in outs),
        in_specs=[specs[k.lower()] for k in spaces],
        out_specs=tuple([specs["v"]] * len(outs)),
        scratch_shapes=scratch,
        cost_estimate=pl.CostEstimate(flops=flops, bytes_accessed=moved, transcendentals=0),
        compiler_params=pltpu.CompilerParams(vmem_limit_bytes=limit << 20),
    )(*args)


def composite_kernel(bricks, got_ref, rate_ref, rank_ref, out_ref, order_ref):
    shape = out_ref.shape[2:]
    for view in range(2):
        def place(d, carry, view=view):
            order_ref[view, rank_ref[view, d]] = d
            return carry

        lax.fori_loop(0, bricks, place, 0, unroll=bricks <= 8)
        rate = jnp.broadcast_to(rate_ref[view : view + 1, :], shape)

        def nearer(p, carry, view=view, rate=rate):
            front, red, green, blue = carry
            d = order_ref[view, p]
            seen = jnp.exp2(front * rate * -LOG2E)
            red = red + got_ref[d, 3 * view] * seen
            green = green + got_ref[d, 3 * view + 1] * seen
            blue = blue + got_ref[d, 3 * view + 2] * seen
            return front + got_ref[d, 6], red, green, blue

        zero = jnp.zeros(shape, F32)
        depth, *colors = lax.fori_loop(0, bricks, nearer, (zero,) * 4, unroll=bricks <= 8)
        for k in range(3):
            out_ref[view, k] = colors[k]
        out_ref[view, 3] = opacity(depth * rate)


def composite(got, rate, rank):
    bricks, _, rows, columns = got.shape
    vmem, smem = pl.BlockSpec(memory_space=pltpu.VMEM), pl.BlockSpec(memory_space=pltpu.SMEM)
    return pl.pallas_call(
        functools.partial(composite_kernel, bricks),
        out_shape=jax.ShapeDtypeStruct((2, 4, rows, columns), F32),
        in_specs=[vmem, vmem, smem],
        out_specs=vmem,
        scratch_shapes=[pltpu.SMEM((2, bricks), jnp.int32)],
        compiler_params=pltpu.CompilerParams(vmem_limit_bytes=8 << 20),
    )(pltpu.with_memory_space_constraint(got, pltpu.VMEM), rate, rank)


def opacity(depth):
    small = jnp.full(depth.shape, 1.0, F32)
    for n in range(8, 1, -1):
        small = 1.0 - depth * (1.0 / n) * small
    return jnp.where(depth < 0.35, depth * small, 1.0 - jnp.exp2(depth * -LOG2E))


def slots_kernel(place_ref, rank_ref, rate_ref, own_ref, sibling_ref, *refs):
    *chip_refs, out_ref = refs
    shape = out_ref.shape[2:]
    blocks = [own_ref.at[0, 0], sibling_ref.at[0]] + [ref.at[t] for ref in chip_refs for t in range(2)]
    depths = [block[6] for block in blocks]
    for view in range(2):
        rate = jnp.broadcast_to(rate_ref[view : view + 1, :], shape)
        ranks = [rank_ref[view, place_ref[0] ^ slot] for slot in range(len(blocks))]
        colors = [jnp.zeros(shape, F32)] * 3
        for i, block in enumerate(blocks):
            front = jnp.zeros(shape, F32)
            for j, depth in enumerate(depths):
                if j != i:
                    front = front + depth * (ranks[j] < ranks[i]).astype(F32)
            seen = jnp.exp2(front * rate * -LOG2E)
            colors = [colors[k] + block[3 * view + k] * seen for k in range(3)]
        for k in range(3):
            out_ref[view, k] = colors[k]
        out_ref[view, 3] = opacity(sum(depths) * rate)


def composite_slots(place, rank, rate, own, sibling, chips):
    vmem, smem = pl.BlockSpec(memory_space=pltpu.VMEM), pl.BlockSpec(memory_space=pltpu.SMEM)
    blocks = [pltpu.with_memory_space_constraint(x, pltpu.VMEM) for x in (own, sibling, *chips)]
    _, rows, columns = own.shape[2:]
    return pl.pallas_call(
        slots_kernel,
        out_shape=jax.ShapeDtypeStruct((2, 4, rows, columns), F32),
        in_specs=[smem, smem, vmem] + [vmem] * len(blocks),
        out_specs=vmem,
        compiler_params=pltpu.CompilerParams(vmem_limit_bytes=8 << 20),
    )(*(pltpu.with_memory_space_constraint(x, pltpu.SMEM) for x in (place, rank)), pltpu.with_memory_space_constraint(rate, pltpu.VMEM), *blocks)


def swap(x, stride, n, first=0, last=None):
    return lax.ppermute(x, "light", [(i, i ^ stride) for i in range(first, n if last is None else last)])


def halves_below(keep, sibling, sums, stride, n):
    odd = (lax.axis_index("light") // stride) % 2 == 1
    below = lower(sums, 2 * stride, n)
    first = swap(keep, stride, n, 0, 2 * stride)
    mine = below + jnp.where(odd, sibling, 0.0)
    other = swap(below + jnp.where(odd, 0.0, keep), stride, n, 2 * stride)
    return mine, other, first


def lower(x, stride, n):
    if stride == n:
        return jnp.zeros_like(x)
    odd = (lax.axis_index("light") // stride) % 2 == 1
    if 2 * stride == n:
        return jnp.where(odd, swap(x, stride, n), 0.0)
    half = x.shape[0] // 2
    first, last = x[:half], x[half:]
    keep, sibling = jnp.where(odd, last, first), swap(jnp.where(odd, first, last), stride, n)
    mine, other, early = halves_below(keep, sibling, keep + sibling, stride, n)
    other = other + jnp.where(odd, early, 0.0)
    return jnp.where(odd, jnp.concatenate([other, mine]), jnp.concatenate([mine, other]))


def shards(depth_n, light_n, density, light_rate, view_rate, centers, rank):
    samples, rows, columns = density.shape
    rho = density.reshape(samples * rows, columns)
    half = samples // 2
    light = light_rate.reshape(1, -1)
    whole, part = (samples * rows, columns), (half, columns)
    sem = pltpu.SemaphoreType.DMA
    (send,) = call(
        functools.partial(send_kernel, half, rows), [(part, F32)], "A",
        [pltpu.VMEM((half * rows, columns), jnp.bfloat16), sem], 1 << 20, 1 << 19, rho,
    )
    keep, total, rho = call(
        functools.partial(keep_kernel, half, rows), [(part, F32), ((rows, columns), F32), (whole, jnp.bfloat16)], "A",
        [sem], 1 << 20, 1 << 20, rho,
    )
    sibling = swap(send, 1, light_n)
    sums = keep + sibling
    near, far, red, green, blue = call(
        functools.partial(pre_kernel, samples, rows, 256), [(whole, F32)] * 5, "VVVVS",
        [pltpu.VMEM(whole, F32)], 1 << 20, 12 << 20, rho, total, light, view_rate, centers,
    )
    mine, other, early = halves_below(keep, sibling, sums, 1, light_n)
    own = columns // depth_n
    place = lax.axis_index("depth")
    rate = lax.dynamic_slice_in_dim(view_rate, place * own, own, axis=1)
    place = place.reshape(1)
    sliced = own == LANES and depth_n <= 8 and depth_n & (depth_n - 1) == 0
    packed = total
    for second, below in enumerate(([mine], [other, early])):
        (packed,) = call(
            functools.partial(post_kernel, rows, second, sliced), [((2, columns // (2 * LANES), 7, rows, LANES), F32)], "S" + "V" * len(below) + "VSVVVVVV",
            [pltpu.VMEM(part, F32)], 1 << 10, 1 << 10,
            place, *below, light, centers, near, far, red, green, blue, packed,
        )
    if sliced:
        def send_to(x, stride):
            return lax.ppermute(x, "depth", [(i, i ^ stride) for i in range(depth_n)])

        got = send_to(packed[1], 1)
        chips = [send_to(jnp.stack([packed[0, chip], got[chip]]), 2 * chip) for chip in range(1, depth_n // 2)]
        return composite_slots(place, rank, rate, packed, got, chips)
    parts = packed.transpose(1, 0, 2, 3, 4).reshape(columns // LANES, 7, rows, LANES)
    if own % LANES == 0:
        parts = parts.reshape(depth_n, own // LANES, 7, rows, LANES).transpose(0, 2, 3, 1, 4)
    else:
        parts = parts.reshape(columns // LANES, 7, rows, LANES // own, own).transpose(0, 3, 1, 2, 4)
    got = lax.all_to_all(parts.reshape(depth_n, 7, rows, own), "depth", split_axis=0, concat_axis=0, tiled=True)
    return composite(got, rate, rank)


def solution(mesh):
    return jax.shard_map(
        functools.partial(shards, mesh.shape["depth"], mesh.shape["light"]),
        mesh=mesh,
        in_specs=(P("depth", "light", None), P(), P(), P(), P()),
        out_specs=P(None, None, "light", "depth"),
        check_vma=False,
    )
```

```python
import functools
import math

import jax
import jax.numpy as jnp
from jax import lax
from jax.experimental import pallas as pl
from jax.experimental.pallas import tpu as pltpu
from jax.sharding import PartitionSpec as P

F32 = jnp.float32
LOG2E = math.log2(math.e)
LANES = 128
TONES = 8


def sample_sums(rho, samples, rows):
    wide = (samples, samples * rows)
    target = lax.broadcasted_iota(jnp.int32, wide, 0)
    source = lax.broadcasted_iota(jnp.int32, wide, 1)
    return jnp.dot((source // rows == target).astype(jnp.bfloat16), rho, preferred_element_type=F32)


def send_kernel(half, rows, rho_hbm, send_ref, rho_ref, sem):
    odd = lax.axis_index("light") % 2
    first = pl.multiple_of((1 - odd) * half * rows, half * rows)
    copy = pltpu.make_async_copy(rho_hbm.at[pl.ds(first, half * rows)], rho_ref, sem)
    copy.start()
    copy.wait()
    send_ref[...] = sample_sums(rho_ref[...], half, rows)


def keep_kernel(half, rows, rho_hbm, keep_ref, rho_ref, sem):
    odd = lax.axis_index("light") % 2
    copy = pltpu.make_async_copy(rho_hbm, rho_ref, sem)
    copy.start()
    copy.wait()
    first = pl.multiple_of(odd * half * rows, half * rows)
    keep_ref[...] = sample_sums(rho_ref[pl.ds(first, half * rows), :], half, rows)


def table_kernel(sliced, rho_ref, rank_ref, center_ref, total_ref, table_ref):
    rows = total_ref.shape[0]
    narrow = (rows, rho_ref.shape[0])
    of_row = lax.broadcasted_iota(jnp.int32, narrow, 1) % rows == lax.broadcasted_iota(jnp.int32, narrow, 0)
    total_ref[...] = jnp.dot(of_row.astype(jnp.bfloat16), rho_ref[...], preferred_element_type=F32)
    for k in range(3):
        c = jnp.full((1, LANES), center_ref[k], F32)
        table_ref[k : k + 1, :] = c * (16.0 * LOG2E)
        table_ref[3 + k : 4 + k, :] = 4.0 * jnp.exp2(c * c * (-8.0 * LOG2E))
    if sliced:
        bricks = rank_ref.shape[1]
        place = lax.axis_index("depth")
        for view in range(2):
            for slot in range(bricks):
                row = TONES + bricks * view + slot
                table_ref[row : row + 1, :] = jnp.full((1, LANES), rank_ref[view, place ^ slot].astype(F32))


def pre_kernel(
    samples, rows, width, rho_ref, total_ref, light_ref, view_ref, table_ref,
    near_ref, far_ref, red_ref, green_ref, blue_ref, above_ref,
):
    columns = rho_ref.shape[1]
    block = 256
    square = (block, block)
    i = lax.broadcasted_iota(jnp.int32, square, 0)
    j = lax.broadcasted_iota(jnp.int32, square, 1)
    above = ((i // rows == j // rows) & (j < i)).astype(jnp.bfloat16)
    for start in range(0, samples * rows, block):
        above_ref[start : start + block, :] = jnp.dot(
            above, rho_ref[start : start + block, :], preferred_element_type=F32
        )

    shape = (rows, width)
    tone = [jnp.broadcast_to(jnp.concatenate([table_ref[k : k + 1, :]] * (width // LANES), 1), shape) for k in range(3)]
    for first in range(0, columns, width):
        at = pl.ds(first, width)
        light = jnp.broadcast_to(light_ref[:, at] * LOG2E, shape)
        r0, r1 = view_ref[0:1, at], view_ref[1:2, at]
        fade = [jnp.broadcast_to(c, shape) for c in (r0, r0 * r0 * 0.5, r0 * r0 * r0 * (1 / 6))]
        grow = [jnp.broadcast_to(c, shape) for c in (r1, r1 * r1 * 0.5, r1 * r1 * r1 * (1 / 6))]

        def pair(step, carry):
            clear, behind = carry
            two = rho_ref[pl.ds(pl.multiple_of(step * 2 * rows, 2 * rows), 2 * rows), at].astype(F32)
            for part in range(2):
                rho = two[part * rows : (part + 1) * rows]
                here = pl.ds(pl.multiple_of((step * 2 + part) * rows, rows), rows)
                tint = jnp.exp2(rho * rho * (-8.0 * LOG2E) - light * above_ref[here, at])
                w0 = clear * (rho * (fade[0] - rho * (fade[1] - rho * fade[2])))
                clear = clear - w0
                w1 = behind * (rho * (grow[0] + rho * (grow[1] + rho * grow[2])))
                behind = behind + w1
                near_ref[here, at] = w0 * tint
                far_ref[here, at] = w1 * tint
                for k, color_ref in enumerate((red_ref, green_ref, blue_ref)):
                    color_ref[here, at] = jnp.exp2(rho * tone[k])
            return clear, behind

        start = (jnp.ones(shape, F32), jnp.exp2(total_ref[:, at] * view_ref[1:2, at] * -LOG2E))
        lax.fori_loop(0, samples // 2, pair, start, unroll=True)


def post_kernel(
    rows, second, sliced, below_ref, light_ref, table_ref, near_ref, far_ref, red_ref, green_ref, blue_ref,
    rest_ref, out_ref, lit_ref,
):
    half, columns = below_ref.shape
    odd = lax.axis_index("light") % 2
    base = (1 - odd if second else odd) * half
    place = lax.axis_index("depth") if sliced else 0
    chip, core = place // 2, place % 2
    lit_ref[...] = jnp.exp2(below_ref[...] * (light_ref[...] * -LOG2E))
    width = 2 * LANES
    shape = (rows, width)
    scales = [jnp.broadcast_to(table_ref[3 + k : 4 + k, :], (rows, LANES)) for k in range(3)]
    for slot in range(columns // width):
        at = pl.ds(pl.multiple_of((slot ^ chip) * width, width), width)
        sums = [jnp.zeros(shape, F32)] * 6
        for group in range(half // 8):
            lit = lit_ref[group * 8 : group * 8 + 8, at]
            for part in range(8):
                here = pl.ds(pl.multiple_of((base + group * 8 + part) * rows, rows), rows)
                shade = jnp.broadcast_to(lit[part : part + 1], shape)
                weights = near_ref[here, at] * shade, far_ref[here, at] * shade
                colors = [ref[here, at] for ref in (red_ref, green_ref, blue_ref)]
                sums = [sums[3 * v + k] + weights[v] * colors[k] for v in range(2) for k in range(3)]
        for tile in range(2):
            lanes = slice(tile * LANES, (tile + 1) * LANES)
            for n in range(6):
                value = sums[n][:, lanes] * scales[n % 3]
                if second:
                    value = value + rest_ref[tile ^ core, slot, n]
                out_ref[tile ^ core, slot, n] = value
            out_ref[tile ^ core, slot, 6] = rest_ref[tile ^ core, slot, 6] if second else rest_ref[:, at][:, lanes]


def call(kernel, outs, spaces, scratch, flops, moved, *args, limit=8):
    specs = {"v": pl.BlockSpec(memory_space=pltpu.VMEM), "s": pl.BlockSpec(memory_space=pltpu.SMEM), "a": pl.BlockSpec(memory_space=pl.ANY)}
    forced = {"V": pltpu.VMEM, "A": pltpu.HBM, "S": pltpu.SMEM}
    args = [pltpu.with_memory_space_constraint(a, forced[k]) if k in forced else a for a, k in zip(args, spaces, strict=True)]
    return pl.pallas_call(
        kernel,
        out_shape=tuple(pltpu.VMEM(o, t) for o, t in outs),
        in_specs=[specs[k.lower()] for k in spaces],
        out_specs=tuple([specs["v"]] * len(outs)),
        scratch_shapes=scratch,
        cost_estimate=pl.CostEstimate(flops=flops, bytes_accessed=moved, transcendentals=0),
        compiler_params=pltpu.CompilerParams(vmem_limit_bytes=limit << 20),
    )(*args)


def composite_kernel(bricks, got_ref, rate_ref, rank_ref, out_ref, order_ref):
    shape = out_ref.shape[2:]
    for view in range(2):
        def place(d, carry, view=view):
            order_ref[view, rank_ref[view, d]] = d
            return carry

        lax.fori_loop(0, bricks, place, 0, unroll=bricks <= 8)
        rate = jnp.broadcast_to(rate_ref[view : view + 1, :], shape)

        def nearer(p, carry, view=view, rate=rate):
            front, red, green, blue = carry
            d = order_ref[view, p]
            seen = jnp.exp2(front * rate * -LOG2E)
            red = red + got_ref[d, 3 * view] * seen
            green = green + got_ref[d, 3 * view + 1] * seen
            blue = blue + got_ref[d, 3 * view + 2] * seen
            return front + got_ref[d, 6], red, green, blue

        zero = jnp.zeros(shape, F32)
        depth, *colors = lax.fori_loop(0, bricks, nearer, (zero,) * 4, unroll=bricks <= 8)
        for k in range(3):
            out_ref[view, k] = colors[k]
        out_ref[view, 3] = opacity(depth * rate)


def composite(got, rate, rank):
    bricks, _, rows, columns = got.shape
    vmem, smem = pl.BlockSpec(memory_space=pltpu.VMEM), pl.BlockSpec(memory_space=pltpu.SMEM)
    return pl.pallas_call(
        functools.partial(composite_kernel, bricks),
        out_shape=jax.ShapeDtypeStruct((2, 4, rows, columns), F32),
        in_specs=[vmem, vmem, smem],
        out_specs=vmem,
        scratch_shapes=[pltpu.SMEM((2, bricks), jnp.int32)],
        compiler_params=pltpu.CompilerParams(vmem_limit_bytes=8 << 20),
    )(pltpu.with_memory_space_constraint(got, pltpu.VMEM), rate, rank)


def opacity(depth):
    small = jnp.full(depth.shape, 1.0, F32)
    for n in range(8, 1, -1):
        small = 1.0 - depth * (1.0 / n) * small
    return jnp.where(depth < 0.35, depth * small, 1.0 - jnp.exp2(depth * -LOG2E))


def slots_kernel(table_ref, rate_ref, own_ref, sibling_ref, *refs):
    *chip_refs, out_ref = refs
    shape = out_ref.shape[2:]
    blocks = [own_ref.at[0, 0], sibling_ref.at[0]] + [ref.at[t] for ref in chip_refs for t in range(2)]
    depths = [block[6] for block in blocks]
    for view in range(2):
        rate = jnp.broadcast_to(rate_ref[view : view + 1, :], shape)
        first = TONES + len(blocks) * view
        ranks = [jnp.broadcast_to(table_ref[first + slot : first + slot + 1, :], shape) for slot in range(len(blocks))]
        colors = [jnp.zeros(shape, F32)] * 3
        for i, block in enumerate(blocks):
            front = jnp.zeros(shape, F32)
            for j, depth in enumerate(depths):
                if j != i:
                    front = front + jnp.where(ranks[j] < ranks[i], depth, 0.0)
            seen = jnp.exp2(front * rate * -LOG2E)
            colors = [colors[k] + block[3 * view + k] * seen for k in range(3)]
        for k in range(3):
            out_ref[view, k] = colors[k]
        out_ref[view, 3] = opacity(sum(depths) * rate)


def composite_slots(table, rate, own, sibling, chips):
    blocks = [own, sibling, *chips]
    _, rows, columns = own.shape[2:]
    (image,) = call(
        slots_kernel, [((2, 4, rows, columns), F32)], "VV" + "V" * len(blocks), [], 1 << 10, 1 << 10,
        table, rate, *blocks,
    )
    return image


def swap(x, stride, n):
    return lax.ppermute(x, "light", [(i, i ^ stride) for i in range(n)])


def halves_below(keep, sibling, sums, stride, n):
    odd = (lax.axis_index("light") // stride) % 2 == 1
    below = lower(sums, 2 * stride, n)
    other = swap(below + jnp.where(odd, 0.0, keep), stride, n)
    return below + jnp.where(odd, sibling, 0.0), other


def lower(x, stride, n):
    if stride == n:
        return jnp.zeros_like(x)
    odd = (lax.axis_index("light") // stride) % 2 == 1
    if 2 * stride == n:
        return jnp.where(odd, swap(x, stride, n), 0.0)
    half = x.shape[0] // 2
    first, last = x[:half], x[half:]
    keep, sibling = jnp.where(odd, last, first), swap(jnp.where(odd, first, last), stride, n)
    mine, other = halves_below(keep, sibling, keep + sibling, stride, n)
    return jnp.where(odd, jnp.concatenate([other, mine]), jnp.concatenate([mine, other]))


def shards(depth_n, light_n, density, light_rate, view_rate, centers, rank):
    samples, rows, columns = density.shape
    rho = density.reshape(samples * rows, columns)
    half = samples // 2
    light = light_rate.reshape(1, -1)
    whole, part = (samples * rows, columns), (half, columns)
    sem = pltpu.SemaphoreType.DMA
    (send,) = call(
        functools.partial(send_kernel, half, rows), [(part, F32)], "A",
        [pltpu.VMEM((half * rows, columns), jnp.bfloat16), sem], 1 << 20, 1 << 19, rho,
    )
    own = columns // depth_n
    sliced = own == LANES and depth_n <= 8 and depth_n & (depth_n - 1) == 0
    table = (TONES + 2 * depth_n if sliced else TONES, LANES)
    keep, rho = call(
        functools.partial(keep_kernel, half, rows), [(part, F32), (whole, jnp.bfloat16)], "A", [sem], 1 << 20, 1 << 20, rho,
    )
    total, table = call(
        functools.partial(table_kernel, sliced), [((rows, columns), F32), (table, F32)], "Vss", [], 1 << 20, 1 << 20,
        rho, rank, centers,
    )
    sibling = swap(send, 1, light_n)
    sums = keep + sibling
    near, far, red, green, blue = call(
        functools.partial(pre_kernel, samples, rows, 256), [(whole, F32)] * 5, "VVVVV",
        [pltpu.VMEM(whole, F32)], 1 << 20, 12 << 20, rho, total, light, view_rate, table,
    )
    mine, other = halves_below(keep, sibling, sums, 1, light_n)
    place = lax.axis_index("depth")
    rate = lax.dynamic_slice_in_dim(view_rate, place * own, own, axis=1)
    packed = total
    for second, below in enumerate((mine, other)):
        (packed,) = call(
            functools.partial(post_kernel, rows, second, sliced), [((2, columns // (2 * LANES), 7, rows, LANES), F32)], "VVVVVVVVV",
            [pltpu.VMEM(part, F32)], 1 << 10, 1 << 10,
            below, light, table, near, far, red, green, blue, packed,
        )
    if sliced:
        def send_to(x, stride):
            return lax.ppermute(x, "depth", [(i, i ^ stride) for i in range(depth_n)])

        got = send_to(packed[1], 1)
        chips = [send_to(jnp.stack([packed[0, chip], got[chip]]), 2 * chip) for chip in range(1, depth_n // 2)]
        return composite_slots(table, rate, packed, got, chips)
    parts = packed.transpose(1, 0, 2, 3, 4).reshape(columns // LANES, 7, rows, LANES)
    if own % LANES == 0:
        parts = parts.reshape(depth_n, own // LANES, 7, rows, LANES).transpose(0, 2, 3, 1, 4)
    else:
        parts = parts.reshape(columns // LANES, 7, rows, LANES // own, own).transpose(0, 3, 1, 2, 4)
    got = lax.all_to_all(parts.reshape(depth_n, 7, rows, own), "depth", split_axis=0, concat_axis=0, tiled=True)
    return composite(got, rate, rank)


def solution(mesh):
    return jax.shard_map(
        functools.partial(shards, mesh.shape["depth"], mesh.shape["light"]),
        mesh=mesh,
        in_specs=(P("depth", "light", None), P(), P(), P(), P()),
        out_specs=P(None, None, "light", "depth"),
        check_vma=False,
    )
```

```python
import functools
import math

import jax
import jax.numpy as jnp
from jax import lax
from jax.experimental import pallas as pl
from jax.experimental.pallas import tpu as pltpu
from jax.sharding import PartitionSpec as P

F32 = jnp.float32
LOG2E = math.log2(math.e)
LANES = 128
TONES = 8


def sample_sums(rho, samples, rows):
    wide = (samples, samples * rows)
    target = lax.broadcasted_iota(jnp.int32, wide, 0)
    source = lax.broadcasted_iota(jnp.int32, wide, 1)
    return jnp.dot((source // rows == target).astype(jnp.bfloat16), rho, preferred_element_type=F32)


def sums_kernel(rows, places, sliced, rho_hbm, rank_hbm, center_hbm, *refs):
    *out_refs, table_ref, rho_ref, sums_ref, rank_ref, center_ref, sems = refs
    copy = pltpu.make_async_copy(rho_hbm, rho_ref, sems.at[0])
    small = pltpu.make_async_copy(rank_hbm, rank_ref, sems.at[1]), pltpu.make_async_copy(center_hbm, center_ref, sems.at[2])
    copy.start()
    for part in small:
        part.start()
    for part in small:
        part.wait()
    for k in range(3):
        c = jnp.full((1, LANES), center_ref[k], F32)
        table_ref[k : k + 1, :] = c * (16.0 * LOG2E)
        table_ref[3 + k : 4 + k, :] = 4.0 * jnp.exp2(c * c * (-8.0 * LOG2E))
    if sliced:
        bricks = rank_ref.shape[1]
        place = lax.axis_index("depth")
        for view in range(2):
            for slot in range(bricks):
                row = TONES + bricks * view + slot
                table_ref[row : row + 1, :] = jnp.full((1, LANES), rank_ref[view, place ^ slot].astype(F32))
    copy.wait()
    samples = sums_ref.shape[0]
    half = samples // 2
    for first in (0, half):
        sums_ref[first : first + half, :] = sample_sums(rho_ref[first * rows : (first + half) * rows, :], half, rows)
    odd = lax.axis_index("light") % 2
    for out_ref, (even_first, odd_first) in zip(out_refs, places, strict=True):
        first = pl.multiple_of(even_first + odd * (odd_first - even_first), 8)
        out_ref[...] = sums_ref[pl.ds(first, out_ref.shape[0]), :]


def pair_kernel(hold_ref, given_ref, cross_ref, pair_ref, late_ref):
    many = hold_ref.shape[0]
    pair_ref[...] = hold_ref[...] + given_ref[...]
    late_ref[:many, :] = hold_ref[...]
    late_ref[many:, :] = cross_ref[...]


def upper_kernel(straight_ref, across_ref, same_ref, cross_ref, below_ref, send_ref):
    me = lax.axis_index("light")
    few = same_ref.shape[0]
    below = jnp.where(me >= 2, straight_ref[...] + across_ref[...], 0.0)
    below_ref[...] = below
    send_ref[:few, :] = below + jnp.where(me % 2 == 1, 0.0, same_ref[...])


def pre_kernel(
    samples, rows, width, rho_ref, light_ref, view_ref, table_ref,
    near_ref, far_ref, red_ref, green_ref, blue_ref, total_ref, above_ref,
):
    columns = rho_ref.shape[1]
    narrow = (rows, samples * rows)
    of_row = lax.broadcasted_iota(jnp.int32, narrow, 1) % rows == lax.broadcasted_iota(jnp.int32, narrow, 0)
    total_ref[...] = jnp.dot(of_row.astype(jnp.bfloat16), rho_ref[...], preferred_element_type=F32)
    block = 256
    square = (block, block)
    i = lax.broadcasted_iota(jnp.int32, square, 0)
    j = lax.broadcasted_iota(jnp.int32, square, 1)
    above = ((i // rows == j // rows) & (j < i)).astype(jnp.bfloat16)
    for start in range(0, samples * rows, block):
        above_ref[start : start + block, :] = jnp.dot(
            above, rho_ref[start : start + block, :], preferred_element_type=F32
        )

    shape = (rows, width)
    tone = [jnp.broadcast_to(jnp.concatenate([table_ref[k : k + 1, :]] * (width // LANES), 1), shape) for k in range(3)]
    for first in range(0, columns, width):
        at = pl.ds(first, width)
        light = jnp.broadcast_to(light_ref[:, at] * LOG2E, shape)
        r0, r1 = view_ref[0:1, at], view_ref[1:2, at]
        fade = [jnp.broadcast_to(c, shape) for c in (r0, r0 * r0 * 0.5, r0 * r0 * r0 * (1 / 6))]
        grow = [jnp.broadcast_to(c, shape) for c in (r1, r1 * r1 * 0.5, r1 * r1 * r1 * (1 / 6))]

        def pair(step, carry):
            clear, behind = carry
            two = rho_ref[pl.ds(pl.multiple_of(step * 2 * rows, 2 * rows), 2 * rows), at].astype(F32)
            for part in range(2):
                rho = two[part * rows : (part + 1) * rows]
                here = pl.ds(pl.multiple_of((step * 2 + part) * rows, rows), rows)
                tint = jnp.exp2(rho * rho * (-8.0 * LOG2E) - light * above_ref[here, at])
                w0 = clear * (rho * (fade[0] - rho * (fade[1] - rho * fade[2])))
                clear = clear - w0
                w1 = behind * (rho * (grow[0] + rho * (grow[1] + rho * grow[2])))
                behind = behind + w1
                near_ref[here, at] = w0 * tint
                far_ref[here, at] = w1 * tint
                for k, color_ref in enumerate((red_ref, green_ref, blue_ref)):
                    color_ref[here, at] = jnp.exp2(rho * tone[k])
            return clear, behind

        start = (jnp.ones(shape, F32), jnp.exp2(total_ref[:, at] * view_ref[1:2, at] * -LOG2E))
        lax.fori_loop(0, samples // 2, pair, start, unroll=True)


def straight_below(refs, below_ref):
    same, given = (ref[...] for ref in refs)
    me = lax.axis_index("light")
    below_ref[...] = jnp.where(me >= 2, same, 0.0) + jnp.where(me % 2 == 1, given, 0.0)


def crossed_below(refs, below_ref):
    mine, other, cross, late = (ref[...] for ref in refs)
    few, many = mine.shape[0], cross.shape[0]
    me = lax.axis_index("light")
    odd = me % 2 == 1
    below_ref[:few, :] = jnp.where(odd, other[:few], mine)
    below_ref[few : 2 * few, :] = jnp.where(odd, mine + late[many:], other[:few])
    below_ref[2 * few :, :] = jnp.where(me >= 2, cross, 0.0) + jnp.where(odd, late[:many], 0.0)


def whole_below(refs, below_ref):
    first = 0
    for ref in refs:
        below_ref[first : first + ref.shape[0], :] = ref[...]
        first += ref.shape[0]


def post_kernel(
    rows, second, runs, sliced, assemble, light_ref, table_ref, near_ref, far_ref, red_ref, green_ref, blue_ref, rest_ref, *refs
):
    *refs, out_ref, lit_ref = refs
    assemble(refs, lit_ref)
    _, columns = lit_ref.shape
    place = lax.axis_index("depth") if sliced else 0
    chip, core = place // 2, place % 2
    odd = lax.axis_index("light") % 2
    firsts = [even_first + odd * (odd_first - even_first) for even_first, odd_first, _ in runs]
    groups = [(first, start) for first, (_, _, count) in zip(firsts, runs, strict=True) for start in range(0, count, 8)]
    lit_ref[...] = jnp.exp2(lit_ref[...] * (light_ref[...] * -LOG2E))
    width = 2 * LANES
    shape = (rows, width)
    scales = [jnp.broadcast_to(table_ref[3 + k : 4 + k, :], (rows, LANES)) for k in range(3)]
    for slot in range(columns // width):
        at = pl.ds(pl.multiple_of((slot ^ chip) * width, width), width)
        sums = [jnp.zeros(shape, F32)] * 6
        for group, (first, start) in enumerate(groups):
            lit = lit_ref[group * 8 : group * 8 + 8, at]
            for part in range(8):
                here = pl.ds(pl.multiple_of((first + start + part) * rows, rows), rows)
                shade = jnp.broadcast_to(lit[part : part + 1], shape)
                weights = near_ref[here, at] * shade, far_ref[here, at] * shade
                colors = [ref[here, at] for ref in (red_ref, green_ref, blue_ref)]
                sums = [sums[3 * v + k] + weights[v] * colors[k] for v in range(2) for k in range(3)]
        for tile in range(2):
            lanes = slice(tile * LANES, (tile + 1) * LANES)
            for n in range(6):
                value = sums[n][:, lanes] * scales[n % 3]
                if second:
                    value = value + rest_ref[tile ^ core, slot, n]
                out_ref[tile ^ core, slot, n] = value
            out_ref[tile ^ core, slot, 6] = rest_ref[tile ^ core, slot, 6] if second else rest_ref[:, at][:, lanes]


def call(kernel, outs, spaces, scratch, flops, moved, *args, limit=8):
    specs = {"v": pl.BlockSpec(memory_space=pltpu.VMEM), "s": pl.BlockSpec(memory_space=pltpu.SMEM), "a": pl.BlockSpec(memory_space=pl.ANY)}
    forced = {"V": pltpu.VMEM, "A": pltpu.HBM, "S": pltpu.SMEM}
    args = [pltpu.with_memory_space_constraint(a, forced[k]) if k in forced else a for a, k in zip(args, spaces, strict=True)]
    return pl.pallas_call(
        kernel,
        out_shape=tuple(pltpu.VMEM(o, t) for o, t in outs),
        in_specs=[specs[k.lower()] for k in spaces],
        out_specs=tuple([specs["v"]] * len(outs)),
        scratch_shapes=scratch,
        cost_estimate=pl.CostEstimate(flops=flops, bytes_accessed=moved, transcendentals=0),
        compiler_params=pltpu.CompilerParams(vmem_limit_bytes=limit << 20),
    )(*args)


def composite_kernel(bricks, got_ref, rate_ref, rank_ref, out_ref, order_ref):
    shape = out_ref.shape[2:]
    for view in range(2):
        def place(d, carry, view=view):
            order_ref[view, rank_ref[view, d]] = d
            return carry

        lax.fori_loop(0, bricks, place, 0, unroll=bricks <= 8)
        rate = jnp.broadcast_to(rate_ref[view : view + 1, :], shape)

        def nearer(p, carry, view=view, rate=rate):
            front, red, green, blue = carry
            d = order_ref[view, p]
            seen = jnp.exp2(front * rate * -LOG2E)
            red = red + got_ref[d, 3 * view] * seen
            green = green + got_ref[d, 3 * view + 1] * seen
            blue = blue + got_ref[d, 3 * view + 2] * seen
            return front + got_ref[d, 6], red, green, blue

        zero = jnp.zeros(shape, F32)
        depth, *colors = lax.fori_loop(0, bricks, nearer, (zero,) * 4, unroll=bricks <= 8)
        for k in range(3):
            out_ref[view, k] = colors[k]
        out_ref[view, 3] = opacity(depth * rate)


def composite(got, rate, rank):
    bricks, _, rows, columns = got.shape
    vmem, smem = pl.BlockSpec(memory_space=pltpu.VMEM), pl.BlockSpec(memory_space=pltpu.SMEM)
    return pl.pallas_call(
        functools.partial(composite_kernel, bricks),
        out_shape=jax.ShapeDtypeStruct((2, 4, rows, columns), F32),
        in_specs=[vmem, vmem, smem],
        out_specs=vmem,
        scratch_shapes=[pltpu.SMEM((2, bricks), jnp.int32)],
        compiler_params=pltpu.CompilerParams(vmem_limit_bytes=8 << 20),
    )(pltpu.with_memory_space_constraint(got, pltpu.VMEM), rate, rank)


def opacity(depth):
    small = jnp.full(depth.shape, 1.0, F32)
    for n in range(8, 1, -1):
        small = 1.0 - depth * (1.0 / n) * small
    return jnp.where(depth < 0.35, depth * small, 1.0 - jnp.exp2(depth * -LOG2E))


def slots_kernel(table_ref, rate_ref, own_ref, sibling_ref, *refs):
    *chip_refs, out_ref = refs
    shape = out_ref.shape[2:]
    blocks = [own_ref.at[0, 0], sibling_ref.at[0]] + [ref.at[t] for ref in chip_refs for t in range(2)]
    depths = [block[6] for block in blocks]
    for view in range(2):
        rate = jnp.broadcast_to(rate_ref[view : view + 1, :], shape)
        first = TONES + len(blocks) * view
        ranks = [jnp.broadcast_to(table_ref[first + slot : first + slot + 1, :], shape) for slot in range(len(blocks))]
        colors = [jnp.zeros(shape, F32)] * 3
        for i, block in enumerate(blocks):
            front = jnp.zeros(shape, F32)
            for j, depth in enumerate(depths):
                if j != i:
                    front = front + jnp.where(ranks[j] < ranks[i], depth, 0.0)
            seen = jnp.exp2(front * rate * -LOG2E)
            colors = [colors[k] + block[3 * view + k] * seen for k in range(3)]
        for k in range(3):
            out_ref[view, k] = colors[k]
        out_ref[view, 3] = opacity(sum(depths) * rate)


def composite_slots(table, rate, own, sibling, chips):
    blocks = [own, sibling, *chips]
    _, rows, columns = own.shape[2:]
    (image,) = call(
        slots_kernel, [((2, 4, rows, columns), F32)], "VV" + "V" * len(blocks), [], 1 << 10, 1 << 10,
        table, rate, *blocks,
    )
    return image


def swap(x, stride, n):
    return lax.ppermute(x, "light", [(i, i ^ stride) for i in range(n)])


def lower(x, stride, n):
    if stride == n:
        return jnp.zeros_like(x)
    odd = (lax.axis_index("light") // stride) % 2 == 1
    if 2 * stride == n:
        return jnp.where(odd, swap(x, stride, n), 0.0)
    half = x.shape[0] // 2
    first, last = x[:half], x[half:]
    keep, sibling = jnp.where(odd, last, first), swap(jnp.where(odd, first, last), stride, n)
    below = lower(keep + sibling, 2 * stride, n)
    other = swap(below + jnp.where(odd, 0.0, keep), stride, n)
    mine = below + jnp.where(odd, sibling, 0.0)
    return jnp.where(odd, jnp.concatenate([other, mine]), jnp.concatenate([mine, other]))


def lower_of_four(give, hold, same, cross):
    given = swap(give, 1, 4)
    straight, across = swap(same, 2, 4), swap(cross, 3, 4)
    columns = same.shape[1]
    pair, late = call(
        pair_kernel, [(hold.shape, F32), ((hold.shape[0] + cross.shape[0], columns), F32)], "VVV", [], 1 << 10, 1 << 10, hold, given, cross
    )
    from_same, from_cross = swap(pair, 2, 4), swap(pair, 3, 4)
    late = swap(late, 1, 4)
    mine, send = call(
        upper_kernel, [(same.shape, F32), ((same.shape[0], columns), F32)], "VVVV", [], 1 << 34, 1 << 10, straight, across, same, cross
    )
    other = swap(send, 1, 4)
    return (from_same, given), (mine, other, from_cross, late)


def shards(depth_n, light_n, density, light_rate, view_rate, centers, rank):
    samples, rows, columns = density.shape
    rho = density.reshape(samples * rows, columns)
    light = light_rate.reshape(1, -1)
    whole = (samples * rows, columns)
    few, many = samples // 8, 3 * samples // 8
    places = ((2 * few + many, 2 * few), (2 * few, 2 * few + many), (0, few), (few, 0)) if light_n == 4 else ((0, 0),)
    sizes = (many, many, few, few) if light_n == 4 else (samples,)
    own = columns // depth_n
    sliced = own == LANES and depth_n <= 8 and depth_n & (depth_n - 1) == 0
    table = (TONES + 2 * depth_n if sliced else TONES, LANES)
    *sums, table, rho = call(
        functools.partial(sums_kernel, rows, places, sliced),
        [((n, columns), F32) for n in sizes] + [(table, F32), (whole, jnp.bfloat16)], "AAA",
        [pltpu.VMEM((samples, columns), F32), pltpu.SMEM(rank.shape, jnp.int32), pltpu.SMEM(centers.shape, F32), pltpu.SemaphoreType.DMA((3,))],
        1 << 20, 1 << 20, rho, rank, centers,
    )
    if light_n == 4:
        pieces = lower_of_four(*sums)
        assemble = straight_below, crossed_below
    else:
        below = lower(sums[0], 1, light_n)
        pieces = [below[2 * few : 2 * few + many]], [below[: 2 * few], below[2 * few + many :]]
        assemble = whole_below, whole_below
    near, far, red, green, blue, total = call(
        functools.partial(pre_kernel, samples, rows, 256), [(whole, F32)] * 5 + [((rows, columns), F32)], "VVVV",
        [pltpu.VMEM(whole, F32)], 1 << 20, 12 << 20, rho, light, view_rate, table,
    )
    place = lax.axis_index("depth")
    rate = lax.dynamic_slice_in_dim(view_rate, place * own, own, axis=1)
    packed = total
    late = 2 * few + many
    runs = ((2 * few, late, many),), ((0, 0, 2 * few), (late, 2 * few, many))
    if light_n != 4:
        runs = ((2 * few, 2 * few, many),), ((0, 0, 2 * few), (late, late, many))
    for second in range(2):
        (packed,) = call(
            functools.partial(post_kernel, rows, second, runs[second], sliced, assemble[second]),
            [((2, columns // (2 * LANES), 7, rows, LANES), F32)], "V" * (8 + len(pieces[second])),
            [pltpu.VMEM((sum(run[2] for run in runs[second]), columns), F32)], 1 << 10, 1 << 10,
            light, table, near, far, red, green, blue, packed, *pieces[second],
        )
    if sliced:
        def send_to(x, stride):
            return lax.ppermute(x, "depth", [(i, i ^ stride) for i in range(depth_n)])

        got = send_to(packed[1], 1)
        chips = [send_to(jnp.stack([packed[0, chip], got[chip]]), 2 * chip) for chip in range(1, depth_n // 2)]
        return composite_slots(table, rate, packed, got, chips)
    parts = packed.transpose(1, 0, 2, 3, 4).reshape(columns // LANES, 7, rows, LANES)
    if own % LANES == 0:
        parts = parts.reshape(depth_n, own // LANES, 7, rows, LANES).transpose(0, 2, 3, 1, 4)
    else:
        parts = parts.reshape(columns // LANES, 7, rows, LANES // own, own).transpose(0, 3, 1, 2, 4)
    got = lax.all_to_all(parts.reshape(depth_n, 7, rows, own), "depth", split_axis=0, concat_axis=0, tiled=True)
    return composite(got, rate, rank)


def solution(mesh):
    return jax.shard_map(
        functools.partial(shards, mesh.shape["depth"], mesh.shape["light"]),
        mesh=mesh,
        in_specs=(P("depth", "light", None), P(), P(), P(), P()),
        out_specs=P(None, None, "light", "depth"),
        check_vma=False,
    )
```

```python
import functools
import math

import jax
import jax.numpy as jnp
from jax import lax
from jax.experimental import pallas as pl
from jax.experimental.pallas import tpu as pltpu
from jax.sharding import PartitionSpec as P

F32 = jnp.float32
LOG2E = math.log2(math.e)
LANES = 128
TONES = 8


def sample_sums(rho, samples, rows):
    wide = (samples, samples * rows)
    target = lax.broadcasted_iota(jnp.int32, wide, 0)
    source = lax.broadcasted_iota(jnp.int32, wide, 1)
    return jnp.dot((source // rows == target).astype(jnp.bfloat16), rho, preferred_element_type=F32)


def sums_kernel(rows, places, sliced, rho_hbm, rank_hbm, center_hbm, *refs):
    *out_refs, table_ref, rho_ref, sums_ref, rank_ref, center_ref, sems = refs
    copy = pltpu.make_async_copy(rho_hbm, rho_ref, sems.at[0])
    small = pltpu.make_async_copy(rank_hbm, rank_ref, sems.at[1]), pltpu.make_async_copy(center_hbm, center_ref, sems.at[2])
    copy.start()
    for part in small:
        part.start()
    for part in small:
        part.wait()
    for k in range(3):
        c = jnp.full((1, LANES), center_ref[k], F32)
        table_ref[k : k + 1, :] = c * (16.0 * LOG2E)
        table_ref[3 + k : 4 + k, :] = 4.0 * jnp.exp2(c * c * (-8.0 * LOG2E))
    if sliced:
        bricks = rank_ref.shape[1]
        place = lax.axis_index("depth")
        for view in range(2):
            for slot in range(bricks):
                row = TONES + bricks * view + slot
                table_ref[row : row + 1, :] = jnp.full((1, LANES), rank_ref[view, place ^ slot].astype(F32))
    copy.wait()
    samples = sums_ref.shape[0]
    half = samples // 2
    for first in (0, half):
        sums_ref[first : first + half, :] = sample_sums(rho_ref[first * rows : (first + half) * rows, :], half, rows)
    odd = lax.axis_index("light") % 2
    for out_ref, (even_first, odd_first) in zip(out_refs, places, strict=True):
        first = pl.multiple_of(even_first + odd * (odd_first - even_first), 8)
        out_ref[...] = sums_ref[pl.ds(first, out_ref.shape[0]), :]


def pair_kernel(hold_ref, given_ref, pair_ref):
    pair_ref[...] = hold_ref[...] + given_ref[...]


def upper_kernel(straight_ref, across_ref, same_ref, cross_ref, below_ref, send_ref):
    me = lax.axis_index("light")
    odd = me % 2 == 1
    few = same_ref.shape[0]
    below = jnp.where(me >= 2, straight_ref[...] + across_ref[...], 0.0)
    below_ref[...] = below
    send_ref[:few, :] = below + jnp.where(odd, 0.0, same_ref[...])
    send_ref[few:, :] = cross_ref[...]


def late_kernel(late_ref, send_ref, add_ref, out_ref):
    odd = lax.axis_index("light") % 2 == 1
    add_ref[...] = jnp.where(odd, late_ref[...], 0.0)
    out_ref[...] = send_ref[...]


def pre_kernel(
    samples, rows, width, rho_ref, light_ref, view_ref, table_ref,
    near_ref, far_ref, red_ref, green_ref, blue_ref, total_ref, above_ref,
):
    columns = rho_ref.shape[1]
    narrow = (rows, samples * rows)
    of_row = lax.broadcasted_iota(jnp.int32, narrow, 1) % rows == lax.broadcasted_iota(jnp.int32, narrow, 0)
    total_ref[...] = jnp.dot(of_row.astype(jnp.bfloat16), rho_ref[...], preferred_element_type=F32)
    block = 256
    square = (block, block)
    i = lax.broadcasted_iota(jnp.int32, square, 0)
    j = lax.broadcasted_iota(jnp.int32, square, 1)
    above = ((i // rows == j // rows) & (j < i)).astype(jnp.bfloat16)
    for start in range(0, samples * rows, block):
        above_ref[start : start + block, :] = jnp.dot(
            above, rho_ref[start : start + block, :], preferred_element_type=F32
        )

    shape = (rows, width)
    tone = [jnp.broadcast_to(jnp.concatenate([table_ref[k : k + 1, :]] * (width // LANES), 1), shape) for k in range(3)]
    for first in range(0, columns, width):
        at = pl.ds(first, width)
        light = jnp.broadcast_to(light_ref[:, at] * LOG2E, shape)
        r0, r1 = view_ref[0:1, at], view_ref[1:2, at]
        fade = [jnp.broadcast_to(c, shape) for c in (r0, r0 * r0 * 0.5, r0 * r0 * r0 * (1 / 6))]
        grow = [jnp.broadcast_to(c, shape) for c in (r1, r1 * r1 * 0.5, r1 * r1 * r1 * (1 / 6))]

        def pair(step, carry):
            clear, behind = carry
            two = rho_ref[pl.ds(pl.multiple_of(step * 2 * rows, 2 * rows), 2 * rows), at].astype(F32)
            for part in range(2):
                rho = two[part * rows : (part + 1) * rows]
                here = pl.ds(pl.multiple_of((step * 2 + part) * rows, rows), rows)
                tint = jnp.exp2(rho * rho * (-8.0 * LOG2E) - light * above_ref[here, at])
                w0 = clear * (rho * (fade[0] - rho * (fade[1] - rho * fade[2])))
                clear = clear - w0
                w1 = behind * (rho * (grow[0] + rho * (grow[1] + rho * grow[2])))
                behind = behind + w1
                near_ref[here, at] = w0 * tint
                far_ref[here, at] = w1 * tint
                for k, color_ref in enumerate((red_ref, green_ref, blue_ref)):
                    color_ref[here, at] = jnp.exp2(rho * tone[k])
            return clear, behind

        start = (jnp.ones(shape, F32), jnp.exp2(total_ref[:, at] * view_ref[1:2, at] * -LOG2E))
        lax.fori_loop(0, samples // 2, pair, start, unroll=True)


def straight_below(refs, below_ref):
    same, given = (ref[...] for ref in refs)
    me = lax.axis_index("light")
    below_ref[...] = jnp.where(me >= 2, same, 0.0) + jnp.where(me % 2 == 1, given, 0.0)


def crossed_below(refs, below_ref):
    mine, other, cross, late = (ref[...] for ref in refs)
    few = mine.shape[0]
    me = lax.axis_index("light")
    odd = me % 2 == 1
    below_ref[:few, :] = jnp.where(odd, other[:few], mine)
    below_ref[few : 2 * few, :] = jnp.where(odd, mine + other[few:], other[:few])
    below_ref[2 * few :, :] = jnp.where(me >= 2, cross, 0.0) + late


def whole_below(refs, below_ref):
    first = 0
    for ref in refs:
        below_ref[first : first + ref.shape[0], :] = ref[...]
        first += ref.shape[0]


def post_kernel(
    rows, second, runs, sliced, assemble, light_ref, table_ref, near_ref, far_ref, red_ref, green_ref, blue_ref, rest_ref, *refs
):
    *refs, out_ref, lit_ref = refs
    assemble(refs, lit_ref)
    _, columns = lit_ref.shape
    place = lax.axis_index("depth") if sliced else 0
    chip, core = place // 2, place % 2
    odd = lax.axis_index("light") % 2
    firsts = [even_first + odd * (odd_first - even_first) for even_first, odd_first, _ in runs]
    groups = [(first, start) for first, (_, _, count) in zip(firsts, runs, strict=True) for start in range(0, count, 8)]
    lit_ref[...] = jnp.exp2(lit_ref[...] * (light_ref[...] * -LOG2E))
    width = 2 * LANES
    shape = (rows, width)
    scales = [jnp.broadcast_to(table_ref[3 + k : 4 + k, :], (rows, LANES)) for k in range(3)]
    for slot in range(columns // width):
        at = pl.ds(pl.multiple_of((slot ^ chip) * width, width), width)
        sums = [jnp.zeros(shape, F32)] * 6
        for group, (first, start) in enumerate(groups):
            lit = lit_ref[group * 8 : group * 8 + 8, at]
            for part in range(8):
                here = pl.ds(pl.multiple_of((first + start + part) * rows, rows), rows)
                shade = jnp.broadcast_to(lit[part : part + 1], shape)
                weights = near_ref[here, at] * shade, far_ref[here, at] * shade
                colors = [ref[here, at] for ref in (red_ref, green_ref, blue_ref)]
                sums = [sums[3 * v + k] + weights[v] * colors[k] for v in range(2) for k in range(3)]
        for tile in range(2):
            lanes = slice(tile * LANES, (tile + 1) * LANES)
            for n in range(6):
                value = sums[n][:, lanes] * scales[n % 3]
                if second:
                    value = value + rest_ref[tile ^ core, slot, n]
                out_ref[tile ^ core, slot, n] = value
            out_ref[tile ^ core, slot, 6] = rest_ref[tile ^ core, slot, 6] if second else rest_ref[:, at][:, lanes]


def call(kernel, outs, spaces, scratch, flops, moved, *args, limit=8):
    specs = {"v": pl.BlockSpec(memory_space=pltpu.VMEM), "s": pl.BlockSpec(memory_space=pltpu.SMEM), "a": pl.BlockSpec(memory_space=pl.ANY)}
    forced = {"V": pltpu.VMEM, "A": pltpu.HBM, "S": pltpu.SMEM}
    args = [pltpu.with_memory_space_constraint(a, forced[k]) if k in forced else a for a, k in zip(args, spaces, strict=True)]
    return pl.pallas_call(
        kernel,
        out_shape=tuple(pltpu.VMEM(o, t) for o, t in outs),
        in_specs=[specs[k.lower()] for k in spaces],
        out_specs=tuple([specs["v"]] * len(outs)),
        scratch_shapes=scratch,
        cost_estimate=pl.CostEstimate(flops=flops, bytes_accessed=moved, transcendentals=0),
        compiler_params=pltpu.CompilerParams(vmem_limit_bytes=limit << 20),
    )(*args)


def composite_kernel(bricks, got_ref, rate_ref, rank_ref, out_ref, order_ref):
    shape = out_ref.shape[2:]
    for view in range(2):
        def place(d, carry, view=view):
            order_ref[view, rank_ref[view, d]] = d
            return carry

        lax.fori_loop(0, bricks, place, 0, unroll=bricks <= 8)
        rate = jnp.broadcast_to(rate_ref[view : view + 1, :], shape)

        def nearer(p, carry, view=view, rate=rate):
            front, red, green, blue = carry
            d = order_ref[view, p]
            seen = jnp.exp2(front * rate * -LOG2E)
            red = red + got_ref[d, 3 * view] * seen
            green = green + got_ref[d, 3 * view + 1] * seen
            blue = blue + got_ref[d, 3 * view + 2] * seen
            return front + got_ref[d, 6], red, green, blue

        zero = jnp.zeros(shape, F32)
        depth, *colors = lax.fori_loop(0, bricks, nearer, (zero,) * 4, unroll=bricks <= 8)
        for k in range(3):
            out_ref[view, k] = colors[k]
        out_ref[view, 3] = opacity(depth * rate)


def composite(got, rate, rank):
    bricks, _, rows, columns = got.shape
    vmem, smem = pl.BlockSpec(memory_space=pltpu.VMEM), pl.BlockSpec(memory_space=pltpu.SMEM)
    return pl.pallas_call(
        functools.partial(composite_kernel, bricks),
        out_shape=jax.ShapeDtypeStruct((2, 4, rows, columns), F32),
        in_specs=[vmem, vmem, smem],
        out_specs=vmem,
        scratch_shapes=[pltpu.SMEM((2, bricks), jnp.int32)],
        compiler_params=pltpu.CompilerParams(vmem_limit_bytes=8 << 20),
    )(pltpu.with_memory_space_constraint(got, pltpu.VMEM), rate, rank)


def opacity(depth):
    small = jnp.full(depth.shape, 1.0, F32)
    for n in range(8, 1, -1):
        small = 1.0 - depth * (1.0 / n) * small
    return jnp.where(depth < 0.35, depth * small, 1.0 - jnp.exp2(depth * -LOG2E))


def slots_kernel(table_ref, rate_ref, own_ref, sibling_ref, *refs):
    *chip_refs, out_ref = refs
    shape = out_ref.shape[2:]
    blocks = [own_ref.at[0, 0], sibling_ref.at[0]] + [ref.at[t] for ref in chip_refs for t in range(2)]
    depths = [block[6] for block in blocks]
    for view in range(2):
        rate = jnp.broadcast_to(rate_ref[view : view + 1, :], shape)
        first = TONES + len(blocks) * view
        ranks = [jnp.broadcast_to(table_ref[first + slot : first + slot + 1, :], shape) for slot in range(len(blocks))]
        colors = [jnp.zeros(shape, F32)] * 3
        for i, block in enumerate(blocks):
            front = jnp.zeros(shape, F32)
            for j, depth in enumerate(depths):
                if j != i:
                    front = front + jnp.where(ranks[j] < ranks[i], depth, 0.0)
            seen = jnp.exp2(front * rate * -LOG2E)
            colors = [colors[k] + block[3 * view + k] * seen for k in range(3)]
        for k in range(3):
            out_ref[view, k] = colors[k]
        out_ref[view, 3] = opacity(sum(depths) * rate)


def composite_slots(table, rate, own, sibling, chips):
    blocks = [own, sibling, *chips]
    _, rows, columns = own.shape[2:]
    (image,) = call(
        slots_kernel, [((2, 4, rows, columns), F32)], "VV" + "V" * len(blocks), [], 1 << 10, 1 << 10,
        table, rate, *blocks,
    )
    return image


def swap(x, stride, n):
    return lax.ppermute(x, "light", [(i, i ^ stride) for i in range(n)])


def lower(x, stride, n):
    if stride == n:
        return jnp.zeros_like(x)
    odd = (lax.axis_index("light") // stride) % 2 == 1
    if 2 * stride == n:
        return jnp.where(odd, swap(x, stride, n), 0.0)
    half = x.shape[0] // 2
    first, last = x[:half], x[half:]
    keep, sibling = jnp.where(odd, last, first), swap(jnp.where(odd, first, last), stride, n)
    below = lower(keep + sibling, 2 * stride, n)
    other = swap(below + jnp.where(odd, 0.0, keep), stride, n)
    mine = below + jnp.where(odd, sibling, 0.0)
    return jnp.where(odd, jnp.concatenate([other, mine]), jnp.concatenate([mine, other]))


def lower_of_four(give, hold, same, cross):
    given = swap(give, 1, 4)
    straight, across = swap(same, 2, 4), swap(cross, 3, 4)
    columns = same.shape[1]
    late = swap(hold, 1, 4)
    (pair,) = call(pair_kernel, [(hold.shape, F32)], "VV", [], 1 << 10, 1 << 10, hold, given)
    from_same, from_cross = swap(pair, 2, 4), swap(pair, 3, 4)
    sent = 2 * same.shape[0], columns
    mine, send = call(
        upper_kernel, [(same.shape, F32), (sent, F32)], "VVVV", [], 1 << 30, 1 << 10, straight, across, same, cross
    )
    late, send = call(late_kernel, [(late.shape, F32), (sent, F32)], "VV", [], 1 << 10, 1 << 10, late, send)
    other = swap(send, 1, 4)
    return (from_same, given), (mine, other, from_cross, late)


def shards(depth_n, light_n, density, light_rate, view_rate, centers, rank):
    samples, rows, columns = density.shape
    rho = density.reshape(samples * rows, columns)
    light = light_rate.reshape(1, -1)
    whole = (samples * rows, columns)
    few, many = samples // 8, 3 * samples // 8
    places = ((2 * few + many, 2 * few), (2 * few, 2 * few + many), (0, few), (few, 0)) if light_n == 4 else ((0, 0),)
    sizes = (many, many, few, few) if light_n == 4 else (samples,)
    own = columns // depth_n
    sliced = own == LANES and depth_n <= 8 and depth_n & (depth_n - 1) == 0
    table = (TONES + 2 * depth_n if sliced else TONES, LANES)
    *sums, table, rho = call(
        functools.partial(sums_kernel, rows, places, sliced),
        [((n, columns), F32) for n in sizes] + [(table, F32), (whole, jnp.bfloat16)], "AAA",
        [pltpu.VMEM((samples, columns), F32), pltpu.SMEM(rank.shape, jnp.int32), pltpu.SMEM(centers.shape, F32), pltpu.SemaphoreType.DMA((3,))],
        1 << 20, 1 << 20, rho, rank, centers,
    )
    if light_n == 4:
        pieces = lower_of_four(*sums)
        assemble = straight_below, crossed_below
    else:
        below = lower(sums[0], 1, light_n)
        pieces = [below[2 * few : 2 * few + many]], [below[: 2 * few], below[2 * few + many :]]
        assemble = whole_below, whole_below
    near, far, red, green, blue, total = call(
        functools.partial(pre_kernel, samples, rows, 256), [(whole, F32)] * 5 + [((rows, columns), F32)], "VVVV",
        [pltpu.VMEM(whole, F32)], 1 << 20, 12 << 20, rho, light, view_rate, table,
    )
    place = lax.axis_index("depth")
    rate = lax.dynamic_slice_in_dim(view_rate, place * own, own, axis=1)
    packed = total
    late = 2 * few + many
    runs = ((2 * few, late, many),), ((0, 0, 2 * few), (late, 2 * few, many))
    if light_n != 4:
        runs = ((2 * few, 2 * few, many),), ((0, 0, 2 * few), (late, late, many))
    for second in range(2):
        (packed,) = call(
            functools.partial(post_kernel, rows, second, runs[second], sliced, assemble[second]),
            [((2, columns // (2 * LANES), 7, rows, LANES), F32)], "V" * (8 + len(pieces[second])),
            [pltpu.VMEM((sum(run[2] for run in runs[second]), columns), F32)], 1 << 10, 1 << 10,
            light, table, near, far, red, green, blue, packed, *pieces[second],
        )
    if sliced:
        def send_to(x, stride):
            return lax.ppermute(x, "depth", [(i, i ^ stride) for i in range(depth_n)])

        got = send_to(packed[1], 1)
        chips = [send_to(jnp.stack([packed[0, chip], got[chip]]), 2 * chip) for chip in range(1, depth_n // 2)]
        return composite_slots(table, rate, packed, got, chips)
    parts = packed.transpose(1, 0, 2, 3, 4).reshape(columns // LANES, 7, rows, LANES)
    if own % LANES == 0:
        parts = parts.reshape(depth_n, own // LANES, 7, rows, LANES).transpose(0, 2, 3, 1, 4)
    else:
        parts = parts.reshape(columns // LANES, 7, rows, LANES // own, own).transpose(0, 3, 1, 2, 4)
    got = lax.all_to_all(parts.reshape(depth_n, 7, rows, own), "depth", split_axis=0, concat_axis=0, tiled=True)
    return composite(got, rate, rank)


def solution(mesh):
    return jax.shard_map(
        functools.partial(shards, mesh.shape["depth"], mesh.shape["light"]),
        mesh=mesh,
        in_specs=(P("depth", "light", None), P(), P(), P(), P()),
        out_specs=P(None, None, "light", "depth"),
        check_vma=False,
    )
```

```python
import functools
import math

import jax
import jax.numpy as jnp
from jax import lax
from jax.experimental import pallas as pl
from jax.experimental.pallas import tpu as pltpu
from jax.sharding import PartitionSpec as P

F32 = jnp.float32
LOG2E = math.log2(math.e)
LANES = 128
TONES = 8


def sample_sums(rho, samples, rows):
    wide = (samples, samples * rows)
    target = lax.broadcasted_iota(jnp.int32, wide, 0)
    source = lax.broadcasted_iota(jnp.int32, wide, 1)
    return jnp.dot((source // rows == target).astype(jnp.bfloat16), rho, preferred_element_type=F32)


def sums_kernel(rows, places, sliced, rho_hbm, rank_hbm, center_hbm, *refs):
    *out_refs, table_ref, rho_ref, sums_ref, rank_ref, center_ref, sems = refs
    copy = pltpu.make_async_copy(rho_hbm, rho_ref, sems.at[0])
    small = pltpu.make_async_copy(rank_hbm, rank_ref, sems.at[1]), pltpu.make_async_copy(center_hbm, center_ref, sems.at[2])
    copy.start()
    for part in small:
        part.start()
    for part in small:
        part.wait()
    for k in range(3):
        c = jnp.full((1, LANES), center_ref[k], F32)
        table_ref[k : k + 1, :] = c * (16.0 * LOG2E)
        table_ref[3 + k : 4 + k, :] = 4.0 * jnp.exp2(c * c * (-8.0 * LOG2E))
    if sliced:
        bricks = rank_ref.shape[1]
        place = lax.axis_index("depth")
        for view in range(2):
            for slot in range(bricks):
                row = TONES + bricks * view + slot
                table_ref[row : row + 1, :] = jnp.full((1, LANES), rank_ref[view, place ^ slot].astype(F32))
    copy.wait()
    samples = sums_ref.shape[0]
    half = samples // 2
    for first in (0, half):
        sums_ref[first : first + half, :] = sample_sums(rho_ref[first * rows : (first + half) * rows, :], half, rows)
    odd = lax.axis_index("light") % 2
    for out_ref, pieces in zip(out_refs, places, strict=True):
        row, width = 0, out_ref.shape[1]
        for even_first, odd_first, count, column in pieces:
            first = pl.multiple_of(even_first + odd * (odd_first - even_first), 8)
            out_ref[row : row + count, :] = sums_ref[pl.ds(first, count), column : column + width]
            row += count


def pair_kernel(hold_ref, given_ref, pair_ref):
    pair_ref[...] = hold_ref[...] + given_ref[...]


def upper_kernel(straight_ref, across_ref, same_ref, below_ref, send_ref):
    me = lax.axis_index("light")
    odd = me % 2 == 1
    below = jnp.where(me >= 2, straight_ref[...] + across_ref[...], 0.0)
    below_ref[...] = below
    send_ref[...] = below + jnp.where(odd, 0.0, same_ref[...])


def late_kernel(late_ref, add_ref):
    add_ref[...] = jnp.where(lax.axis_index("light") % 2 == 1, late_ref[...], 0.0)


def pre_kernel(
    samples, rows, width, rho_ref, light_ref, view_ref, table_ref, _,
    near_ref, far_ref, red_ref, green_ref, blue_ref, total_ref, above_ref,
):
    columns = rho_ref.shape[1]
    narrow = (rows, samples * rows)
    of_row = lax.broadcasted_iota(jnp.int32, narrow, 1) % rows == lax.broadcasted_iota(jnp.int32, narrow, 0)
    total_ref[...] = jnp.dot(of_row.astype(jnp.bfloat16), rho_ref[...], preferred_element_type=F32)
    block = 256
    square = (block, block)
    i = lax.broadcasted_iota(jnp.int32, square, 0)
    j = lax.broadcasted_iota(jnp.int32, square, 1)
    above = ((i // rows == j // rows) & (j < i)).astype(jnp.bfloat16)
    for start in range(0, samples * rows, block):
        above_ref[start : start + block, :] = jnp.dot(
            above, rho_ref[start : start + block, :], preferred_element_type=F32
        )

    shape = (rows, width)
    tone = [jnp.broadcast_to(jnp.concatenate([table_ref[k : k + 1, :]] * (width // LANES), 1), shape) for k in range(3)]
    for first in range(0, columns, width):
        at = pl.ds(first, width)
        light = jnp.broadcast_to(light_ref[:, at] * LOG2E, shape)
        r0, r1 = view_ref[0:1, at], view_ref[1:2, at]
        fade = [jnp.broadcast_to(c, shape) for c in (r0, r0 * r0 * 0.5, r0 * r0 * r0 * (1 / 6))]
        grow = [jnp.broadcast_to(c, shape) for c in (r1, r1 * r1 * 0.5, r1 * r1 * r1 * (1 / 6))]

        def pair(step, carry):
            clear, behind = carry
            two = rho_ref[pl.ds(pl.multiple_of(step * 2 * rows, 2 * rows), 2 * rows), at].astype(F32)
            for part in range(2):
                rho = two[part * rows : (part + 1) * rows]
                here = pl.ds(pl.multiple_of((step * 2 + part) * rows, rows), rows)
                tint = jnp.exp2(rho * rho * (-8.0 * LOG2E) - light * above_ref[here, at])
                w0 = clear * (rho * (fade[0] - rho * (fade[1] - rho * fade[2])))
                clear = clear - w0
                w1 = behind * (rho * (grow[0] + rho * (grow[1] + rho * grow[2])))
                behind = behind + w1
                near_ref[here, at] = w0 * tint
                far_ref[here, at] = w1 * tint
                for k, color_ref in enumerate((red_ref, green_ref, blue_ref)):
                    color_ref[here, at] = jnp.exp2(rho * tone[k])
            return clear, behind

        start = (jnp.ones(shape, F32), jnp.exp2(total_ref[:, at] * view_ref[1:2, at] * -LOG2E))
        lax.fori_loop(0, samples // 2, pair, start, unroll=True)


def straight_below(refs, below_ref):
    same, given = (ref[...] for ref in refs)
    me = lax.axis_index("light")
    below_ref[...] = jnp.where(me >= 2, same, 0.0) + jnp.where(me % 2 == 1, given, 0.0)


def first_below(refs, below_ref):
    mine, other, late = (ref[...] for ref in refs)
    few = mine.shape[0]
    odd = lax.axis_index("light") % 2 == 1
    below_ref[:few, :] = jnp.where(odd, other, mine)
    below_ref[few:, :] = jnp.where(odd, mine + late[-few:], other)


def crossed_below(refs, below_ref):
    cross, late = (ref[...] for ref in refs)
    below_ref[...] = jnp.where(lax.axis_index("light") >= 2, cross, 0.0) + late[: cross.shape[0]]


def whole_below(refs, below_ref):
    count, columns = refs[0].shape
    below_ref[:count, :] = refs[0][:, : columns // 2]
    below_ref[count:, :] = refs[0][:, columns // 2 :]


def post_kernel(
    rows, second, runs, sliced, assemble, light_ref, table_ref, near_ref, far_ref, red_ref, green_ref, blue_ref, rest_ref, *refs
):
    *refs, out_ref, lit_ref = refs
    assemble(refs, lit_ref)
    columns = near_ref.shape[1]
    place = lax.axis_index("depth") if sliced else 0
    chip, core = place // 2, place % 2
    odd = lax.axis_index("light") % 2
    width = 2 * LANES
    shape = (rows, width)
    scales = [jnp.broadcast_to(table_ref[3 + k : 4 + k, :], (rows, LANES)) for k in range(3)]
    for side, pieces in enumerate(runs):
        start = side * columns // 2
        light = light_ref[:, start : start + columns // 2] * -LOG2E
        for _, _, count, row in pieces:
            lit_ref[row : row + count, :] = jnp.exp2(lit_ref[row : row + count, :] * light)
    for block in range(columns // width):
        at = slice(block * width, (block + 1) * width)
        side, here_at = divmod(block * width, columns // 2)
        sums = [jnp.zeros(shape, F32)] * 6
        for even_first, odd_first, count, row in runs[side]:
            first = even_first + odd * (odd_first - even_first)
            for group in range(0, count, 8):
                lit = lit_ref[row + group : row + group + 8, here_at : here_at + width]
                for part in range(8):
                    here = pl.ds(pl.multiple_of((first + group + part) * rows, rows), rows)
                    shade = jnp.broadcast_to(lit[part : part + 1], shape)
                    weights = near_ref[here, at] * shade, far_ref[here, at] * shade
                    colors = [ref[here, at] for ref in (red_ref, green_ref, blue_ref)]
                    sums = [sums[3 * v + k] + weights[v] * colors[k] for v in range(2) for k in range(3)]
        slot = block ^ chip
        for tile in range(2):
            lanes = slice(tile * LANES, (tile + 1) * LANES)
            for n in range(6):
                value = sums[n][:, lanes] * scales[n % 3]
                if second:
                    value = value + rest_ref[tile ^ core, slot, n]
                out_ref[tile ^ core, slot, n] = value
            out_ref[tile ^ core, slot, 6] = rest_ref[tile ^ core, slot, 6] if second else rest_ref[:, at][:, lanes]


def call(kernel, outs, spaces, scratch, flops, moved, *args, limit=8):
    specs = {"v": pl.BlockSpec(memory_space=pltpu.VMEM), "s": pl.BlockSpec(memory_space=pltpu.SMEM), "a": pl.BlockSpec(memory_space=pl.ANY)}
    forced = {"V": pltpu.VMEM, "A": pltpu.HBM, "S": pltpu.SMEM}
    args = [pltpu.with_memory_space_constraint(a, forced[k]) if k in forced else a for a, k in zip(args, spaces, strict=True)]
    return pl.pallas_call(
        kernel,
        out_shape=tuple(pltpu.VMEM(o, t) for o, t in outs),
        in_specs=[specs[k.lower()] for k in spaces],
        out_specs=tuple([specs["v"]] * len(outs)),
        scratch_shapes=scratch,
        cost_estimate=pl.CostEstimate(flops=flops, bytes_accessed=moved, transcendentals=0),
        compiler_params=pltpu.CompilerParams(vmem_limit_bytes=limit << 20),
    )(*args)


def composite_kernel(bricks, got_ref, rate_ref, rank_ref, out_ref, order_ref):
    shape = out_ref.shape[2:]
    for view in range(2):
        def place(d, carry, view=view):
            order_ref[view, rank_ref[view, d]] = d
            return carry

        lax.fori_loop(0, bricks, place, 0, unroll=bricks <= 8)
        rate = jnp.broadcast_to(rate_ref[view : view + 1, :], shape)

        def nearer(p, carry, view=view, rate=rate):
            front, red, green, blue = carry
            d = order_ref[view, p]
            seen = jnp.exp2(front * rate * -LOG2E)
            red = red + got_ref[d, 3 * view] * seen
            green = green + got_ref[d, 3 * view + 1] * seen
            blue = blue + got_ref[d, 3 * view + 2] * seen
            return front + got_ref[d, 6], red, green, blue

        zero = jnp.zeros(shape, F32)
        depth, *colors = lax.fori_loop(0, bricks, nearer, (zero,) * 4, unroll=bricks <= 8)
        for k in range(3):
            out_ref[view, k] = colors[k]
        out_ref[view, 3] = opacity(depth * rate)


def composite(got, rate, rank):
    bricks, _, rows, columns = got.shape
    vmem, smem = pl.BlockSpec(memory_space=pltpu.VMEM), pl.BlockSpec(memory_space=pltpu.SMEM)
    return pl.pallas_call(
        functools.partial(composite_kernel, bricks),
        out_shape=jax.ShapeDtypeStruct((2, 4, rows, columns), F32),
        in_specs=[vmem, vmem, smem],
        out_specs=vmem,
        scratch_shapes=[pltpu.SMEM((2, bricks), jnp.int32)],
        compiler_params=pltpu.CompilerParams(vmem_limit_bytes=8 << 20),
    )(pltpu.with_memory_space_constraint(got, pltpu.VMEM), rate, rank)


def opacity(depth):
    small = jnp.full(depth.shape, 1.0, F32)
    for n in range(8, 1, -1):
        small = 1.0 - depth * (1.0 / n) * small
    return jnp.where(depth < 0.35, depth * small, 1.0 - jnp.exp2(depth * -LOG2E))


def slots_kernel(table_ref, rate_ref, own_ref, sibling_ref, *refs):
    *chip_refs, out_ref = refs
    shape = out_ref.shape[2:]
    blocks = [own_ref.at[0, 0], sibling_ref.at[0]] + [ref.at[t] for ref in chip_refs for t in range(2)]
    depths = [block[6] for block in blocks]
    for view in range(2):
        rate = jnp.broadcast_to(rate_ref[view : view + 1, :], shape)
        first = TONES + len(blocks) * view
        ranks = [jnp.broadcast_to(table_ref[first + slot : first + slot + 1, :], shape) for slot in range(len(blocks))]
        colors = [jnp.zeros(shape, F32)] * 3
        for i, block in enumerate(blocks):
            front = jnp.zeros(shape, F32)
            for j, depth in enumerate(depths):
                if j != i:
                    front = front + jnp.where(ranks[j] < ranks[i], depth, 0.0)
            seen = jnp.exp2(front * rate * -LOG2E)
            colors = [colors[k] + block[3 * view + k] * seen for k in range(3)]
        for k in range(3):
            out_ref[view, k] = colors[k]
        out_ref[view, 3] = opacity(sum(depths) * rate)


def composite_slots(table, rate, own, sibling, chips):
    blocks = [own, sibling, *chips]
    _, rows, columns = own.shape[2:]
    (image,) = call(
        slots_kernel, [((2, 4, rows, columns), F32)], "VV" + "V" * len(blocks), [], 1 << 10, 1 << 10,
        table, rate, *blocks,
    )
    return image


def swap(x, stride, n):
    return lax.ppermute(x, "light", [(i, i ^ stride) for i in range(n)])


def lower(x, stride, n):
    if stride == n:
        return jnp.zeros_like(x)
    odd = (lax.axis_index("light") // stride) % 2 == 1
    if 2 * stride == n:
        return jnp.where(odd, swap(x, stride, n), 0.0)
    half = x.shape[0] // 2
    first, last = x[:half], x[half:]
    keep, sibling = jnp.where(odd, last, first), swap(jnp.where(odd, first, last), stride, n)
    below = lower(keep + sibling, 2 * stride, n)
    other = swap(below + jnp.where(odd, 0.0, keep), stride, n)
    mine = below + jnp.where(odd, sibling, 0.0)
    return jnp.where(odd, jnp.concatenate([other, mine]), jnp.concatenate([mine, other]))


def lower_of_four(give, hold, same, cross, late):
    given = swap(give, 1, 4)
    straight, across = swap(same, 2, 4), swap(cross, 3, 4)
    columns = same.shape[1]
    late = swap(late, 1, 4)
    (pair,) = call(pair_kernel, [(hold.shape, F32)], "VV", [], 1 << 10, 1 << 10, hold, given)
    from_same, from_cross = swap(pair, 2, 4), swap(pair, 3, 4)
    mine, send = call(upper_kernel, [(same.shape, F32)] * 2, "VVV", [], 1 << 31, 1 << 10, straight, across, same)
    (late,) = call(late_kernel, [(late.shape, F32)], "V", [], 1 << 10, 1 << 10, late)
    other = swap(send, 1, 4)
    return (from_same, given), (mine, other, late), (from_cross, late)


def shards(depth_n, light_n, density, light_rate, view_rate, centers, rank):
    samples, rows, columns = density.shape
    rho = density.reshape(samples * rows, columns)
    light = light_rate.reshape(1, -1)
    whole = (samples * rows, columns)
    sizes = [(samples // 8 * (side + 1), samples // 8 * (3 - side), columns // 2 * side) for side in range(2)]
    give = [(2 * few + many, 2 * few, many, at) for few, many, at in sizes]
    hold = [(2 * few, 2 * few + many, many, at) for few, many, at in sizes]
    same = [(0, few, few, at) for few, many, at in sizes]
    cross = [(few, 0, few, at) for few, many, at in sizes]
    places, width = [give, hold, same, cross, hold + cross], columns // 2
    if light_n != 4:
        places, width = [[(0, 0, samples, 0)]], columns
    own = columns // depth_n
    sliced = own == LANES and depth_n <= 8 and depth_n & (depth_n - 1) == 0
    table = (TONES + 2 * depth_n if sliced else TONES, LANES)
    *sums, table, rho = call(
        functools.partial(sums_kernel, rows, places, sliced),
        [((sum(piece[2] for piece in pieces), width), F32) for pieces in places] + [(table, F32), (whole, jnp.bfloat16)], "AAA",
        [pltpu.VMEM((samples, columns), F32), pltpu.SMEM(rank.shape, jnp.int32), pltpu.SMEM(centers.shape, F32), pltpu.SemaphoreType.DMA((3,))],
        1 << 20, 1 << 20, rho, rank, centers,
    )
    if light_n == 4:
        pieces = lower_of_four(*sums)
        assemble = straight_below, first_below, crossed_below
    else:
        below = lower(sums[0], 1, light_n)
        pieces = [below[: samples // 2]], [below[samples // 2 :]]
        assemble = whole_below, whole_below
    near, far, red, green, blue, total = call(
        functools.partial(pre_kernel, samples, rows, 256), [(whole, F32)] * 5 + [((rows, columns), F32)], "VVVVV",
        [pltpu.VMEM(whole, F32)], 1 << 20, 12 << 20, rho, light, view_rate, table, pieces[1][-1],
    )
    place = lax.axis_index("depth")
    rate = lax.dynamic_slice_in_dim(view_rate, place * own, own, axis=1)
    packed = total
    runs = [[], []], [[], []], [[], []]
    first, last = sum(few for few, _, _ in sizes), sum(many for _, many, _ in sizes)
    row, much = 0, 0
    for side, (few, many, _) in enumerate(sizes):
        runs[0][side].append((2 * few, 2 * few + many, many, much))
        runs[1][side] += [(0, 0, few, row), (few, few, few, first + row)]
        runs[2][side].append((2 * few + many, 2 * few, many, much))
        row, much = row + few, much + many
    rows_of = last, 2 * first, last
    if light_n != 4:
        half = samples // 2
        runs = [[[(start, start, half, half * side)] for side in range(2)] for start in (0, half)]
        rows_of = samples, samples
    for second in range(len(runs)):
        (packed,) = call(
            functools.partial(post_kernel, rows, second > 0, runs[second], sliced, assemble[second]),
            [((2, columns // (2 * LANES), 7, rows, LANES), F32)], "V" * (8 + len(pieces[second])),
            [pltpu.VMEM((rows_of[second], columns // 2), F32)], 1 << 10, 1 << 10,
            light, table, near, far, red, green, blue, packed, *pieces[second],
        )
    if sliced:
        def send_to(x, stride):
            return lax.ppermute(x, "depth", [(i, i ^ stride) for i in range(depth_n)])

        got = send_to(packed[1], 1)
        chips = [send_to(jnp.stack([packed[0, chip], got[chip]]), 2 * chip) for chip in range(1, depth_n // 2)]
        return composite_slots(table, rate, packed, got, chips)
    parts = packed.transpose(1, 0, 2, 3, 4).reshape(columns // LANES, 7, rows, LANES)
    if own % LANES == 0:
        parts = parts.reshape(depth_n, own // LANES, 7, rows, LANES).transpose(0, 2, 3, 1, 4)
    else:
        parts = parts.reshape(columns // LANES, 7, rows, LANES // own, own).transpose(0, 3, 1, 2, 4)
    got = lax.all_to_all(parts.reshape(depth_n, 7, rows, own), "depth", split_axis=0, concat_axis=0, tiled=True)
    return composite(got, rate, rank)


def solution(mesh):
    return jax.shard_map(
        functools.partial(shards, mesh.shape["depth"], mesh.shape["light"]),
        mesh=mesh,
        in_specs=(P("depth", "light", None), P(), P(), P(), P()),
        out_specs=P(None, None, "light", "depth"),
        check_vma=False,
    )
```

```python
import functools
import math

import jax
import jax.numpy as jnp
from jax import lax
from jax.experimental import pallas as pl
from jax.experimental.pallas import tpu as pltpu
from jax.sharding import PartitionSpec as P

F32 = jnp.float32
LOG2E = math.log2(math.e)
LANES = 128
TONES = 8


def sample_sums(rho, samples, rows):
    wide = (samples, samples * rows)
    target = lax.broadcasted_iota(jnp.int32, wide, 0)
    source = lax.broadcasted_iota(jnp.int32, wide, 1)
    return jnp.dot((source // rows == target).astype(jnp.bfloat16), rho, preferred_element_type=F32)


def sums_kernel(rows, places, sliced, rho_hbm, rank_hbm, center_hbm, *refs):
    *out_refs, table_ref, rho_ref, sums_ref, rank_ref, center_ref, sems = refs
    copy = pltpu.make_async_copy(rho_hbm, rho_ref, sems.at[0])
    small = pltpu.make_async_copy(rank_hbm, rank_ref, sems.at[1]), pltpu.make_async_copy(center_hbm, center_ref, sems.at[2])
    copy.start()
    for part in small:
        part.start()
    for part in small:
        part.wait()
    for k in range(3):
        c = jnp.full((1, LANES), center_ref[k], F32)
        table_ref[k : k + 1, :] = c * (16.0 * LOG2E)
        table_ref[3 + k : 4 + k, :] = 4.0 * jnp.exp2(c * c * (-8.0 * LOG2E))
    if sliced:
        bricks = rank_ref.shape[1]
        place = lax.axis_index("depth")
        for view in range(2):
            for slot in range(bricks):
                row = TONES + bricks * view + slot
                table_ref[row : row + 1, :] = jnp.full((1, LANES), rank_ref[view, place ^ slot].astype(F32))
    copy.wait()
    samples = sums_ref.shape[0]
    half = samples // 2
    for first in (0, half):
        sums_ref[first : first + half, :] = sample_sums(rho_ref[first * rows : (first + half) * rows, :], half, rows)
    odd = lax.axis_index("light") % 2
    for out_ref, pieces in zip(out_refs, places, strict=True):
        row, width = 0, out_ref.shape[1]
        for even_first, odd_first, count, column in pieces:
            first = pl.multiple_of(even_first + odd * (odd_first - even_first), 8)
            out_ref[row : row + count, :] = sums_ref[pl.ds(first, count), column : column + width]
            row += count


def pair_kernel(hold_ref, given_ref, pair_ref):
    pair_ref[...] = hold_ref[...] + given_ref[...]


def upper_kernel(straight_ref, across_ref, same_ref, below_ref, send_ref):
    me = lax.axis_index("light")
    odd = me % 2 == 1
    below = jnp.where(me >= 2, straight_ref[...] + across_ref[...], 0.0)
    below_ref[...] = below
    send_ref[...] = below + jnp.where(odd, 0.0, same_ref[...])


def late_kernel(late_ref, add_ref):
    add_ref[...] = jnp.where(lax.axis_index("light") % 2 == 1, late_ref[...], 0.0)


def pre_kernel(
    samples, rows, width, rho_ref, light_ref, view_ref, table_ref, _,
    near_ref, far_ref, red_ref, green_ref, blue_ref, total_ref, above_ref,
):
    columns = rho_ref.shape[1]
    narrow = (rows, samples * rows)
    of_row = lax.broadcasted_iota(jnp.int32, narrow, 1) % rows == lax.broadcasted_iota(jnp.int32, narrow, 0)
    total_ref[...] = jnp.dot(of_row.astype(jnp.bfloat16), rho_ref[...], preferred_element_type=F32)
    block = 256
    square = (block, block)
    i = lax.broadcasted_iota(jnp.int32, square, 0)
    j = lax.broadcasted_iota(jnp.int32, square, 1)
    above = ((i // rows == j // rows) & (j < i)).astype(jnp.bfloat16)
    for start in range(0, samples * rows, block):
        above_ref[start : start + block, :] = jnp.dot(
            above, rho_ref[start : start + block, :], preferred_element_type=F32
        )

    shape = (rows, width)
    tone = [jnp.broadcast_to(jnp.concatenate([table_ref[k : k + 1, :]] * (width // LANES), 1), shape) for k in range(3)]
    for first in range(0, columns, width):
        at = pl.ds(first, width)
        light = jnp.broadcast_to(light_ref[:, at] * LOG2E, shape)
        r0, r1 = view_ref[0:1, at], view_ref[1:2, at]
        fade = [jnp.broadcast_to(c, shape) for c in (r0, r0 * r0 * 0.5, r0 * r0 * r0 * (1 / 6))]
        grow = [jnp.broadcast_to(c, shape) for c in (r1, r1 * r1 * 0.5, r1 * r1 * r1 * (1 / 6))]

        def pair(step, carry):
            clear, behind = carry
            two = rho_ref[pl.ds(pl.multiple_of(step * 2 * rows, 2 * rows), 2 * rows), at].astype(F32)
            for part in range(2):
                rho = two[part * rows : (part + 1) * rows]
                here = pl.ds(pl.multiple_of((step * 2 + part) * rows, rows), rows)
                tint = jnp.exp2(rho * rho * (-8.0 * LOG2E) - light * above_ref[here, at])
                w0 = clear * (rho * (fade[0] - rho * (fade[1] - rho * fade[2])))
                clear = clear - w0
                w1 = behind * (rho * (grow[0] + rho * (grow[1] + rho * grow[2])))
                behind = behind + w1
                near_ref[here, at] = w0 * tint
                far_ref[here, at] = w1 * tint
                for k, color_ref in enumerate((red_ref, green_ref, blue_ref)):
                    color_ref[here, at] = jnp.exp2(rho * tone[k])
            return clear, behind

        start = (jnp.ones(shape, F32), jnp.exp2(total_ref[:, at] * view_ref[1:2, at] * -LOG2E))
        lax.fori_loop(0, samples // 2, pair, start, unroll=True)


def straight_below(refs, below_ref):
    same, given = (ref[...] for ref in refs)
    me = lax.axis_index("light")
    below_ref[...] = jnp.where(me >= 2, same, 0.0) + jnp.where(me % 2 == 1, given, 0.0)


def first_below(refs, below_ref):
    mine, other, late = (ref[...] for ref in refs)
    few = mine.shape[0]
    odd = lax.axis_index("light") % 2 == 1
    below_ref[:few, :] = jnp.where(odd, other, mine)
    below_ref[few:, :] = jnp.where(odd, mine + late[-few:], other)


def crossed_below(refs, below_ref):
    cross, late = (ref[...] for ref in refs)
    below_ref[...] = jnp.where(lax.axis_index("light") >= 2, cross, 0.0) + late[: cross.shape[0]]


def whole_below(refs, below_ref):
    count, columns = refs[0].shape
    below_ref[:count, :] = refs[0][:, : columns // 2]
    below_ref[count:, :] = refs[0][:, columns // 2 :]


def post_kernel(
    rows, second, runs, sliced, assemble, light_ref, table_ref, near_ref, far_ref, red_ref, green_ref, blue_ref, rest_ref, *refs
):
    *refs, out_ref, lit_ref = refs
    assemble(refs, lit_ref)
    columns = near_ref.shape[1]
    place = lax.axis_index("depth") if sliced else 0
    chip, core = place // 2, place % 2
    odd = lax.axis_index("light") % 2
    width = 2 * LANES
    shape = (rows, width)
    scales = [jnp.broadcast_to(table_ref[3 + k : 4 + k, :], (rows, LANES)) for k in range(3)]
    for side, pieces in enumerate(runs):
        start = side * columns // 2
        light = light_ref[:, start : start + columns // 2] * -LOG2E
        for _, _, count, row in pieces:
            lit_ref[row : row + count, :] = jnp.exp2(lit_ref[row : row + count, :] * light)
    for block in range(columns // width):
        at = slice(block * width, (block + 1) * width)
        side, here_at = divmod(block * width, columns // 2)
        sums = [jnp.zeros(shape, F32)] * 6
        for even_first, odd_first, count, row in runs[side]:
            first = even_first + odd * (odd_first - even_first)
            for group in range(0, count, 8):
                lit = lit_ref[row + group : row + group + 8, here_at : here_at + width]
                for part in range(8):
                    here = pl.ds(pl.multiple_of((first + group + part) * rows, rows), rows)
                    shade = jnp.broadcast_to(lit[part : part + 1], shape)
                    weights = near_ref[here, at] * shade, far_ref[here, at] * shade
                    colors = [ref[here, at] for ref in (red_ref, green_ref, blue_ref)]
                    sums = [sums[3 * v + k] + weights[v] * colors[k] for v in range(2) for k in range(3)]
        slot = block ^ chip
        for tile in range(2):
            lanes = slice(tile * LANES, (tile + 1) * LANES)
            for n in range(6):
                value = sums[n][:, lanes] * scales[n % 3]
                if second:
                    value = value + rest_ref[tile ^ core, slot, n]
                out_ref[tile ^ core, slot, n] = value
            out_ref[tile ^ core, slot, 6] = rest_ref[tile ^ core, slot, 6] if second else rest_ref[:, at][:, lanes]


def post_tiles_kernel(
    rows, which, runs, assemble, light_ref, table_ref, near_ref, far_ref, red_ref, green_ref, blue_ref, rest_ref, *refs
):
    *refs, out_ref, lit_ref = refs
    assemble(refs, lit_ref)
    columns = near_ref.shape[1]
    place = lax.axis_index("depth")
    chip, core = place // 2, place % 2
    odd = lax.axis_index("light") % 2
    shape = (rows, LANES)
    scales = [jnp.broadcast_to(table_ref[3 + k : 4 + k, :], shape) for k in range(3)]
    blocks = columns // (2 * LANES)
    for side, pieces in enumerate(runs):
        start = side * columns // 2
        light = light_ref[:, start : start + columns // 2] * -LOG2E
        for _, _, count, row in pieces:
            lit_ref[row : row + count, :] = jnp.exp2(lit_ref[row : row + count, :] * light)
        tiles = range(side * blocks // 2, (side + 1) * blocks // 2)
        lanes = [pl.ds(pl.multiple_of((2 * tile + (which ^ core)) * LANES, LANES), LANES) for tile in tiles]
        near_lanes = [pl.ds(pl.multiple_of((2 * tile + (which ^ core)) * LANES - start, LANES), LANES) for tile in tiles]
        sums = [[jnp.zeros(shape, F32)] * 6 for _ in tiles]
        for even_first, odd_first, count, row in pieces:
            first = even_first + odd * (odd_first - even_first)
            for group in range(0, count, 8):
                lits = [lit_ref[row + group : row + group + 8, at] for at in near_lanes]
                for part in range(8):
                    here = pl.ds(pl.multiple_of((first + group + part) * rows, rows), rows)
                    for n, at in enumerate(lanes):
                        shade = jnp.broadcast_to(lits[n][part : part + 1], shape)
                        weights = near_ref[here, at] * shade, far_ref[here, at] * shade
                        colors = [ref[here, at] for ref in (red_ref, green_ref, blue_ref)]
                        sums[n] = [sums[n][3 * v + k] + weights[v] * colors[k] for v in range(2) for k in range(3)]
        for n, tile in enumerate(tiles):
            slot = tile ^ chip
            for channel in range(6):
                out_ref[slot, channel] = sums[n][channel] * scales[channel % 3] + rest_ref[which, slot, channel]
            out_ref[slot, 6] = rest_ref[which, slot, 6]


def call(kernel, outs, spaces, scratch, flops, moved, *args, limit=8):
    specs = {"v": pl.BlockSpec(memory_space=pltpu.VMEM), "s": pl.BlockSpec(memory_space=pltpu.SMEM), "a": pl.BlockSpec(memory_space=pl.ANY)}
    forced = {"V": pltpu.VMEM, "A": pltpu.HBM, "S": pltpu.SMEM}
    args = [pltpu.with_memory_space_constraint(a, forced[k]) if k in forced else a for a, k in zip(args, spaces, strict=True)]
    return pl.pallas_call(
        kernel,
        out_shape=tuple(pltpu.VMEM(o, t) for o, t in outs),
        in_specs=[specs[k.lower()] for k in spaces],
        out_specs=tuple([specs["v"]] * len(outs)),
        scratch_shapes=scratch,
        cost_estimate=pl.CostEstimate(flops=flops, bytes_accessed=moved, transcendentals=0),
        compiler_params=pltpu.CompilerParams(vmem_limit_bytes=limit << 20),
    )(*args)


def composite_kernel(bricks, got_ref, rate_ref, rank_ref, out_ref, order_ref):
    shape = out_ref.shape[2:]
    for view in range(2):
        def place(d, carry, view=view):
            order_ref[view, rank_ref[view, d]] = d
            return carry

        lax.fori_loop(0, bricks, place, 0, unroll=bricks <= 8)
        rate = jnp.broadcast_to(rate_ref[view : view + 1, :], shape)

        def nearer(p, carry, view=view, rate=rate):
            front, red, green, blue = carry
            d = order_ref[view, p]
            seen = jnp.exp2(front * rate * -LOG2E)
            red = red + got_ref[d, 3 * view] * seen
            green = green + got_ref[d, 3 * view + 1] * seen
            blue = blue + got_ref[d, 3 * view + 2] * seen
            return front + got_ref[d, 6], red, green, blue

        zero = jnp.zeros(shape, F32)
        depth, *colors = lax.fori_loop(0, bricks, nearer, (zero,) * 4, unroll=bricks <= 8)
        for k in range(3):
            out_ref[view, k] = colors[k]
        out_ref[view, 3] = opacity(depth * rate)


def composite(got, rate, rank):
    bricks, _, rows, columns = got.shape
    vmem, smem = pl.BlockSpec(memory_space=pltpu.VMEM), pl.BlockSpec(memory_space=pltpu.SMEM)
    return pl.pallas_call(
        functools.partial(composite_kernel, bricks),
        out_shape=jax.ShapeDtypeStruct((2, 4, rows, columns), F32),
        in_specs=[vmem, vmem, smem],
        out_specs=vmem,
        scratch_shapes=[pltpu.SMEM((2, bricks), jnp.int32)],
        compiler_params=pltpu.CompilerParams(vmem_limit_bytes=8 << 20),
    )(pltpu.with_memory_space_constraint(got, pltpu.VMEM), rate, rank)


def opacity(depth):
    small = jnp.full(depth.shape, 1.0, F32)
    for n in range(8, 1, -1):
        small = 1.0 - depth * (1.0 / n) * small
    return jnp.where(depth < 0.35, depth * small, 1.0 - jnp.exp2(depth * -LOG2E))


def slots_kernel(order, table_ref, rate_ref, own_ref, sibling_ref, *refs):
    *chip_refs, out_ref = refs
    shape = out_ref.shape[2:]
    chips = dict(zip(order, chip_refs, strict=True))
    blocks = [own_ref.at[0], sibling_ref.at[0]] + [chips[chip].at[t] for chip in sorted(order) for t in range(2)]
    depths = [block[6] for block in blocks]
    for view in range(2):
        rate = jnp.broadcast_to(rate_ref[view : view + 1, :], shape)
        first = TONES + len(blocks) * view
        ranks = [jnp.broadcast_to(table_ref[first + slot : first + slot + 1, :], shape) for slot in range(len(blocks))]
        colors = [jnp.zeros(shape, F32)] * 3
        for i, block in enumerate(blocks):
            front = jnp.zeros(shape, F32)
            for j, depth in enumerate(depths):
                if j != i:
                    front = front + jnp.where(ranks[j] < ranks[i], depth, 0.0)
            seen = jnp.exp2(front * rate * -LOG2E)
            colors = [colors[k] + block[3 * view + k] * seen for k in range(3)]
        for k in range(3):
            out_ref[view, k] = colors[k]
        out_ref[view, 3] = opacity(sum(depths) * rate)


def composite_slots(table, rate, own, sibling, order, chips):
    blocks = [own, sibling, *chips]
    _, rows, columns = own.shape[1:]
    (image,) = call(
        functools.partial(slots_kernel, order), [((2, 4, rows, columns), F32)], "VV" + "V" * len(blocks), [], 1 << 10, 1 << 10,
        table, rate, *blocks,
    )
    return image


def swap(x, stride, n):
    return lax.ppermute(x, "light", [(i, i ^ stride) for i in range(n)])


def lower(x, stride, n):
    if stride == n:
        return jnp.zeros_like(x)
    odd = (lax.axis_index("light") // stride) % 2 == 1
    if 2 * stride == n:
        return jnp.where(odd, swap(x, stride, n), 0.0)
    half = x.shape[0] // 2
    first, last = x[:half], x[half:]
    keep, sibling = jnp.where(odd, last, first), swap(jnp.where(odd, first, last), stride, n)
    below = lower(keep + sibling, 2 * stride, n)
    other = swap(below + jnp.where(odd, 0.0, keep), stride, n)
    mine = below + jnp.where(odd, sibling, 0.0)
    return jnp.where(odd, jnp.concatenate([other, mine]), jnp.concatenate([mine, other]))


def lower_of_four(give, hold, same, cross, late):
    given = swap(give, 1, 4)
    straight, across = swap(same, 2, 4), swap(cross, 3, 4)
    columns = same.shape[1]
    late = swap(late, 1, 4)
    (pair,) = call(pair_kernel, [(hold.shape, F32)], "VV", [], 1 << 10, 1 << 10, hold, given)
    from_same, from_cross = swap(pair, 2, 4), swap(pair, 3, 4)
    mine, send = call(upper_kernel, [(same.shape, F32)] * 2, "VVV", [], 1 << 31, 1 << 10, straight, across, same)
    (late,) = call(late_kernel, [(late.shape, F32)], "V", [], 1 << 10, 1 << 10, late)
    other = swap(send, 1, 4)
    return (from_same, given), (mine, other, late), (from_cross, late)


def shards(depth_n, light_n, density, light_rate, view_rate, centers, rank):
    samples, rows, columns = density.shape
    rho = density.reshape(samples * rows, columns)
    light = light_rate.reshape(1, -1)
    whole = (samples * rows, columns)
    sizes = [(samples // 8 * (side + 1), samples // 8 * (3 - side), columns // 2 * side) for side in range(2)]
    give = [(2 * few + many, 2 * few, many, at) for few, many, at in sizes]
    hold = [(2 * few, 2 * few + many, many, at) for few, many, at in sizes]
    same = [(0, few, few, at) for few, many, at in sizes]
    cross = [(few, 0, few, at) for few, many, at in sizes]
    places, width = [give, hold, same, cross, hold + cross], columns // 2
    if light_n != 4:
        places, width = [[(0, 0, samples, 0)]], columns
    own = columns // depth_n
    sliced = own == LANES and depth_n <= 8 and depth_n & (depth_n - 1) == 0
    table = (TONES + 2 * depth_n if sliced else TONES, LANES)
    *sums, table, rho = call(
        functools.partial(sums_kernel, rows, places, sliced),
        [((sum(piece[2] for piece in pieces), width), F32) for pieces in places] + [(table, F32), (whole, jnp.bfloat16)], "AAA",
        [pltpu.VMEM((samples, columns), F32), pltpu.SMEM(rank.shape, jnp.int32), pltpu.SMEM(centers.shape, F32), pltpu.SemaphoreType.DMA((3,))],
        1 << 20, 1 << 20, rho, rank, centers,
    )
    if light_n == 4:
        pieces = lower_of_four(*sums)
        assemble = straight_below, first_below, crossed_below
    else:
        below = lower(sums[0], 1, light_n)
        pieces = [below[: samples // 2]], [below[samples // 2 :]]
        assemble = whole_below, whole_below
    near, far, red, green, blue, total = call(
        functools.partial(pre_kernel, samples, rows, 256), [(whole, F32)] * 5 + [((rows, columns), F32)], "VVVVV",
        [pltpu.VMEM(whole, F32)], 1 << 20, 12 << 20, rho, light, view_rate, table, pieces[1][-1],
    )
    place = lax.axis_index("depth")
    rate = lax.dynamic_slice_in_dim(view_rate, place * own, own, axis=1)
    packed = total
    runs = [[], []], [[], []], [[], []]
    first, last = sum(few for few, _, _ in sizes), sum(many for _, many, _ in sizes)
    row, much = 0, 0
    for side, (few, many, _) in enumerate(sizes):
        runs[0][side].append((2 * few, 2 * few + many, many, much))
        runs[1][side] += [(0, 0, few, row), (few, few, few, first + row)]
        runs[2][side].append((2 * few + many, 2 * few, many, much))
        row, much = row + few, much + many
    rows_of = last, 2 * first, last
    if light_n != 4:
        half = samples // 2
        runs = [[[(start, start, half, half * side)] for side in range(2)] for start in (0, half)]
        rows_of = samples, samples
    def post(kernel, second, out, packed):
        return call(
            kernel, [(out, F32)], "V" * (8 + len(pieces[second])), [pltpu.VMEM((rows_of[second], columns // 2), F32)],
            1 << 10, 1 << 10, light, table, near, far, red, green, blue, packed, *pieces[second],
        )[0]

    packs = columns // (2 * LANES), 7, rows, LANES
    whole_runs = len(runs) - 1 if sliced else len(runs)
    for second in range(whole_runs):
        kernel = functools.partial(post_kernel, rows, second > 0, runs[second], sliced, assemble[second])
        packed = post(kernel, second, (2, *packs), packed)
    if sliced:
        def send_to(x, stride):
            return lax.ppermute(x, "depth", [(i, i ^ stride) for i in range(depth_n)])

        theirs, mine = (
            post(functools.partial(post_tiles_kernel, rows, which, runs[-1], assemble[-1]), len(runs) - 1, packs, packed)
            for which in (1, 0)
        )
        got = send_to(theirs, 1)
        order = sorted(range(1, depth_n // 2), key=lambda chip: (chip % 2, chip))
        sent = {chip: send_to(jnp.stack([mine[chip], got[chip]]), 2 * chip) for chip in order}
        return composite_slots(table, rate, mine, got, order, [sent[chip] for chip in order])
    parts = packed.transpose(1, 0, 2, 3, 4).reshape(columns // LANES, 7, rows, LANES)
    if own % LANES == 0:
        parts = parts.reshape(depth_n, own // LANES, 7, rows, LANES).transpose(0, 2, 3, 1, 4)
    else:
        parts = parts.reshape(columns // LANES, 7, rows, LANES // own, own).transpose(0, 3, 1, 2, 4)
    got = lax.all_to_all(parts.reshape(depth_n, 7, rows, own), "depth", split_axis=0, concat_axis=0, tiled=True)
    return composite(got, rate, rank)


def solution(mesh):
    return jax.shard_map(
        functools.partial(shards, mesh.shape["depth"], mesh.shape["light"]),
        mesh=mesh,
        in_specs=(P("depth", "light", None), P(), P(), P(), P()),
        out_specs=P(None, None, "light", "depth"),
        check_vma=False,
    )
```

```python
import functools
import math

import jax
import jax.numpy as jnp
from jax import lax
from jax.experimental import pallas as pl
from jax.experimental.pallas import tpu as pltpu
from jax.sharding import PartitionSpec as P

F32 = jnp.float32
LOG2E = math.log2(math.e)
LANES = 128
TONES = 8


def sample_sums(rho, samples, rows):
    wide = (samples, samples * rows)
    target = lax.broadcasted_iota(jnp.int32, wide, 0)
    source = lax.broadcasted_iota(jnp.int32, wide, 1)
    return jnp.dot((source // rows == target).astype(jnp.bfloat16), rho, preferred_element_type=F32)


def sums_kernel(rows, places, sliced, rho_hbm, rank_hbm, center_hbm, *refs):
    *out_refs, table_ref, rho_ref, sums_ref, rank_ref, center_ref, sems = refs
    copy = pltpu.make_async_copy(rho_hbm, rho_ref, sems.at[0])
    small = pltpu.make_async_copy(rank_hbm, rank_ref, sems.at[1]), pltpu.make_async_copy(center_hbm, center_ref, sems.at[2])
    copy.start()
    for part in small:
        part.start()
    for part in small:
        part.wait()
    for k in range(3):
        c = jnp.full((1, LANES), center_ref[k], F32)
        table_ref[k : k + 1, :] = c * (16.0 * LOG2E)
        table_ref[3 + k : 4 + k, :] = 4.0 * jnp.exp2(c * c * (-8.0 * LOG2E))
    if sliced:
        bricks = rank_ref.shape[1]
        place = lax.axis_index("depth")
        for view in range(2):
            for slot in range(bricks):
                row = TONES + bricks * view + slot
                table_ref[row : row + 1, :] = jnp.full((1, LANES), rank_ref[view, place ^ slot].astype(F32))
    copy.wait()
    samples = sums_ref.shape[0]
    half = samples // 2
    for first in (0, half):
        sums_ref[first : first + half, :] = sample_sums(rho_ref[first * rows : (first + half) * rows, :], half, rows)
    odd = lax.axis_index("light") % 2
    for out_ref, pieces in zip(out_refs, places, strict=True):
        row, width = 0, out_ref.shape[1]
        for even_first, odd_first, count, column in pieces:
            first = pl.multiple_of(even_first + odd * (odd_first - even_first), 8)
            out_ref[row : row + count, :] = sums_ref[pl.ds(first, count), column : column + width]
            row += count


def pair_kernel(hold_ref, given_ref, pair_ref):
    pair_ref[...] = hold_ref[...] + given_ref[...]


def upper_kernel(straight_ref, across_ref, same_ref, below_ref, send_ref):
    me = lax.axis_index("light")
    odd = me % 2 == 1
    below = jnp.where(me >= 2, straight_ref[...] + across_ref[...], 0.0)
    below_ref[...] = below
    send_ref[...] = below + jnp.where(odd, 0.0, same_ref[...])


def late_kernel(late_ref, add_ref):
    add_ref[...] = jnp.where(lax.axis_index("light") % 2 == 1, late_ref[...], 0.0)


def pre_kernel(
    samples, rows, width, rho_ref, light_ref, view_ref, table_ref,
    near_ref, far_ref, red_ref, green_ref, blue_ref, total_ref, above_ref,
):
    columns = rho_ref.shape[1]
    narrow = (rows, samples * rows)
    of_row = lax.broadcasted_iota(jnp.int32, narrow, 1) % rows == lax.broadcasted_iota(jnp.int32, narrow, 0)
    total_ref[...] = jnp.dot(of_row.astype(jnp.bfloat16), rho_ref[...], preferred_element_type=F32)
    block = 256
    square = (block, block)
    i = lax.broadcasted_iota(jnp.int32, square, 0)
    j = lax.broadcasted_iota(jnp.int32, square, 1)
    above = ((i // rows == j // rows) & (j < i)).astype(jnp.bfloat16)
    for start in range(0, samples * rows, block):
        above_ref[start : start + block, :] = jnp.dot(
            above, rho_ref[start : start + block, :], preferred_element_type=F32
        )

    shape = (rows, width)
    tone = [jnp.broadcast_to(jnp.concatenate([table_ref[k : k + 1, :]] * (width // LANES), 1), shape) for k in range(3)]
    for first in range(0, columns, width):
        at = pl.ds(first, width)
        light = jnp.broadcast_to(light_ref[:, at] * LOG2E, shape)
        r0, r1 = view_ref[0:1, at], view_ref[1:2, at]
        fade = [jnp.broadcast_to(c, shape) for c in (r0, r0 * r0 * 0.5, r0 * r0 * r0 * (1 / 6))]
        grow = [jnp.broadcast_to(c, shape) for c in (r1, r1 * r1 * 0.5, r1 * r1 * r1 * (1 / 6))]

        def pair(step, carry):
            clear, behind = carry
            two = rho_ref[pl.ds(pl.multiple_of(step * 2 * rows, 2 * rows), 2 * rows), at].astype(F32)
            for part in range(2):
                rho = two[part * rows : (part + 1) * rows]
                here = pl.ds(pl.multiple_of((step * 2 + part) * rows, rows), rows)
                tint = jnp.exp2(rho * rho * (-8.0 * LOG2E) - light * above_ref[here, at])
                w0 = clear * (rho * (fade[0] - rho * (fade[1] - rho * fade[2])))
                clear = clear - w0
                w1 = behind * (rho * (grow[0] + rho * (grow[1] + rho * grow[2])))
                behind = behind + w1
                near_ref[here, at] = w0 * tint
                far_ref[here, at] = w1 * tint
                for k, color_ref in enumerate((red_ref, green_ref, blue_ref)):
                    color_ref[here, at] = jnp.exp2(rho * tone[k])
            return clear, behind

        start = (jnp.ones(shape, F32), jnp.exp2(total_ref[:, at] * view_ref[1:2, at] * -LOG2E))
        lax.fori_loop(0, samples // 2, pair, start, unroll=True)


def straight_below(refs, below_ref):
    same, given = (ref[...] for ref in refs)
    me = lax.axis_index("light")
    below_ref[...] = jnp.where(me >= 2, same, 0.0) + jnp.where(me % 2 == 1, given, 0.0)


def first_below(refs, below_ref):
    mine, other, late = (ref[...] for ref in refs)
    few = mine.shape[0]
    odd = lax.axis_index("light") % 2 == 1
    below_ref[:few, :] = jnp.where(odd, other, mine)
    below_ref[few:, :] = jnp.where(odd, mine + late[-few:], other)


def crossed_below(refs, below_ref):
    cross, late = (ref[...] for ref in refs)
    below_ref[...] = jnp.where(lax.axis_index("light") >= 2, cross, 0.0) + late[: cross.shape[0]]


def whole_below(refs, below_ref):
    count, columns = refs[0].shape
    below_ref[:count, :] = refs[0][:, : columns // 2]
    below_ref[count:, :] = refs[0][:, columns // 2 :]


def post_kernel(
    rows, second, runs, sliced, assemble, light_ref, table_ref, near_ref, far_ref, red_ref, green_ref, blue_ref, rest_ref, *refs
):
    *refs, out_ref, lit_ref = refs
    assemble(refs, lit_ref)
    columns = near_ref.shape[1]
    place = lax.axis_index("depth") if sliced else 0
    chip, core = place // 2, place % 2
    odd = lax.axis_index("light") % 2
    width = 2 * LANES
    shape = (rows, width)
    scales = [jnp.broadcast_to(table_ref[3 + k : 4 + k, :], (rows, LANES)) for k in range(3)]
    for side, pieces in enumerate(runs):
        start = side * columns // 2
        light = light_ref[:, start : start + columns // 2] * -LOG2E
        for _, _, count, row in pieces:
            lit_ref[row : row + count, :] = jnp.exp2(lit_ref[row : row + count, :] * light)
    for block in range(columns // width):
        at = slice(block * width, (block + 1) * width)
        side, here_at = divmod(block * width, columns // 2)
        sums = [jnp.zeros(shape, F32)] * 6
        for even_first, odd_first, count, row in runs[side]:
            first = even_first + odd * (odd_first - even_first)
            for group in range(0, count, 8):
                lit = lit_ref[row + group : row + group + 8, here_at : here_at + width]
                for part in range(8):
                    here = pl.ds(pl.multiple_of((first + group + part) * rows, rows), rows)
                    shade = jnp.broadcast_to(lit[part : part + 1], shape)
                    weights = near_ref[here, at] * shade, far_ref[here, at] * shade
                    colors = [ref[here, at] for ref in (red_ref, green_ref, blue_ref)]
                    sums = [sums[3 * v + k] + weights[v] * colors[k] for v in range(2) for k in range(3)]
        slot = block ^ chip
        for tile in range(2):
            lanes = slice(tile * LANES, (tile + 1) * LANES)
            for n in range(6):
                value = sums[n][:, lanes] * scales[n % 3]
                if second:
                    value = value + rest_ref[tile ^ core, slot, n]
                out_ref[tile ^ core, slot, n] = value
            out_ref[tile ^ core, slot, 6] = rest_ref[tile ^ core, slot, 6] if second else rest_ref[:, at][:, lanes]


def post_tiles_kernel(
    rows, which, runs, assemble, light_ref, table_ref, near_ref, far_ref, red_ref, green_ref, blue_ref, rest_ref, *refs
):
    *refs, out_ref, lit_ref = refs
    assemble(refs, lit_ref)
    columns = near_ref.shape[1]
    place = lax.axis_index("depth")
    chip, core = place // 2, place % 2
    odd = lax.axis_index("light") % 2
    shape = (rows, LANES)
    scales = [jnp.broadcast_to(table_ref[3 + k : 4 + k, :], shape) for k in range(3)]
    blocks = columns // (2 * LANES)
    for side, pieces in enumerate(runs):
        start = side * columns // 2
        light = light_ref[:, start : start + columns // 2] * -LOG2E
        for _, _, count, row in pieces:
            lit_ref[row : row + count, :] = jnp.exp2(lit_ref[row : row + count, :] * light)
        tiles = range(side * blocks // 2, (side + 1) * blocks // 2)
        lanes = [pl.ds(pl.multiple_of((2 * tile + (which ^ core)) * LANES, LANES), LANES) for tile in tiles]
        near_lanes = [pl.ds(pl.multiple_of((2 * tile + (which ^ core)) * LANES - start, LANES), LANES) for tile in tiles]
        sums = [[jnp.zeros(shape, F32)] * 6 for _ in tiles]
        for even_first, odd_first, count, row in pieces:
            first = even_first + odd * (odd_first - even_first)
            for group in range(0, count, 8):
                lits = [lit_ref[row + group : row + group + 8, at] for at in near_lanes]
                for part in range(8):
                    here = pl.ds(pl.multiple_of((first + group + part) * rows, rows), rows)
                    for n, at in enumerate(lanes):
                        shade = jnp.broadcast_to(lits[n][part : part + 1], shape)
                        weights = near_ref[here, at] * shade, far_ref[here, at] * shade
                        colors = [ref[here, at] for ref in (red_ref, green_ref, blue_ref)]
                        sums[n] = [sums[n][3 * v + k] + weights[v] * colors[k] for v in range(2) for k in range(3)]
        for n, tile in enumerate(tiles):
            slot = tile ^ chip
            for channel in range(6):
                out_ref[slot, channel] = sums[n][channel] * scales[channel % 3] + rest_ref[which, slot, channel]
            out_ref[slot, 6] = rest_ref[which, slot, 6]


def call(kernel, outs, spaces, scratch, flops, moved, *args, limit=8):
    specs = {"v": pl.BlockSpec(memory_space=pltpu.VMEM), "s": pl.BlockSpec(memory_space=pltpu.SMEM), "a": pl.BlockSpec(memory_space=pl.ANY)}
    forced = {"V": pltpu.VMEM, "A": pltpu.HBM, "S": pltpu.SMEM}
    args = [pltpu.with_memory_space_constraint(a, forced[k]) if k in forced else a for a, k in zip(args, spaces, strict=True)]
    return pl.pallas_call(
        kernel,
        out_shape=tuple(pltpu.VMEM(o, t) for o, t in outs),
        in_specs=[specs[k.lower()] for k in spaces],
        out_specs=tuple([specs["v"]] * len(outs)),
        scratch_shapes=scratch,
        cost_estimate=pl.CostEstimate(flops=flops, bytes_accessed=moved, transcendentals=0),
        compiler_params=pltpu.CompilerParams(vmem_limit_bytes=limit << 20),
    )(*args)


def composite_kernel(bricks, got_ref, rate_ref, rank_ref, out_ref, order_ref):
    shape = out_ref.shape[2:]
    for view in range(2):
        def place(d, carry, view=view):
            order_ref[view, rank_ref[view, d]] = d
            return carry

        lax.fori_loop(0, bricks, place, 0, unroll=bricks <= 8)
        rate = jnp.broadcast_to(rate_ref[view : view + 1, :], shape)

        def nearer(p, carry, view=view, rate=rate):
            front, red, green, blue = carry
            d = order_ref[view, p]
            seen = jnp.exp2(front * rate * -LOG2E)
            red = red + got_ref[d, 3 * view] * seen
            green = green + got_ref[d, 3 * view + 1] * seen
            blue = blue + got_ref[d, 3 * view + 2] * seen
            return front + got_ref[d, 6], red, green, blue

        zero = jnp.zeros(shape, F32)
        depth, *colors = lax.fori_loop(0, bricks, nearer, (zero,) * 4, unroll=bricks <= 8)
        for k in range(3):
            out_ref[view, k] = colors[k]
        out_ref[view, 3] = opacity(depth * rate)


def composite(got, rate, rank):
    bricks, _, rows, columns = got.shape
    vmem, smem = pl.BlockSpec(memory_space=pltpu.VMEM), pl.BlockSpec(memory_space=pltpu.SMEM)
    return pl.pallas_call(
        functools.partial(composite_kernel, bricks),
        out_shape=jax.ShapeDtypeStruct((2, 4, rows, columns), F32),
        in_specs=[vmem, vmem, smem],
        out_specs=vmem,
        scratch_shapes=[pltpu.SMEM((2, bricks), jnp.int32)],
        compiler_params=pltpu.CompilerParams(vmem_limit_bytes=8 << 20),
    )(pltpu.with_memory_space_constraint(got, pltpu.VMEM), rate, rank)


def opacity(depth):
    small = jnp.full(depth.shape, 1.0, F32)
    for n in range(8, 1, -1):
        small = 1.0 - depth * (1.0 / n) * small
    return jnp.where(depth < 0.35, depth * small, 1.0 - jnp.exp2(depth * -LOG2E))


def slots_kernel(order, table_ref, rate_ref, own_ref, sibling_ref, *refs):
    *chip_refs, out_ref = refs
    shape = out_ref.shape[2:]
    chips = dict(zip(order, chip_refs, strict=True))
    blocks = [own_ref.at[0], sibling_ref.at[0]] + [chips[chip].at[t] for chip in sorted(order) for t in range(2)]
    depths = [block[6] for block in blocks]
    for view in range(2):
        rate = jnp.broadcast_to(rate_ref[view : view + 1, :], shape)
        first = TONES + len(blocks) * view
        ranks = [jnp.broadcast_to(table_ref[first + slot : first + slot + 1, :], shape) for slot in range(len(blocks))]
        colors = [jnp.zeros(shape, F32)] * 3
        for i, block in enumerate(blocks):
            front = jnp.zeros(shape, F32)
            for j, depth in enumerate(depths):
                if j != i:
                    front = front + jnp.where(ranks[j] < ranks[i], depth, 0.0)
            seen = jnp.exp2(front * rate * -LOG2E)
            colors = [colors[k] + block[3 * view + k] * seen for k in range(3)]
        for k in range(3):
            out_ref[view, k] = colors[k]
        out_ref[view, 3] = opacity(sum(depths) * rate)


def composite_slots(table, rate, own, sibling, order, chips):
    blocks = [own, sibling, *chips]
    _, rows, columns = own.shape[1:]
    (image,) = call(
        functools.partial(slots_kernel, order), [((2, 4, rows, columns), F32)], "VV" + "V" * len(blocks), [], 1 << 10, 1 << 10,
        table, rate, *blocks,
    )
    return image


def swap(x, stride, n):
    return lax.ppermute(x, "light", [(i, i ^ stride) for i in range(n)])


def lower(x, stride, n):
    if stride == n:
        return jnp.zeros_like(x)
    odd = (lax.axis_index("light") // stride) % 2 == 1
    if 2 * stride == n:
        return jnp.where(odd, swap(x, stride, n), 0.0)
    half = x.shape[0] // 2
    first, last = x[:half], x[half:]
    keep, sibling = jnp.where(odd, last, first), swap(jnp.where(odd, first, last), stride, n)
    below = lower(keep + sibling, 2 * stride, n)
    other = swap(below + jnp.where(odd, 0.0, keep), stride, n)
    mine = below + jnp.where(odd, sibling, 0.0)
    return jnp.where(odd, jnp.concatenate([other, mine]), jnp.concatenate([mine, other]))


def lower_of_four(give, hold, same, cross, late):
    given = swap(give, 1, 4)
    straight, across = swap(same, 2, 4), swap(cross, 3, 4)
    columns = same.shape[1]
    late = swap(late, 1, 4)
    (pair,) = call(pair_kernel, [(hold.shape, F32)], "VV", [], 1 << 10, 1 << 10, hold, given)
    from_same, from_cross = swap(pair, 2, 4), swap(pair, 3, 4)
    mine, send = call(upper_kernel, [(same.shape, F32)] * 2, "VVV", [], 1 << 31, 1 << 10, straight, across, same)
    (late,) = call(late_kernel, [(late.shape, F32)], "V", [], 1 << 10, 1 << 10, late)
    other = swap(send, 1, 4)
    return (from_same, given), (mine, other, late), (from_cross, late)


def shards(depth_n, light_n, density, light_rate, view_rate, centers, rank):
    samples, rows, columns = density.shape
    rho = density.reshape(samples * rows, columns)
    light = light_rate.reshape(1, -1)
    whole = (samples * rows, columns)
    sizes = [(samples // 8 * (side + 1), samples // 8 * (3 - side), columns // 2 * side) for side in range(2)]
    give = [(2 * few + many, 2 * few, many, at) for few, many, at in sizes]
    hold = [(2 * few, 2 * few + many, many, at) for few, many, at in sizes]
    same = [(0, few, few, at) for few, many, at in sizes]
    cross = [(few, 0, few, at) for few, many, at in sizes]
    places, width = [give, hold, same, cross, hold + cross], columns // 2
    if light_n != 4:
        places, width = [[(0, 0, samples, 0)]], columns
    own = columns // depth_n
    sliced = own == LANES and depth_n <= 8 and depth_n & (depth_n - 1) == 0
    table = (TONES + 2 * depth_n if sliced else TONES, LANES)
    *sums, table, rho = call(
        functools.partial(sums_kernel, rows, places, sliced),
        [((sum(piece[2] for piece in pieces), width), F32) for pieces in places] + [(table, F32), (whole, jnp.bfloat16)], "AAA",
        [pltpu.VMEM((samples, columns), F32), pltpu.SMEM(rank.shape, jnp.int32), pltpu.SMEM(centers.shape, F32), pltpu.SemaphoreType.DMA((3,))],
        1 << 20, 1 << 20, rho, rank, centers,
    )
    if light_n == 4:
        pieces = lower_of_four(*sums)
        assemble = straight_below, first_below, crossed_below
    else:
        below = lower(sums[0], 1, light_n)
        pieces = [below[: samples // 2]], [below[samples // 2 :]]
        assemble = whole_below, whole_below
    near, far, red, green, blue, total = call(
        functools.partial(pre_kernel, samples, rows, 256), [(whole, F32)] * 5 + [((rows, columns), F32)], "VVVV",
        [pltpu.VMEM(whole, F32)], 1 << 20, 12 << 20, rho, light, view_rate, table,
    )
    place = lax.axis_index("depth")
    rate = lax.dynamic_slice_in_dim(view_rate, place * own, own, axis=1)
    packed = total
    runs = [[], []], [[], []], [[], []]
    first, last = sum(few for few, _, _ in sizes), sum(many for _, many, _ in sizes)
    row, much = 0, 0
    for side, (few, many, _) in enumerate(sizes):
        runs[0][side].append((2 * few, 2 * few + many, many, much))
        runs[1][side] += [(0, 0, few, row), (few, few, few, first + row)]
        runs[2][side].append((2 * few + many, 2 * few, many, much))
        row, much = row + few, much + many
    rows_of = last, 2 * first, last
    if light_n != 4:
        half = samples // 2
        runs = [[[(start, start, half, half * side)] for side in range(2)] for start in (0, half)]
        rows_of = samples, samples
    def post(kernel, second, out, packed):
        return call(
            kernel, [(out, F32)], "V" * (8 + len(pieces[second])), [pltpu.VMEM((rows_of[second], columns // 2), F32)],
            1 << 10, 1 << 10, light, table, near, far, red, green, blue, packed, *pieces[second],
        )[0]

    packs = columns // (2 * LANES), 7, rows, LANES
    whole_runs = len(runs) - 1 if sliced else len(runs)
    for second in range(whole_runs):
        kernel = functools.partial(post_kernel, rows, second > 0, runs[second], sliced, assemble[second])
        packed = post(kernel, second, (2, *packs), packed)
    if sliced:
        def send_to(x, stride):
            return lax.ppermute(x, "depth", [(i, i ^ stride) for i in range(depth_n)])

        theirs, mine = (
            post(functools.partial(post_tiles_kernel, rows, which, runs[-1], assemble[-1]), len(runs) - 1, packs, packed)
            for which in (1, 0)
        )
        got = send_to(theirs, 1)
        order = sorted(range(1, depth_n // 2), key=lambda chip: (chip % 2, chip))
        sent = {chip: send_to(jnp.stack([mine[chip], got[chip]]), 2 * chip) for chip in order}
        return composite_slots(table, rate, mine, got, order, [sent[chip] for chip in order])
    parts = packed.transpose(1, 0, 2, 3, 4).reshape(columns // LANES, 7, rows, LANES)
    if own % LANES == 0:
        parts = parts.reshape(depth_n, own // LANES, 7, rows, LANES).transpose(0, 2, 3, 1, 4)
    else:
        parts = parts.reshape(columns // LANES, 7, rows, LANES // own, own).transpose(0, 3, 1, 2, 4)
    got = lax.all_to_all(parts.reshape(depth_n, 7, rows, own), "depth", split_axis=0, concat_axis=0, tiled=True)
    return composite(got, rate, rank)


def solution(mesh):
    return jax.shard_map(
        functools.partial(shards, mesh.shape["depth"], mesh.shape["light"]),
        mesh=mesh,
        in_specs=(P("depth", "light", None), P(), P(), P(), P()),
        out_specs=P(None, None, "light", "depth"),
        check_vma=False,
    )
```

```python
import functools
import math

import jax
import jax.numpy as jnp
from jax import lax
from jax.experimental import pallas as pl
from jax.experimental.pallas import tpu as pltpu
from jax.sharding import PartitionSpec as P

F32 = jnp.float32
LOG2E = math.log2(math.e)
LANES = 128
TONES = 8


def sample_sums(rho, samples, rows):
    wide = (samples, samples * rows)
    target = lax.broadcasted_iota(jnp.int32, wide, 0)
    source = lax.broadcasted_iota(jnp.int32, wide, 1)
    return jnp.dot((source // rows == target).astype(jnp.bfloat16), rho, preferred_element_type=F32)


def sums_kernel(rows, places, sliced, rho_hbm, rank_hbm, center_hbm, *refs):
    *out_refs, table_ref, rho_ref, sums_ref, rank_ref, center_ref, sems = refs
    copy = pltpu.make_async_copy(rho_hbm, rho_ref, sems.at[0])
    small = pltpu.make_async_copy(rank_hbm, rank_ref, sems.at[1]), pltpu.make_async_copy(center_hbm, center_ref, sems.at[2])
    copy.start()
    for part in small:
        part.start()
    for part in small:
        part.wait()
    for k in range(3):
        c = jnp.full((1, LANES), center_ref[k], F32)
        table_ref[k : k + 1, :] = c * (16.0 * LOG2E)
        table_ref[3 + k : 4 + k, :] = 4.0 * jnp.exp2(c * c * (-8.0 * LOG2E))
    if sliced:
        bricks = rank_ref.shape[1]
        place = lax.axis_index("depth")
        for view in range(2):
            for slot in range(bricks):
                row = TONES + bricks * view + slot
                table_ref[row : row + 1, :] = jnp.full((1, LANES), rank_ref[view, place ^ slot].astype(F32))
    copy.wait()
    samples = sums_ref.shape[0]
    half = samples // 2
    for first in (0, half):
        sums_ref[first : first + half, :] = sample_sums(rho_ref[first * rows : (first + half) * rows, :], half, rows)
    odd = lax.axis_index("light") % 2
    for out_ref, pieces in zip(out_refs, places, strict=True):
        row, width = 0, out_ref.shape[1]
        for even_first, odd_first, count, column in pieces:
            first = pl.multiple_of(even_first + odd * (odd_first - even_first), 8)
            out_ref[row : row + count, :] = sums_ref[pl.ds(first, count), column : column + width]
            row += count


def pair_kernel(hold_ref, given_ref, pair_ref):
    pair_ref[...] = hold_ref[...] + given_ref[...]


def upper_kernel(straight_ref, across_ref, same_ref, below_ref, send_ref):
    me = lax.axis_index("light")
    odd = me % 2 == 1
    below = jnp.where(me >= 2, straight_ref[...] + across_ref[...], 0.0)
    below_ref[...] = below
    send_ref[...] = below + jnp.where(odd, 0.0, same_ref[...])


def late_kernel(late_ref, add_ref):
    add_ref[...] = jnp.where(lax.axis_index("light") % 2 == 1, late_ref[...], 0.0)


def pre_kernel(
    samples, rows, width, rho_ref, light_ref, view_ref, table_ref,
    near_ref, far_ref, red_ref, green_ref, blue_ref, total_ref,
):
    columns = rho_ref.shape[1]
    narrow = (rows, samples * rows)
    of_row = lax.broadcasted_iota(jnp.int32, narrow, 1) % rows == lax.broadcasted_iota(jnp.int32, narrow, 0)
    of_row = of_row.astype(jnp.bfloat16)
    block = 256
    square = (block, block)
    i = lax.broadcasted_iota(jnp.int32, square, 0)
    j = lax.broadcasted_iota(jnp.int32, square, 1)
    above = ((i // rows == j // rows) & (j < i)).astype(jnp.bfloat16)

    shape = (rows, width)
    tone = [jnp.broadcast_to(jnp.concatenate([table_ref[k : k + 1, :]] * (width // LANES), 1), shape) for k in range(3)]
    for first in range(0, columns, width):
        at = pl.ds(first, width)
        total_ref[:, at] = jnp.dot(of_row, rho_ref[:, at], preferred_element_type=F32)
        inner = [
            jnp.dot(above, rho_ref[start : start + block, at], preferred_element_type=F32)
            for start in range(0, samples * rows, block)
        ]
        light = jnp.broadcast_to(light_ref[:, at] * LOG2E, shape)
        r0, r1 = view_ref[0:1, at], view_ref[1:2, at]
        fade = [jnp.broadcast_to(c, shape) for c in (r0, r0 * r0 * 0.5, r0 * r0 * r0 * (1 / 6))]
        grow = [jnp.broadcast_to(c, shape) for c in (r1, r1 * r1 * 0.5, r1 * r1 * r1 * (1 / 6))]

        clear = jnp.ones(shape, F32)
        behind = jnp.exp2(total_ref[:, at] * view_ref[1:2, at] * -LOG2E)
        for start in range(0, samples * rows, 2 * rows):
            two = rho_ref[start : start + 2 * rows, at].astype(F32)
            for part in range(2):
                rho = two[part * rows : (part + 1) * rows]
                first_row = start + part * rows
                here = slice(first_row, first_row + rows)
                shade = inner[first_row // block][first_row % block : first_row % block + rows]
                tint = jnp.exp2(rho * rho * (-8.0 * LOG2E) - light * shade)
                w0 = clear * (rho * (fade[0] - rho * (fade[1] - rho * fade[2])))
                clear = clear - w0
                w1 = behind * (rho * (grow[0] + rho * (grow[1] + rho * grow[2])))
                behind = behind + w1
                near_ref[here, at] = w0 * tint
                far_ref[here, at] = w1 * tint
                for k, color_ref in enumerate((red_ref, green_ref, blue_ref)):
                    color_ref[here, at] = jnp.exp2(rho * tone[k])


def straight_below(refs, below_ref):
    same, given = (ref[...] for ref in refs)
    me = lax.axis_index("light")
    below_ref[...] = jnp.where(me >= 2, same, 0.0) + jnp.where(me % 2 == 1, given, 0.0)


def first_below(refs, below_ref):
    mine, other, late = (ref[...] for ref in refs)
    few = mine.shape[0]
    odd = lax.axis_index("light") % 2 == 1
    below_ref[:few, :] = jnp.where(odd, other, mine)
    below_ref[few:, :] = jnp.where(odd, mine + late[-few:], other)


def crossed_below(refs, below_ref):
    cross, late = (ref[...] for ref in refs)
    below_ref[...] = jnp.where(lax.axis_index("light") >= 2, cross, 0.0) + late[: cross.shape[0]]


def whole_below(refs, below_ref):
    count, columns = refs[0].shape
    below_ref[:count, :] = refs[0][:, : columns // 2]
    below_ref[count:, :] = refs[0][:, columns // 2 :]


def post_kernel(
    rows, second, runs, sliced, assemble, light_ref, table_ref, near_ref, far_ref, red_ref, green_ref, blue_ref, rest_ref, *refs
):
    *refs, out_ref, lit_ref = refs
    assemble(refs, lit_ref)
    columns = near_ref.shape[1]
    place = lax.axis_index("depth") if sliced else 0
    chip, core = place // 2, place % 2
    odd = lax.axis_index("light") % 2
    width = 2 * LANES
    shape = (rows, width)
    scales = [jnp.broadcast_to(table_ref[3 + k : 4 + k, :], (rows, LANES)) for k in range(3)]
    for side, pieces in enumerate(runs):
        start = side * columns // 2
        light = light_ref[:, start : start + columns // 2] * -LOG2E
        for _, _, count, row in pieces:
            lit_ref[row : row + count, :] = jnp.exp2(lit_ref[row : row + count, :] * light)
    for block in range(columns // width):
        at = slice(block * width, (block + 1) * width)
        side, here_at = divmod(block * width, columns // 2)
        sums = [jnp.zeros(shape, F32)] * 6
        for even_first, odd_first, count, row in runs[side]:
            first = even_first + odd * (odd_first - even_first)
            for group in range(0, count, 8):
                lit = lit_ref[row + group : row + group + 8, here_at : here_at + width]
                for part in range(8):
                    here = pl.ds(pl.multiple_of((first + group + part) * rows, rows), rows)
                    shade = jnp.broadcast_to(lit[part : part + 1], shape)
                    weights = near_ref[here, at] * shade, far_ref[here, at] * shade
                    colors = [ref[here, at] for ref in (red_ref, green_ref, blue_ref)]
                    sums = [sums[3 * v + k] + weights[v] * colors[k] for v in range(2) for k in range(3)]
        slot = block ^ chip
        for tile in range(2):
            lanes = slice(tile * LANES, (tile + 1) * LANES)
            for n in range(6):
                value = sums[n][:, lanes] * scales[n % 3]
                if second:
                    value = value + rest_ref[tile ^ core, slot, n]
                out_ref[tile ^ core, slot, n] = value
            out_ref[tile ^ core, slot, 6] = rest_ref[tile ^ core, slot, 6] if second else rest_ref[:, at][:, lanes]


def post_tiles_kernel(
    rows, which, runs, assemble, light_ref, table_ref, near_ref, far_ref, red_ref, green_ref, blue_ref, rest_ref, *refs
):
    *refs, out_ref, lit_ref = refs
    assemble(refs, lit_ref)
    columns = near_ref.shape[1]
    place = lax.axis_index("depth")
    chip, core = place // 2, place % 2
    odd = lax.axis_index("light") % 2
    shape = (rows, LANES)
    scales = [jnp.broadcast_to(table_ref[3 + k : 4 + k, :], shape) for k in range(3)]
    blocks = columns // (2 * LANES)
    for side, pieces in enumerate(runs):
        start = side * columns // 2
        light = light_ref[:, start : start + columns // 2] * -LOG2E
        for _, _, count, row in pieces:
            lit_ref[row : row + count, :] = jnp.exp2(lit_ref[row : row + count, :] * light)
        tiles = range(side * blocks // 2, (side + 1) * blocks // 2)
        lanes = [pl.ds(pl.multiple_of((2 * tile + (which ^ core)) * LANES, LANES), LANES) for tile in tiles]
        near_lanes = [pl.ds(pl.multiple_of((2 * tile + (which ^ core)) * LANES - start, LANES), LANES) for tile in tiles]
        sums = [[jnp.zeros(shape, F32)] * 6 for _ in tiles]
        for even_first, odd_first, count, row in pieces:
            first = even_first + odd * (odd_first - even_first)
            for group in range(0, count, 8):
                lits = [lit_ref[row + group : row + group + 8, at] for at in near_lanes]
                for part in range(8):
                    here = pl.ds(pl.multiple_of((first + group + part) * rows, rows), rows)
                    for n, at in enumerate(lanes):
                        shade = jnp.broadcast_to(lits[n][part : part + 1], shape)
                        weights = near_ref[here, at] * shade, far_ref[here, at] * shade
                        colors = [ref[here, at] for ref in (red_ref, green_ref, blue_ref)]
                        sums[n] = [sums[n][3 * v + k] + weights[v] * colors[k] for v in range(2) for k in range(3)]
        for n, tile in enumerate(tiles):
            slot = tile ^ chip
            for channel in range(6):
                out_ref[slot, channel] = sums[n][channel] * scales[channel % 3] + rest_ref[which, slot, channel]
            out_ref[slot, 6] = rest_ref[which, slot, 6]


def call(kernel, outs, spaces, scratch, flops, moved, *args, limit=8):
    specs = {"v": pl.BlockSpec(memory_space=pltpu.VMEM), "s": pl.BlockSpec(memory_space=pltpu.SMEM), "a": pl.BlockSpec(memory_space=pl.ANY)}
    forced = {"V": pltpu.VMEM, "A": pltpu.HBM, "S": pltpu.SMEM}
    args = [pltpu.with_memory_space_constraint(a, forced[k]) if k in forced else a for a, k in zip(args, spaces, strict=True)]
    return pl.pallas_call(
        kernel,
        out_shape=tuple(pltpu.VMEM(o, t) for o, t in outs),
        in_specs=[specs[k.lower()] for k in spaces],
        out_specs=tuple([specs["v"]] * len(outs)),
        scratch_shapes=scratch,
        cost_estimate=pl.CostEstimate(flops=flops, bytes_accessed=moved, transcendentals=0),
        compiler_params=pltpu.CompilerParams(vmem_limit_bytes=limit << 20),
    )(*args)


def composite_kernel(bricks, got_ref, rate_ref, rank_ref, out_ref, order_ref):
    shape = out_ref.shape[2:]
    for view in range(2):
        def place(d, carry, view=view):
            order_ref[view, rank_ref[view, d]] = d
            return carry

        lax.fori_loop(0, bricks, place, 0, unroll=bricks <= 8)
        rate = jnp.broadcast_to(rate_ref[view : view + 1, :], shape)

        def nearer(p, carry, view=view, rate=rate):
            front, red, green, blue = carry
            d = order_ref[view, p]
            seen = jnp.exp2(front * rate * -LOG2E)
            red = red + got_ref[d, 3 * view] * seen
            green = green + got_ref[d, 3 * view + 1] * seen
            blue = blue + got_ref[d, 3 * view + 2] * seen
            return front + got_ref[d, 6], red, green, blue

        zero = jnp.zeros(shape, F32)
        depth, *colors = lax.fori_loop(0, bricks, nearer, (zero,) * 4, unroll=bricks <= 8)
        for k in range(3):
            out_ref[view, k] = colors[k]
        out_ref[view, 3] = opacity(depth * rate)


def composite(got, rate, rank):
    bricks, _, rows, columns = got.shape
    vmem, smem = pl.BlockSpec(memory_space=pltpu.VMEM), pl.BlockSpec(memory_space=pltpu.SMEM)
    return pl.pallas_call(
        functools.partial(composite_kernel, bricks),
        out_shape=jax.ShapeDtypeStruct((2, 4, rows, columns), F32),
        in_specs=[vmem, vmem, smem],
        out_specs=vmem,
        scratch_shapes=[pltpu.SMEM((2, bricks), jnp.int32)],
        compiler_params=pltpu.CompilerParams(vmem_limit_bytes=8 << 20),
    )(pltpu.with_memory_space_constraint(got, pltpu.VMEM), rate, rank)


def opacity(depth):
    small = jnp.full(depth.shape, 1.0, F32)
    for n in range(8, 1, -1):
        small = 1.0 - depth * (1.0 / n) * small
    return jnp.where(depth < 0.35, depth * small, 1.0 - jnp.exp2(depth * -LOG2E))


def slots_kernel(order, table_ref, rate_ref, own_ref, sibling_ref, *refs):
    *chip_refs, out_ref = refs
    shape = out_ref.shape[2:]
    chips = dict(zip(order, chip_refs, strict=True))
    blocks = [own_ref.at[0], sibling_ref.at[0]] + [chips[chip].at[t] for chip in sorted(order) for t in range(2)]
    depths = [block[6] for block in blocks]
    for view in range(2):
        rate = jnp.broadcast_to(rate_ref[view : view + 1, :], shape)
        first = TONES + len(blocks) * view
        ranks = [jnp.broadcast_to(table_ref[first + slot : first + slot + 1, :], shape) for slot in range(len(blocks))]
        colors = [jnp.zeros(shape, F32)] * 3
        for i, block in enumerate(blocks):
            front = jnp.zeros(shape, F32)
            for j, depth in enumerate(depths):
                if j != i:
                    front = front + jnp.where(ranks[j] < ranks[i], depth, 0.0)
            seen = jnp.exp2(front * rate * -LOG2E)
            colors = [colors[k] + block[3 * view + k] * seen for k in range(3)]
        for k in range(3):
            out_ref[view, k] = colors[k]
        out_ref[view, 3] = opacity(sum(depths) * rate)


def composite_slots(table, rate, own, sibling, order, chips):
    blocks = [own, sibling, *chips]
    _, rows, columns = own.shape[1:]
    (image,) = call(
        functools.partial(slots_kernel, order), [((2, 4, rows, columns), F32)], "VV" + "V" * len(blocks), [], 1 << 10, 1 << 10,
        table, rate, *blocks,
    )
    return image


def swap(x, stride, n):
    return lax.ppermute(x, "light", [(i, i ^ stride) for i in range(n)])


def lower(x, stride, n):
    if stride == n:
        return jnp.zeros_like(x)
    odd = (lax.axis_index("light") // stride) % 2 == 1
    if 2 * stride == n:
        return jnp.where(odd, swap(x, stride, n), 0.0)
    half = x.shape[0] // 2
    first, last = x[:half], x[half:]
    keep, sibling = jnp.where(odd, last, first), swap(jnp.where(odd, first, last), stride, n)
    below = lower(keep + sibling, 2 * stride, n)
    other = swap(below + jnp.where(odd, 0.0, keep), stride, n)
    mine = below + jnp.where(odd, sibling, 0.0)
    return jnp.where(odd, jnp.concatenate([other, mine]), jnp.concatenate([mine, other]))


def lower_of_four(give, hold, same, cross, late):
    given = swap(give, 1, 4)
    straight, across = swap(same, 2, 4), swap(cross, 3, 4)
    columns = same.shape[1]
    late = swap(late, 1, 4)
    (pair,) = call(pair_kernel, [(hold.shape, F32)], "VV", [], 1 << 10, 1 << 10, hold, given)
    from_same, from_cross = swap(pair, 2, 4), swap(pair, 3, 4)
    mine, send = call(upper_kernel, [(same.shape, F32)] * 2, "VVV", [], 1 << 31, 1 << 10, straight, across, same)
    (late,) = call(late_kernel, [(late.shape, F32)], "V", [], 1 << 10, 1 << 10, late)
    other = swap(send, 1, 4)
    return (from_same, given), (mine, other, late), (from_cross, late)


def shards(depth_n, light_n, density, light_rate, view_rate, centers, rank):
    samples, rows, columns = density.shape
    rho = density.reshape(samples * rows, columns)
    light = light_rate.reshape(1, -1)
    whole = (samples * rows, columns)
    sizes = [(samples // 8 * (side + 1), samples // 8 * (3 - side), columns // 2 * side) for side in range(2)]
    give = [(2 * few + many, 2 * few, many, at) for few, many, at in sizes]
    hold = [(2 * few, 2 * few + many, many, at) for few, many, at in sizes]
    same = [(0, few, few, at) for few, many, at in sizes]
    cross = [(few, 0, few, at) for few, many, at in sizes]
    places, width = [give, hold, same, cross, hold + cross], columns // 2
    if light_n != 4:
        places, width = [[(0, 0, samples, 0)]], columns
    own = columns // depth_n
    sliced = own == LANES and depth_n <= 8 and depth_n & (depth_n - 1) == 0
    table = (TONES + 2 * depth_n if sliced else TONES, LANES)
    *sums, table, rho = call(
        functools.partial(sums_kernel, rows, places, sliced),
        [((sum(piece[2] for piece in pieces), width), F32) for pieces in places] + [(table, F32), (whole, jnp.bfloat16)], "AAA",
        [pltpu.VMEM((samples, columns), F32), pltpu.SMEM(rank.shape, jnp.int32), pltpu.SMEM(centers.shape, F32), pltpu.SemaphoreType.DMA((3,))],
        1 << 20, 1 << 20, rho, rank, centers,
    )
    if light_n == 4:
        pieces = lower_of_four(*sums)
        assemble = straight_below, first_below, crossed_below
    else:
        below = lower(sums[0], 1, light_n)
        pieces = [below[: samples // 2]], [below[samples // 2 :]]
        assemble = whole_below, whole_below
    near, far, red, green, blue, total = call(
        functools.partial(pre_kernel, samples, rows, 256), [(whole, F32)] * 5 + [((rows, columns), F32)], "VVVV",
        [], 1 << 20, 12 << 20, rho, light, view_rate, table,
    )
    place = lax.axis_index("depth")
    rate = lax.dynamic_slice_in_dim(view_rate, place * own, own, axis=1)
    packed = total
    runs = [[], []], [[], []], [[], []]
    first, last = sum(few for few, _, _ in sizes), sum(many for _, many, _ in sizes)
    row, much = 0, 0
    for side, (few, many, _) in enumerate(sizes):
        runs[0][side].append((2 * few, 2 * few + many, many, much))
        runs[1][side] += [(0, 0, few, row), (few, few, few, first + row)]
        runs[2][side].append((2 * few + many, 2 * few, many, much))
        row, much = row + few, much + many
    rows_of = last, 2 * first, last
    if light_n != 4:
        half = samples // 2
        runs = [[[(start, start, half, half * side)] for side in range(2)] for start in (0, half)]
        rows_of = samples, samples
    def post(kernel, second, out, packed):
        return call(
            kernel, [(out, F32)], "V" * (8 + len(pieces[second])), [pltpu.VMEM((rows_of[second], columns // 2), F32)],
            1 << 10, 1 << 10, light, table, near, far, red, green, blue, packed, *pieces[second],
        )[0]

    packs = columns // (2 * LANES), 7, rows, LANES
    whole_runs = len(runs) - 1 if sliced else len(runs)
    for second in range(whole_runs):
        kernel = functools.partial(post_kernel, rows, second > 0, runs[second], sliced, assemble[second])
        packed = post(kernel, second, (2, *packs), packed)
    if sliced:
        def send_to(x, stride):
            return lax.ppermute(x, "depth", [(i, i ^ stride) for i in range(depth_n)])

        theirs, mine = (
            post(functools.partial(post_tiles_kernel, rows, which, runs[-1], assemble[-1]), len(runs) - 1, packs, packed)
            for which in (1, 0)
        )
        got = send_to(theirs, 1)
        order = sorted(range(1, depth_n // 2), key=lambda chip: (chip % 2, chip))
        sent = {chip: send_to(jnp.stack([mine[chip], got[chip]]), 2 * chip) for chip in order}
        return composite_slots(table, rate, mine, got, order, [sent[chip] for chip in order])
    parts = packed.transpose(1, 0, 2, 3, 4).reshape(columns // LANES, 7, rows, LANES)
    if own % LANES == 0:
        parts = parts.reshape(depth_n, own // LANES, 7, rows, LANES).transpose(0, 2, 3, 1, 4)
    else:
        parts = parts.reshape(columns // LANES, 7, rows, LANES // own, own).transpose(0, 3, 1, 2, 4)
    got = lax.all_to_all(parts.reshape(depth_n, 7, rows, own), "depth", split_axis=0, concat_axis=0, tiled=True)
    return composite(got, rate, rank)


def solution(mesh):
    return jax.shard_map(
        functools.partial(shards, mesh.shape["depth"], mesh.shape["light"]),
        mesh=mesh,
        in_specs=(P("depth", "light", None), P(), P(), P(), P()),
        out_specs=P(None, None, "light", "depth"),
        check_vma=False,
    )
```

```python
import functools
import math

import jax
import jax.numpy as jnp
from jax import lax
from jax.experimental import pallas as pl
from jax.experimental.pallas import tpu as pltpu
from jax.sharding import PartitionSpec as P

F32 = jnp.float32
LOG2E = math.log2(math.e)
LANES = 128
TONES = 8


def sample_sums(rho, samples, rows):
    wide = (samples, samples * rows)
    target = lax.broadcasted_iota(jnp.int32, wide, 0)
    source = lax.broadcasted_iota(jnp.int32, wide, 1)
    return jnp.dot((source // rows == target).astype(jnp.bfloat16), rho, preferred_element_type=F32)


def sums_kernel(rows, places, sliced, rho_hbm, rank_hbm, center_hbm, *refs):
    *out_refs, table_ref, rho_ref, sums_ref, rank_ref, center_ref, sems = refs
    copy = pltpu.make_async_copy(rho_hbm, rho_ref, sems.at[0])
    small = pltpu.make_async_copy(rank_hbm, rank_ref, sems.at[1]), pltpu.make_async_copy(center_hbm, center_ref, sems.at[2])
    copy.start()
    for part in small:
        part.start()
    for part in small:
        part.wait()
    for k in range(3):
        c = jnp.full((1, LANES), center_ref[k], F32)
        table_ref[k : k + 1, :] = c * (16.0 * LOG2E)
        table_ref[3 + k : 4 + k, :] = 4.0 * jnp.exp2(c * c * (-8.0 * LOG2E))
    if sliced:
        bricks = rank_ref.shape[1]
        place = lax.axis_index("depth")
        for view in range(2):
            for slot in range(bricks):
                row = TONES + bricks * view + slot
                table_ref[row : row + 1, :] = jnp.full((1, LANES), rank_ref[view, place ^ slot].astype(F32))
    copy.wait()
    samples = sums_ref.shape[0]
    sums_ref[...] = sample_sums(rho_ref[...], samples, rows)
    odd = lax.axis_index("light") % 2
    for out_ref, pieces in zip(out_refs, places, strict=True):
        row, width = 0, out_ref.shape[1]
        for even_first, odd_first, count, column in pieces:
            first = pl.multiple_of(even_first + odd * (odd_first - even_first), 8)
            out_ref[row : row + count, :] = sums_ref[pl.ds(first, count), column : column + width]
            row += count


def pair_kernel(hold_ref, given_ref, pair_ref):
    pair_ref[...] = hold_ref[...] + given_ref[...]


def upper_kernel(straight_ref, across_ref, same_ref, below_ref, send_ref):
    me = lax.axis_index("light")
    odd = me % 2 == 1
    below = jnp.where(me >= 2, straight_ref[...] + across_ref[...], 0.0)
    below_ref[...] = below
    send_ref[...] = below + jnp.where(odd, 0.0, same_ref[...])


def late_kernel(late_ref, add_ref):
    add_ref[...] = jnp.where(lax.axis_index("light") % 2 == 1, late_ref[...], 0.0)


def pre_kernel(
    samples, rows, width, rho_ref, light_ref, view_ref, table_ref,
    near_ref, far_ref, red_ref, green_ref, blue_ref, total_ref,
):
    columns = rho_ref.shape[1]
    narrow = (rows, samples * rows)
    of_row = lax.broadcasted_iota(jnp.int32, narrow, 1) % rows == lax.broadcasted_iota(jnp.int32, narrow, 0)
    of_row = of_row.astype(jnp.bfloat16)
    block = 256
    square = (block, block)
    i = lax.broadcasted_iota(jnp.int32, square, 0)
    j = lax.broadcasted_iota(jnp.int32, square, 1)
    above = ((i // rows == j // rows) & (j < i)).astype(jnp.bfloat16)

    shape = (rows, width)
    tone = [jnp.broadcast_to(jnp.concatenate([table_ref[k : k + 1, :]] * (width // LANES), 1), shape) for k in range(3)]
    for first in range(0, columns, width):
        at = pl.ds(first, width)
        total_ref[:, at] = jnp.dot(of_row, rho_ref[:, at], preferred_element_type=F32)
        inner = [
            jnp.dot(above, rho_ref[start : start + block, at], preferred_element_type=F32)
            for start in range(0, samples * rows, block)
        ]
        light = jnp.broadcast_to(light_ref[:, at] * LOG2E, shape)
        r0, r1 = view_ref[0:1, at], view_ref[1:2, at]
        fade = [jnp.broadcast_to(c, shape) for c in (r0, r0 * r0 * 0.5, r0 * r0 * r0 * (1 / 6))]
        grow = [jnp.broadcast_to(c, shape) for c in (r1, r1 * r1 * 0.5, r1 * r1 * r1 * (1 / 6))]

        clear = jnp.ones(shape, F32)
        behind = jnp.exp2(total_ref[:, at] * view_ref[1:2, at] * -LOG2E)
        for start in range(0, samples * rows, 2 * rows):
            two = rho_ref[start : start + 2 * rows, at].astype(F32)
            for part in range(2):
                rho = two[part * rows : (part + 1) * rows]
                first_row = start + part * rows
                here = slice(first_row, first_row + rows)
                shade = inner[first_row // block][first_row % block : first_row % block + rows]
                tint = jnp.exp2(rho * rho * (-8.0 * LOG2E) - light * shade)
                w0 = clear * (rho * (fade[0] - rho * (fade[1] - rho * fade[2])))
                clear = clear - w0
                w1 = behind * (rho * (grow[0] + rho * (grow[1] + rho * grow[2])))
                behind = behind + w1
                near_ref[here, at] = w0 * tint
                far_ref[here, at] = w1 * tint
                for k, color_ref in enumerate((red_ref, green_ref, blue_ref)):
                    color_ref[here, at] = jnp.exp2(rho * tone[k])


def straight_below(refs, below_ref):
    same, given = (ref[...] for ref in refs)
    me = lax.axis_index("light")
    below_ref[...] = jnp.where(me >= 2, same, 0.0) + jnp.where(me % 2 == 1, given, 0.0)


def first_below(refs, below_ref):
    mine, other, late = (ref[...] for ref in refs)
    few = mine.shape[0]
    odd = lax.axis_index("light") % 2 == 1
    below_ref[:few, :] = jnp.where(odd, other, mine)
    below_ref[few:, :] = jnp.where(odd, mine + late[-few:], other)


def crossed_below(refs, below_ref):
    cross, late = (ref[...] for ref in refs)
    below_ref[...] = jnp.where(lax.axis_index("light") >= 2, cross, 0.0) + late[: cross.shape[0]]


def whole_below(refs, below_ref):
    count, columns = refs[0].shape
    below_ref[:count, :] = refs[0][:, : columns // 2]
    below_ref[count:, :] = refs[0][:, columns // 2 :]


def post_kernel(
    rows, second, runs, sliced, assemble, light_ref, table_ref, near_ref, far_ref, red_ref, green_ref, blue_ref, rest_ref, *refs
):
    *refs, out_ref, lit_ref = refs
    assemble(refs, lit_ref)
    columns = near_ref.shape[1]
    place = lax.axis_index("depth") if sliced else 0
    chip, core = place // 2, place % 2
    odd = lax.axis_index("light") % 2
    width = 2 * LANES
    shape = (rows, width)
    scales = [jnp.broadcast_to(table_ref[3 + k : 4 + k, :], (rows, LANES)) for k in range(3)]
    for side, pieces in enumerate(runs):
        start = side * columns // 2
        light = light_ref[:, start : start + columns // 2] * -LOG2E
        for _, _, count, row in pieces:
            lit_ref[row : row + count, :] = jnp.exp2(lit_ref[row : row + count, :] * light)
    for block in range(columns // width):
        at = slice(block * width, (block + 1) * width)
        side, here_at = divmod(block * width, columns // 2)
        sums = [jnp.zeros(shape, F32)] * 6
        for even_first, odd_first, count, row in runs[side]:
            first = even_first + odd * (odd_first - even_first)
            for group in range(0, count, 8):
                lit = lit_ref[row + group : row + group + 8, here_at : here_at + width]
                for part in range(8):
                    here = pl.ds(pl.multiple_of((first + group + part) * rows, rows), rows)
                    shade = jnp.broadcast_to(lit[part : part + 1], shape)
                    weights = near_ref[here, at] * shade, far_ref[here, at] * shade
                    colors = [ref[here, at] for ref in (red_ref, green_ref, blue_ref)]
                    sums = [sums[3 * v + k] + weights[v] * colors[k] for v in range(2) for k in range(3)]
        slot = block ^ chip
        for tile in range(2):
            lanes = slice(tile * LANES, (tile + 1) * LANES)
            for n in range(6):
                value = sums[n][:, lanes] * scales[n % 3]
                if second:
                    value = value + rest_ref[tile ^ core, slot, n]
                out_ref[tile ^ core, slot, n] = value
            out_ref[tile ^ core, slot, 6] = rest_ref[tile ^ core, slot, 6] if second else rest_ref[:, at][:, lanes]


def post_tiles_kernel(
    rows, which, runs, assemble, light_ref, table_ref, near_ref, far_ref, red_ref, green_ref, blue_ref, rest_ref, *refs
):
    *refs, out_ref, lit_ref = refs
    assemble(refs, lit_ref)
    columns = near_ref.shape[1]
    place = lax.axis_index("depth")
    chip, core = place // 2, place % 2
    odd = lax.axis_index("light") % 2
    shape = (rows, LANES)
    scales = [jnp.broadcast_to(table_ref[3 + k : 4 + k, :], shape) for k in range(3)]
    blocks = columns // (2 * LANES)
    for side, pieces in enumerate(runs):
        start = side * columns // 2
        light = light_ref[:, start : start + columns // 2] * -LOG2E
        for _, _, count, row in pieces:
            lit_ref[row : row + count, :] = jnp.exp2(lit_ref[row : row + count, :] * light)
        tiles = range(side * blocks // 2, (side + 1) * blocks // 2)
        lanes = [pl.ds(pl.multiple_of((2 * tile + (which ^ core)) * LANES, LANES), LANES) for tile in tiles]
        near_lanes = [pl.ds(pl.multiple_of((2 * tile + (which ^ core)) * LANES - start, LANES), LANES) for tile in tiles]
        sums = [[jnp.zeros(shape, F32)] * 6 for _ in tiles]
        for even_first, odd_first, count, row in pieces:
            first = even_first + odd * (odd_first - even_first)
            for group in range(0, count, 8):
                lits = [lit_ref[row + group : row + group + 8, at] for at in near_lanes]
                for part in range(8):
                    here = pl.ds(pl.multiple_of((first + group + part) * rows, rows), rows)
                    for n, at in enumerate(lanes):
                        shade = jnp.broadcast_to(lits[n][part : part + 1], shape)
                        weights = near_ref[here, at] * shade, far_ref[here, at] * shade
                        colors = [ref[here, at] for ref in (red_ref, green_ref, blue_ref)]
                        sums[n] = [sums[n][3 * v + k] + weights[v] * colors[k] for v in range(2) for k in range(3)]
        for n, tile in enumerate(tiles):
            slot = tile ^ chip
            for channel in range(6):
                out_ref[slot, channel] = sums[n][channel] * scales[channel % 3] + rest_ref[which, slot, channel]
            out_ref[slot, 6] = rest_ref[which, slot, 6]


def call(kernel, outs, spaces, scratch, flops, moved, *args, limit=8):
    specs = {"v": pl.BlockSpec(memory_space=pltpu.VMEM), "s": pl.BlockSpec(memory_space=pltpu.SMEM), "a": pl.BlockSpec(memory_space=pl.ANY)}
    forced = {"V": pltpu.VMEM, "A": pltpu.HBM, "S": pltpu.SMEM}
    args = [pltpu.with_memory_space_constraint(a, forced[k]) if k in forced else a for a, k in zip(args, spaces, strict=True)]
    return pl.pallas_call(
        kernel,
        out_shape=tuple(pltpu.VMEM(o, t) for o, t in outs),
        in_specs=[specs[k.lower()] for k in spaces],
        out_specs=tuple([specs["v"]] * len(outs)),
        scratch_shapes=scratch,
        cost_estimate=pl.CostEstimate(flops=flops, bytes_accessed=moved, transcendentals=0),
        compiler_params=pltpu.CompilerParams(vmem_limit_bytes=limit << 20),
    )(*args)


def composite_kernel(bricks, got_ref, rate_ref, rank_ref, out_ref, order_ref):
    shape = out_ref.shape[2:]
    for view in range(2):
        def place(d, carry, view=view):
            order_ref[view, rank_ref[view, d]] = d
            return carry

        lax.fori_loop(0, bricks, place, 0, unroll=bricks <= 8)
        rate = jnp.broadcast_to(rate_ref[view : view + 1, :], shape)

        def nearer(p, carry, view=view, rate=rate):
            front, red, green, blue = carry
            d = order_ref[view, p]
            seen = jnp.exp2(front * rate * -LOG2E)
            red = red + got_ref[d, 3 * view] * seen
            green = green + got_ref[d, 3 * view + 1] * seen
            blue = blue + got_ref[d, 3 * view + 2] * seen
            return front + got_ref[d, 6], red, green, blue

        zero = jnp.zeros(shape, F32)
        depth, *colors = lax.fori_loop(0, bricks, nearer, (zero,) * 4, unroll=bricks <= 8)
        for k in range(3):
            out_ref[view, k] = colors[k]
        out_ref[view, 3] = opacity(depth * rate)


def composite(got, rate, rank):
    bricks, _, rows, columns = got.shape
    vmem, smem = pl.BlockSpec(memory_space=pltpu.VMEM), pl.BlockSpec(memory_space=pltpu.SMEM)
    return pl.pallas_call(
        functools.partial(composite_kernel, bricks),
        out_shape=jax.ShapeDtypeStruct((2, 4, rows, columns), F32),
        in_specs=[vmem, vmem, smem],
        out_specs=vmem,
        scratch_shapes=[pltpu.SMEM((2, bricks), jnp.int32)],
        compiler_params=pltpu.CompilerParams(vmem_limit_bytes=8 << 20),
    )(pltpu.with_memory_space_constraint(got, pltpu.VMEM), rate, rank)


def opacity(depth):
    small = jnp.full(depth.shape, 1.0, F32)
    for n in range(8, 1, -1):
        small = 1.0 - depth * (1.0 / n) * small
    return jnp.where(depth < 0.35, depth * small, 1.0 - jnp.exp2(depth * -LOG2E))


def slots_kernel(order, table_ref, rate_ref, own_ref, sibling_ref, *refs):
    *chip_refs, out_ref = refs
    shape = out_ref.shape[2:]
    chips = dict(zip(order, chip_refs, strict=True))
    blocks = [own_ref.at[0], sibling_ref.at[0]] + [chips[chip].at[t] for chip in sorted(order) for t in range(2)]
    depths = [block[6] for block in blocks]
    for view in range(2):
        rate = jnp.broadcast_to(rate_ref[view : view + 1, :], shape)
        first = TONES + len(blocks) * view
        ranks = [jnp.broadcast_to(table_ref[first + slot : first + slot + 1, :], shape) for slot in range(len(blocks))]
        colors = [jnp.zeros(shape, F32)] * 3
        for i, block in enumerate(blocks):
            front = jnp.zeros(shape, F32)
            for j, depth in enumerate(depths):
                if j != i:
                    front = front + jnp.where(ranks[j] < ranks[i], depth, 0.0)
            seen = jnp.exp2(front * rate * -LOG2E)
            colors = [colors[k] + block[3 * view + k] * seen for k in range(3)]
        for k in range(3):
            out_ref[view, k] = colors[k]
        out_ref[view, 3] = opacity(sum(depths) * rate)


def composite_slots(table, rate, own, sibling, order, chips):
    blocks = [own, sibling, *chips]
    _, rows, columns = own.shape[1:]
    (image,) = call(
        functools.partial(slots_kernel, order), [((2, 4, rows, columns), F32)], "VV" + "V" * len(blocks), [], 1 << 10, 1 << 10,
        table, rate, *blocks,
    )
    return image


def swap(x, stride, n):
    return lax.ppermute(x, "light", [(i, i ^ stride) for i in range(n)])


def lower(x, stride, n):
    if stride == n:
        return jnp.zeros_like(x)
    odd = (lax.axis_index("light") // stride) % 2 == 1
    if 2 * stride == n:
        return jnp.where(odd, swap(x, stride, n), 0.0)
    half = x.shape[0] // 2
    first, last = x[:half], x[half:]
    keep, sibling = jnp.where(odd, last, first), swap(jnp.where(odd, first, last), stride, n)
    below = lower(keep + sibling, 2 * stride, n)
    other = swap(below + jnp.where(odd, 0.0, keep), stride, n)
    mine = below + jnp.where(odd, sibling, 0.0)
    return jnp.where(odd, jnp.concatenate([other, mine]), jnp.concatenate([mine, other]))


def lower_of_four(give, hold, same, cross, late):
    given = swap(give, 1, 4)
    straight, across = swap(same, 2, 4), swap(cross, 3, 4)
    columns = same.shape[1]
    late = swap(late, 1, 4)
    (pair,) = call(pair_kernel, [(hold.shape, F32)], "VV", [], 1 << 10, 1 << 10, hold, given)
    from_same, from_cross = swap(pair, 2, 4), swap(pair, 3, 4)
    mine, send = call(upper_kernel, [(same.shape, F32)] * 2, "VVV", [], 1 << 31, 1 << 10, straight, across, same)
    (late,) = call(late_kernel, [(late.shape, F32)], "V", [], 1 << 10, 1 << 10, late)
    other = swap(send, 1, 4)
    return (from_same, given), (mine, other, late), (from_cross, late)


def shards(depth_n, light_n, density, light_rate, view_rate, centers, rank):
    samples, rows, columns = density.shape
    rho = density.reshape(samples * rows, columns)
    light = light_rate.reshape(1, -1)
    whole = (samples * rows, columns)
    sizes = [(samples // 8 * (side + 1), samples // 8 * (3 - side), columns // 2 * side) for side in range(2)]
    give = [(2 * few + many, 2 * few, many, at) for few, many, at in sizes]
    hold = [(2 * few, 2 * few + many, many, at) for few, many, at in sizes]
    same = [(0, few, few, at) for few, many, at in sizes]
    cross = [(few, 0, few, at) for few, many, at in sizes]
    places, width = [give, hold, same, cross, hold + cross], columns // 2
    if light_n != 4:
        places, width = [[(0, 0, samples, 0)]], columns
    own = columns // depth_n
    sliced = own == LANES and depth_n <= 8 and depth_n & (depth_n - 1) == 0
    table = (TONES + 2 * depth_n if sliced else TONES, LANES)
    *sums, table, rho = call(
        functools.partial(sums_kernel, rows, places, sliced),
        [((sum(piece[2] for piece in pieces), width), F32) for pieces in places] + [(table, F32), (whole, jnp.bfloat16)], "AAA",
        [pltpu.VMEM((samples, columns), F32), pltpu.SMEM(rank.shape, jnp.int32), pltpu.SMEM(centers.shape, F32), pltpu.SemaphoreType.DMA((3,))],
        1 << 20, 1 << 20, rho, rank, centers,
    )
    if light_n == 4:
        pieces = lower_of_four(*sums)
        assemble = straight_below, first_below, crossed_below
    else:
        below = lower(sums[0], 1, light_n)
        pieces = [below[: samples // 2]], [below[samples // 2 :]]
        assemble = whole_below, whole_below
    near, far, red, green, blue, total = call(
        functools.partial(pre_kernel, samples, rows, 256), [(whole, F32)] * 5 + [((rows, columns), F32)], "VVVV",
        [], 1 << 20, 12 << 20, rho, light, view_rate, table,
    )
    place = lax.axis_index("depth")
    rate = lax.dynamic_slice_in_dim(view_rate, place * own, own, axis=1)
    packed = total
    runs = [[], []], [[], []], [[], []]
    first, last = sum(few for few, _, _ in sizes), sum(many for _, many, _ in sizes)
    row, much = 0, 0
    for side, (few, many, _) in enumerate(sizes):
        runs[0][side].append((2 * few, 2 * few + many, many, much))
        runs[1][side] += [(0, 0, few, row), (few, few, few, first + row)]
        runs[2][side].append((2 * few + many, 2 * few, many, much))
        row, much = row + few, much + many
    rows_of = last, 2 * first, last
    if light_n != 4:
        half = samples // 2
        runs = [[[(start, start, half, half * side)] for side in range(2)] for start in (0, half)]
        rows_of = samples, samples
    def post(kernel, second, out, packed):
        return call(
            kernel, [(out, F32)], "V" * (8 + len(pieces[second])), [pltpu.VMEM((rows_of[second], columns // 2), F32)],
            1 << 10, 1 << 10, light, table, near, far, red, green, blue, packed, *pieces[second],
        )[0]

    packs = columns // (2 * LANES), 7, rows, LANES
    whole_runs = len(runs) - 1 if sliced else len(runs)
    for second in range(whole_runs):
        kernel = functools.partial(post_kernel, rows, second > 0, runs[second], sliced, assemble[second])
        packed = post(kernel, second, (2, *packs), packed)
    if sliced:
        def send_to(x, stride):
            return lax.ppermute(x, "depth", [(i, i ^ stride) for i in range(depth_n)])

        theirs, mine = (
            post(functools.partial(post_tiles_kernel, rows, which, runs[-1], assemble[-1]), len(runs) - 1, packs, packed)
            for which in (1, 0)
        )
        got = send_to(theirs, 1)
        order = sorted(range(1, depth_n // 2), key=lambda chip: (chip % 2, chip))
        sent = {chip: send_to(jnp.stack([mine[chip], got[chip]]), 2 * chip) for chip in order}
        return composite_slots(table, rate, mine, got, order, [sent[chip] for chip in order])
    parts = packed.transpose(1, 0, 2, 3, 4).reshape(columns // LANES, 7, rows, LANES)
    if own % LANES == 0:
        parts = parts.reshape(depth_n, own // LANES, 7, rows, LANES).transpose(0, 2, 3, 1, 4)
    else:
        parts = parts.reshape(columns // LANES, 7, rows, LANES // own, own).transpose(0, 3, 1, 2, 4)
    got = lax.all_to_all(parts.reshape(depth_n, 7, rows, own), "depth", split_axis=0, concat_axis=0, tiled=True)
    return composite(got, rate, rank)


def solution(mesh):
    return jax.shard_map(
        functools.partial(shards, mesh.shape["depth"], mesh.shape["light"]),
        mesh=mesh,
        in_specs=(P("depth", "light", None), P(), P(), P(), P()),
        out_specs=P(None, None, "light", "depth"),
        check_vma=False,
    )
```
